256 devices in a mesh: tm: 8 (over z_lo, core), tile: 32 (over y, z_hi, x).
Axes of the slice: x: 4, y: 4, z: 8 (z_hi: 2, z_lo: 4; z = z_hi * 4 + z_lo), core: 2. Of those that a mesh axis runs over, the one named last changes fastest.
Arguments:
- initial_states: float32 [8, 128, 64, 256], P('tm', 'tile'), may hold values from 0 to 2
- material: int32 [128, 64, 256], P('tile'), may hold values from 0 to 11
- conductivity: float32 [12], replicated, may hold values from 0.3 to 1
- dispersivity: float32 [12], replicated, may hold values from 0.01 to 0.03
- freundlich_k: float32 [12], replicated, may hold values from 0.1 to 1
- freundlich_n: float32 [12], replicated, may hold values from 0.5 to 0.95
- surface_load: float32 [128, 64], P('tile'), may hold values from 0 to 1.5
Outputs:
- end_states: float32 [8, 128, 64, 256], P('tm', 'tile')
The draws below stay inside these ranges and needn't reach their ends.
All inputs are finite; a program needn't handle non-finite values.
Results may differ from the reference program's by a relative error of at most 0.0001.
Values sent between devices are 32-bit elements; how exact they have to be, the bound alone decides.
A program may use at most 128 MiB of HBM per device.

```python
import math
import jax
import jax.numpy as jnp

NY = 64
NZ = 256
STEPS = 4
COARSE_STEPS = 2
MATS = 12
SLICES = 8
NX = 128


def with_ends(values, key, smallest, top_value):
    index_at = [jax.random.randint(jax.random.fold_in(key, axis), (), 0, length) for axis, length in enumerate(values.shape)]
    longest = values.shape.index(max(values.shape))
    neighbour = index_at[:longest] + [(index_at[longest] + 1) % values.shape[longest]] + index_at[longest + 1:]
    return values.at[tuple(index_at)].set(smallest).at[tuple(neighbour)].set(top_value)


def shard_levels(own_key, shape, pieces, least, top_value):
    gain, own = 1.0, jax.random.fold_in(own_key, 6)
    for position, shards_of in pieces:
        heights = jnp.exp(jax.random.uniform(jax.random.fold_in(own, position), (shards_of,), jnp.float32, least / len(pieces), top_value / len(pieces)))
        gain = gain * jnp.repeat(heights, shape[position] // shards_of).reshape([-1 if axis == position else 1 for axis in range(len(shape))])
    return gain


def setup_inputs(seed: int = 0) -> dict:
    keys = jax.random.split(jax.random.key(seed), 8)
    return {
        "initial_states": jnp.clip(2.0 * jax.random.uniform(keys[0], (SLICES, NX, NY, NZ), jnp.float32) ** shard_levels(keys[0], (SLICES, NX, NY, NZ), ((0, 8), (1, 32)), -0.2, 0.2), 0.0, 2.0),
        "material": with_ends(jax.random.randint(keys[1], (NX, NY, NZ), 0, MATS), jax.random.fold_in(keys[1], 1), 0, MATS - 1).astype(jnp.int32),
        "conductivity": jnp.clip(jnp.exp(jax.random.uniform(keys[2], (MATS,), jnp.float32, math.log(0.3), math.log(1.0))), 0.3, 1.0),
        "dispersivity": jnp.clip(jnp.exp(jax.random.uniform(keys[3], (MATS,), jnp.float32, math.log(0.01), math.log(0.03))), 0.01, 0.03),
        "freundlich_k": jnp.clip(jnp.exp(jax.random.uniform(keys[4], (MATS,), jnp.float32, math.log(0.1), math.log(1.0))), 0.1, 1.0),
        "freundlich_n": jnp.clip(jax.random.uniform(keys[5], (MATS,), jnp.float32, 0.5, 0.95), 0.5, 0.95),
        "surface_load": jnp.clip(1.5 * jax.random.uniform(keys[6], (NX, NY), jnp.float32) ** shard_levels(keys[6], (NX, NY), ((0, 32),), -0.2, 0.2), 0.0, 1.5),
    }


def coefficients(material, conductivity, dispersivity, freundlich_k, freundlich_n, surface_load):
    cond = conductivity[material]
    drift_x = 0.5 * cond
    drift_z = 0.3 * cond
    spread = dispersivity[material] * cond
    sorb_k = freundlich_k[material]
    sorb_n = freundlich_n[material]
    inflow = jnp.zeros(material.shape, jnp.float32).at[:, :, 0].set(surface_load)
    return (drift_x, drift_z, spread, sorb_k, sorb_n, inflow)


def advance(padded, coefs, spacing, time_step):
    drift_x, drift_z, spread, sorb_k, sorb_n, inflow = coefs
    middle = padded[1:-1]
    behind = padded[:-2]
    ahead = padded[2:]
    padded_yz = jnp.pad(middle, ((0, 0), (1, 1), (1, 1)))
    upper_cell = padded_yz[:, 1:-1, :-2]
    neighbours = behind + ahead + padded_yz[:, 2:, 1:-1] + padded_yz[:, :-2, 1:-1] + padded_yz[:, 1:-1, 2:] + upper_cell
    change = spread / (spacing * spacing) * (neighbours - 6.0 * middle) - drift_x / spacing * (middle - behind) - drift_z / spacing * (middle - upper_cell) + inflow
    retardation = 1.0 + sorb_k * sorb_n * (jnp.abs(middle) + 1.0) ** (sorb_n - 1.0)
    return middle + time_step * change / retardation


def coarsen(field):
    first, second, third = field.shape
    return field.reshape(first // 2, 2, second // 2, 2, third // 2, 2).mean(axis=(1, 3, 5))


def refine(field):
    return jnp.repeat(jnp.repeat(jnp.repeat(field, 2, axis=0), 2, axis=1), 2, axis=2)


def pad_lateral(field):
    return jnp.pad(field, ((1, 1), (0, 0), (0, 0)))


def fine_run(state, coefs):
    for repeat in range(STEPS):
        state = advance(pad_lateral(state), coefs, 1.0, 1.0)
    return state


def coarse_run(state, coefs):
    for repeat in range(COARSE_STEPS):
        state = advance(pad_lateral(state), coefs, 2.0, 2.0)
    return state


def reference(initial_states, material, conductivity, dispersivity, freundlich_k, freundlich_n, surface_load):
    coefs = coefficients(material, conductivity, dispersivity, freundlich_k, freundlich_n, surface_load)
    coarse_coefs = tuple(coarsen(field) for field in coefs)
    deltas = []
    for number in range(SLICES):
        start = initial_states[number]
        guess = coarse_run(coarsen(start), coarse_coefs)
        deltas.append(fine_run(start, coefs) - refine(guess))
    carry = coarsen(initial_states[0])
    results = []
    for number in range(SLICES):
        coarse_now = coarse_run(carry, coarse_coefs)
        results.append(refine(coarse_now) + deltas[number])
        carry = coarse_now + coarsen(deltas[number])
    return jnp.stack(results)
```

```python
import jax
import jax.numpy as jnp
from jax import lax
from jax.experimental import pallas as pl
from jax.experimental.pallas import tpu as pltpu
from jax.sharding import PartitionSpec as P

MESH = pl.DeviceIdType.MESH
F32 = jnp.float32
MATS = 12
TILES = 32
HALF = 128
FY = 64
CY = 32
PAD = 8
WIDE = 4


def lane(rows):
    return lax.broadcasted_iota(jnp.int32, (rows, HALF), 1)


def roll(value, shift):
    return pltpu.roll(value, shift, 1)


def gather(value, index):
    return jnp.take_along_axis(value, index, axis=1)


def update(um, u0, up, ym, yp, zm, zp, a, b, c, d, kn, n1):
    flux = a * ((up + zp) + (ym + yp)) + b * um + c * zm - d * u0
    power = jnp.exp2(n1 * jnp.log2(jnp.abs(u0) + 1.0))
    return u0 + flux / (1.0 + kn * power)


def squeeze_lanes(low, high):
    rows = low.shape[0]
    at = lane(rows)
    index = (2 * at) % HALF
    low = low + roll(low, HALF - 1)
    high = high + roll(high, HALF - 1)
    return jnp.where(at < HALF // 2, gather(low, index), gather(high, index))


def kernel(
    cond, disp, fk, fn, load, init, mat, out,
    U, M, C, L, LD, FL, GC, GU, GG, OWN, SEND, W, CF, CC, RD, GCB, FWB, OUT,
    in_sem, halo_send, halo_recv, cf_send, cf_recv, s_send, s_recv, fw_send, fw_recv,
):
    m = lax.axis_index("tm")
    t = lax.axis_index("tile")

    def device(tm, tile):
        return {"tm": tm, "tile": tile}

    def inside(tile):
        return jnp.logical_and(tile >= 0, tile < TILES)

    lead = jnp.logical_or(m == 3, m == 7)
    count = jnp.where(m == 3, 3, 4)
    first = jnp.where(m == 3, 0, 3)
    head = jnp.where(m < 3, 3, 7)
    place = jnp.where(m < 3, m, m - 3)
    width = head - m
    reach = jnp.where(m == 7, 4, jnp.where(m == 3, 3, 1))
    has = (t < TILES - 1, t > 0)

    loads = []
    for h in range(2):
        loads.append(pltpu.make_async_copy(mat.at[:, :, pl.ds(HALF * h, HALF)], M.at[pl.ds(2, 4), h], in_sem.at[h]))
    for h in range(2):
        loads.append(
            pltpu.make_async_copy(
                init.at[0, :, :, pl.ds(HALF * h, HALF)], U.at[0, pl.ds(3, 4), h, pl.ds(PAD, FY), :], in_sem.at[2 + h]
            )
        )
    for copy in loads:
        copy.start()

    zero = jnp.zeros((PAD, HALF), F32)

    def blank_fine(i, carry):
        for h in range(2):
            U[i // 10, i % 10, h, pl.ds(0, PAD), :] = zero
            U[i // 10, i % 10, h, pl.ds(PAD + FY, PAD), :] = zero
        return carry

    lax.fori_loop(0, 50, blank_fine, 0)

    def blank_coarse(i, carry):
        for k in range(2):
            W[k, i, pl.ds(0, PAD), :] = zero
            W[k, i, pl.ds(PAD + CY, PAD), :] = zero
        return carry

    lax.fori_loop(0, 18, blank_coarse, 0)
    for k in range(2):
        for r in range(6):
            GU[k, r, pl.ds(0, PAD), :] = zero
            GU[k, r, pl.ds(PAD + CY, PAD), :] = zero
    for s in range(2):

        @pl.when(jnp.logical_not(has[s]))
        def _():
            def clear(i, carry):
                for h in range(2):
                    U[i // 3, 7 - 7 * s + i % 3, h, pl.ds(PAD, FY), :] = jnp.zeros((FY, HALF), F32)
                return carry

            lax.fori_loop(0, 12, clear, 0)
            for k in range(2):
                for r in range(2):
                    GU[k, 4 - 4 * s + r, pl.ds(PAD, CY), :] = jnp.zeros((CY, HALF), F32)

    @pl.when(lead)
    def _():
        def clear(i, carry):
            @pl.when(jnp.logical_not(inside(t + i // 2 - WIDE)))
            def _():
                for f in range(5):
                    CF[i, f] = jnp.zeros((CY, HALF), F32)
                for j in range(4):
                    RD[j, i] = jnp.zeros((CY, HALF), F32)

            return carry

        lax.fori_loop(0, 18, clear, 0)

    barrier = pltpu.get_barrier_semaphore()

    def greet(tm, tile, when):
        @pl.when(jnp.logical_and(when, inside(tile)))
        def _():
            pl.semaphore_signal(barrier, inc=1, device_id=device(tm, tile), device_id_type=MESH)

    def greet_all(i, carry):
        d = i - WIDE
        greet(m, t + d, jnp.logical_and(d != 0, jnp.abs(d) <= reach))
        for j in range(4):
            greet(first + j, t + d, jnp.logical_and(jnp.logical_and(lead, j < count), jnp.abs(d) <= count - j))
        return carry

    lax.fori_loop(0, 2 * WIDE + 1, greet_all, 0)
    greet(head, t, jnp.logical_and(jnp.logical_not(lead), m > 0))

    def span(reach):
        return jnp.minimum(t, reach) + jnp.minimum(TILES - 1 - t, reach)

    expected = span(reach) + jnp.where(m == 7, 0, span(width) + 1) + jnp.where(lead, count - 1, 0)

    at = lane(8)
    tables = []
    for ref in (cond, disp, fk, fn):
        table = jnp.zeros((8, HALF), F32)
        for i in range(MATS):
            table = jnp.where(at == i, ref[i], table)
        tables.append(table)
    t_cond, t_disp, t_k, t_n = tables
    t_a = t_disp * t_cond
    tables = [t_a, t_a + 0.5 * t_cond, t_a + 0.3 * t_cond, 6.0 * t_a + 0.8 * t_cond, t_k * t_n, t_n - 1.0, t_k]

    def look_up(r):
        for h in range(2):
            index = M[r, h]
            for f, table in enumerate(tables):
                value = gather(jnp.broadcast_to(table[0:1], (FY, HALF)), index)
                if f == 2 and h == 0:
                    value = jnp.where(lane(FY) == 0, 1.0, value)
                C[f, r, h] = value

    def spread_load(s, i, r):
        row = jnp.broadcast_to(L[s, i : i + 1, :], (FY, HALF))
        here = lax.broadcasted_iota(jnp.int32, (FY, HALF), 0) == lane(FY)
        total = jnp.sum(jnp.where(here, row, 0.0), axis=1, keepdims=True)
        LD[r] = jnp.broadcast_to(total, (FY, HALF))

    def coarse_load(s, i):
        row = jnp.broadcast_to(L[s, i : i + 1, :] + L[s, i + 1 : i + 2, :], (CY, HALF))
        here = lax.broadcasted_iota(jnp.int32, (CY, HALF), 0) == lane(CY) // 2
        total = jnp.sum(jnp.where(here, row, 0.0), axis=1, keepdims=True)
        return jnp.broadcast_to(0.25 * total, (CY, HALF))

    def fine_step(k, r):
        for y in (0, 32):
            rows = pl.ds(PAD + y, 32)
            here = pl.ds(y, 32)
            low, high = U[k, r, 0, rows, :], U[k, r, 1, rows, :]
            at = lane(32)
            back = (roll(low, 1), roll(high, 1))
            ahead = (roll(low, HALF - 1), roll(high, HALF - 1))
            zms = (jnp.where(at == 0, LD[r - 1, here], back[0]), jnp.where(at == 0, back[0], back[1]))
            zps = (jnp.where(at == HALF - 1, ahead[1], ahead[0]), jnp.where(at == HALF - 1, 0.0, ahead[1]))
            for h in range(2):
                U[k + 1, r, h, rows, :] = update(
                    U[k, r - 1, h, rows, :],
                    (low, high)[h],
                    U[k, r + 1, h, rows, :],
                    U[k, r, h, pl.ds(PAD + y - 1, 32), :],
                    U[k, r, h, pl.ds(PAD + y + 1, 32), :],
                    zms[h],
                    zps[h],
                    *[C[f, r - 1, h, here] for f in range(6)],
                )

    def mean_rows(k, r):
        halves = []
        for h in range(2):
            parts = [U[k, r + q, h, pl.ds(PAD + p, CY, stride=2), :] for q in range(2) for p in range(2)]
            halves.append((parts[0] + parts[1]) + (parts[2] + parts[3]))
        return 0.125 * squeeze_lanes(*halves)

    def mean_coefs(j):
        means = []
        for f in (0, 1, 6, 5):
            halves = []
            for h in range(2):
                parts = [C[f, 2 * j + q, h, pl.ds(p, CY, stride=2), :] for q in range(2) for p in range(2)]
                halves.append((parts[0] + parts[1]) + (parts[2] + parts[3]))
            means.append(0.125 * squeeze_lanes(*halves))
        FL[j, 0] = 0.5 * means[0]
        FL[j, 1] = 2.0 * (means[1] - means[0])
        FL[j, 2] = means[2] * (means[3] + 1.0)
        FL[j, 3] = means[3]

    def combine(src, dst, r):
        a, cond = src[r, 0], src[r, 1]
        dst[r, 0] = a
        dst[r, 1] = a + 0.5 * cond
        dst[r, 2] = jnp.where(lane(CY) == 0, 1.0, a + 0.3 * cond)
        dst[r, 3] = 6.0 * a + 0.8 * cond
        dst[r, 4] = src[r, 2]
        dst[r, 5] = src[r, 3]

    def coarse_step(src, k, r, coefs, fields, place):
        rows = pl.ds(PAD, CY)
        at = lane(CY)
        u0 = src[k, r, rows, :]
        return update(
            src[k, r - 1, rows, :],
            u0,
            src[k, r + 1, rows, :],
            src[k, r, pl.ds(PAD - 1, CY), :],
            src[k, r, pl.ds(PAD + 1, CY), :],
            jnp.where(at == 0, fields[place, 4], roll(u0, 1)),
            jnp.where(at == HALF - 1, 0.0, roll(u0, HALF - 1)),
            *[coefs[place, f] for f in range(6)],
        )

    L[1] = jnp.zeros((8, HALF), F32)
    L[1, 0:4, 0:FY] = load[...]
    for i in range(4):
        spread_load(1, i, 2 + i)
    loads[0].wait()
    loads[1].wait()

    def own_rows(r, carry):
        look_up(r)
        return carry

    lax.fori_loop(2, 6, own_rows, 0)
    loads[2].wait()
    loads[3].wait()

    def inner_rows(r, carry):
        fine_step(0, r)
        return carry

    lax.fori_loop(4, 6, inner_rows, 0)
    for j in range(2):
        GU[0, 2 + j, pl.ds(PAD, CY), :] = mean_rows(0, 3 + 2 * j)

    pl.semaphore_wait(barrier, expected)

    rows = pl.ds(PAD, FY)

    def halo(item, s, arriving):
        src, dst = (
            (U.at[0, 3 + 3 * s, :, rows, :], U.at[0, 7 - 5 * s, :, rows, :]),
            (L.at[1], L.at[2 - 2 * s]),
            (M.at[pl.ds(2 + 2 * s, 2)], M.at[pl.ds(6 - 6 * s, 2)]),
            (U.at[0, 4 + s, :, rows, :], U.at[0, 8 - 7 * s, :, rows, :]),
            (GU.at[0, 3 - s, pl.ds(PAD, CY), :], GU.at[0, 5 - 5 * s, pl.ds(PAD, CY), :]),
            (U.at[1, pl.ds(4, 2), :, rows, :], U.at[1, pl.ds(8 - 8 * s, 2), :, rows, :]),
        )[item]
        toward = 2 * s - 1
        return pltpu.make_async_remote_copy(
            src_ref=src,
            dst_ref=dst,
            send_sem=halo_send.at[item, s],
            recv_sem=halo_recv.at[item, s],
            device_id=device(m, t - toward if arriving else t + toward),
            device_id_type=MESH,
        )

    sends = (t > 0, t < TILES - 1)
    for item in range(6):
        for s in range(2):

            @pl.when(sends[s])
            def _():
                halo(item, s, False).start()

    def arrive(items):
        for item in items:
            for s in range(2):

                @pl.when(has[s])
                def _():
                    halo(item, s, True).wait_recv()

    def both_sides(k, near):
        for s in range(2):
            r = 3 + (near if s == 1 else 3 - near)
            if near >= 0:
                fine_step(k, r)
            else:

                @pl.when(has[s])
                def _():
                    fine_step(k, r)

    for j in range(2):
        FL[1 + j, 4] = coarse_load(1, 2 * j)
        mean_coefs(1 + j)

    def coefs_copy(d, arriving):
        return pltpu.make_async_remote_copy(
            src_ref=FL.at[pl.ds(1, 2)],
            dst_ref=CF.at[pl.ds(2 * (WIDE + d if arriving else WIDE - d), 2)],
            send_sem=cf_send.at[WIDE + d],
            recv_sem=cf_recv.at[WIDE + d if arriving else WIDE - d],
            device_id=device(m, t + d),
            device_id_type=MESH,
        )

    def over_window(reach, act):
        def body(i, carry):
            d = i - WIDE

            @pl.when(jnp.logical_and(jnp.abs(d) <= reach, inside(t + d)))
            def _():
                act(d)

            return carry

        lax.fori_loop(0, 2 * WIDE + 1, body, 0)

    @pl.when(lead)
    def _():
        for q in range(2):
            CF[2 * WIDE + q] = FL[1 + q]

        def send(d):
            @pl.when(d != 0)
            def _():
                coefs_copy(d, False).start()

        over_window(reach, send)

    arrive((0,))
    both_sides(0, 0)
    both_sides(1, 1)
    arrive((1, 2, 3))
    for s in range(2):

        @pl.when(has[s])
        def _():
            for q in range(2):
                r = 6 - 6 * s + q
                look_up(r)
                spread_load(2 - 2 * s, q + 2 * s, r)
            FL[3 - 3 * s, 4] = coarse_load(2 - 2 * s, 2 * s)
            mean_coefs(3 - 3 * s)
            GU[0, 4 - 3 * s, pl.ds(PAD, CY), :] = mean_rows(0, 7 - 6 * s)

    both_sides(0, -1)
    both_sides(1, 0)
    both_sides(2, 1)

    arrive((4,))
    for j in (1, 2):
        combine(FL, GC, j)
        GU[1, 1 + j, pl.ds(PAD, CY), :] = coarse_step(GU, 0, 1 + j, GC, FL, j)
    for s in range(2):

        @pl.when(has[s])
        def _():
            j = 3 - 3 * s
            combine(FL, GC, j)
            GU[1, 1 + j, pl.ds(PAD, CY), :] = coarse_step(GU, 0, 1 + j, GC, FL, j)

    for j in (1, 2):
        GG[j - 1] = coarse_step(GU, 1, 1 + j, GC, FL, j)

    arrive((5,))
    both_sides(1, -2)
    both_sides(1, -1)
    both_sides(2, -1)
    both_sides(2, 0)
    both_sides(3, 0)
    both_sides(3, 1)

    for j in range(2):
        mean = mean_rows(4, 3 + 2 * j)
        OWN[j] = jnp.where(m == 0, mean, mean - GG[j])

    def block_copy(src, tm, tile, j, slot, at):
        return pltpu.make_async_remote_copy(
            src_ref=src,
            dst_ref=RD.at[j, pl.ds(2 * slot, 2)],
            send_sem=s_send.at[at],
            recv_sem=s_recv.at[j, slot],
            device_id=device(tm, tile),
            device_id_type=MESH,
        )

    def send_block(src):
        over_window(width, lambda d: block_copy(src, head, t + d, place, WIDE - d, WIDE + d).start())

    def sent_block(src):
        over_window(width, lambda d: block_copy(src, head, t + d, place, WIDE - d, WIDE + d).wait_send())

    @pl.when(jnp.logical_not(lead))
    def _():
        send_block(OWN)

    def forward(j, tm):
        return pltpu.make_async_remote_copy(
            src_ref=GCB.at[j],
            dst_ref=FWB,
            send_sem=fw_send.at[j],
            recv_sem=fw_recv.at[0],
            device_id=device(tm, t),
            device_id_type=MESH,
        )

    @pl.when(lead)
    def _():
        over_window(reach, lambda d: pl.when(d != 0)(lambda: coefs_copy(d, True).wait_recv()))

        def prepare(r, carry):
            combine(CF, CC, r)
            return carry

        lax.fori_loop(2 * (WIDE - count), 2 * (WIDE + count + 1), prepare, 0)

        def chain(j, carry):
            def take(d):
                block_copy(OWN, first + j, t + d, j, WIDE + d, WIDE + d).wait_recv()

            over_window(count - j, take)
            w = count - 1 - j

            @pl.when(j == 0)
            def _():
                def lay(r, carry):
                    W[0, r, pl.ds(PAD, CY), :] = RD[0, r]
                    return carry

                lax.fori_loop(2 * (WIDE - count), 2 * (WIDE + count + 1), lay, 0)

            @pl.when(j > 0)
            def _():
                def add(r, carry):
                    W[0, r, pl.ds(PAD, CY), :] = W[0, r, pl.ds(PAD, CY), :] + RD[j, r]
                    return carry

                lax.fori_loop(2 * (WIDE - w - 1), 2 * (WIDE + w + 2), add, 0)

            def one(i, carry):
                for q in range(2):
                    r = 2 * (WIDE - w) - 1 + 2 * i + q
                    W[1, r, pl.ds(PAD, CY), :] = coarse_step(W, 0, r, CC, CF, r)
                return carry

            lax.fori_loop(0, 2 * w + 2, one, 0)

            def two(i, carry):
                for q in range(2):
                    r = 2 * (WIDE - w) + 2 * i + q
                    W[0, r, pl.ds(PAD, CY), :] = coarse_step(W, 1, r, CC, CF, r)
                return carry

            lax.fori_loop(0, 2 * w + 1, two, 0)
            for q in range(2):
                GCB[j, q] = W[0, 2 * WIDE + q, pl.ds(PAD, CY), :]
            return carry

        lax.fori_loop(0, count, chain, 0)

        @pl.when(m == 3)
        def _():
            for q in range(2):
                SEND[q] = GCB[2, q] + OWN[q]
            send_block(SEND)

        def hand_on(j, carry):
            forward(j, first + 1 + j).start()
            return carry

        lax.fori_loop(0, count - 1, hand_on, 0)
        for q in range(2):
            FWB[q] = GCB[count - 1, q]

    @pl.when(m == 0)
    def _():
        for q in range(2):
            FWB[q] = GG[q]

    @pl.when(jnp.logical_not(jnp.logical_or(lead, m == 0)))
    def _():
        forward(0, head).wait_recv()

    for j in range(2):
        shift = FWB[j] - GG[j]
        for h in range(2):
            wide = gather(shift, lane(CY) // 2 + 64 * h)
            for q in range(2):
                for p in range(2):
                    OUT[2 * j + q, h, pl.ds(p, CY, stride=2), :] = (
                        U[4, 3 + 2 * j + q, h, pl.ds(PAD + p, CY, stride=2), :] + wide
                    )
    stores = [
        pltpu.make_async_copy(OUT.at[:, h], out.at[0, :, :, pl.ds(HALF * h, HALF)], in_sem.at[h]) for h in range(2)
    ]
    for copy in stores:
        copy.start()

    for item in range(6):
        for s in range(2):

            @pl.when(sends[s])
            def _():
                halo(item, s, False).wait_send()

    @pl.when(lead)
    def _():
        over_window(reach, lambda d: pl.when(d != 0)(lambda: coefs_copy(d, False).wait_send()))

        def handed(j, carry):
            forward(j, first + 1 + j).wait_send()
            return carry

        lax.fori_loop(0, count - 1, handed, 0)

    @pl.when(jnp.logical_not(lead))
    def _():
        sent_block(OWN)

    @pl.when(m == 3)
    def _():
        sent_block(SEND)

    for copy in stores:
        copy.wait()


def shards(initial_states, material, conductivity, dispersivity, freundlich_k, freundlich_n, surface_load):
    smem = pl.BlockSpec(memory_space=pltpu.SMEM)
    anywhere = pl.BlockSpec(memory_space=pl.ANY)
    vmem = pl.BlockSpec(memory_space=pltpu.VMEM)
    block = (CY, HALF)
    dma = pltpu.SemaphoreType.DMA
    return pl.pallas_call(
        kernel,
        out_shape=jax.ShapeDtypeStruct(initial_states.shape, F32),
        in_specs=[smem] * 4 + [vmem, anywhere, anywhere],
        out_specs=anywhere,
        scratch_shapes=[
            pltpu.VMEM((5, 10, 2, FY + 2 * PAD, HALF), F32),
            pltpu.VMEM((8, 2, FY, HALF), jnp.int32),
            pltpu.VMEM((7, 8, 2, FY, HALF), F32),
            pltpu.VMEM((3, 8, HALF), F32),
            pltpu.VMEM((8, FY, HALF), F32),
            pltpu.VMEM((4, 5) + block, F32),
            pltpu.VMEM((4, 6) + block, F32),
            pltpu.VMEM((2, 6, CY + 2 * PAD, HALF), F32),
            pltpu.VMEM((2,) + block, F32),
            pltpu.VMEM((2,) + block, F32),
            pltpu.VMEM((2,) + block, F32),
            pltpu.VMEM((2, 4 * WIDE + 2, CY + 2 * PAD, HALF), F32),
            pltpu.VMEM((4 * WIDE + 2, 5) + block, F32),
            pltpu.VMEM((4 * WIDE + 2, 6) + block, F32),
            pltpu.VMEM((4, 4 * WIDE + 2) + block, F32),
            pltpu.VMEM((4, 2) + block, F32),
            pltpu.VMEM((2,) + block, F32),
            pltpu.VMEM((4, 2, FY, HALF), F32),
            dma((4,)),
            dma((6, 2)),
            dma((6, 2)),
            dma((2 * WIDE + 1,)),
            dma((2 * WIDE + 1,)),
            dma((2 * WIDE + 1,)),
            dma((4, 2 * WIDE + 1)),
            dma((4,)),
            dma((1,)),
        ],
        compiler_params=pltpu.CompilerParams(
            collective_id=0, has_side_effects=True, vmem_limit_bytes=40 * 1024 * 1024
        ),
    )(conductivity, dispersivity, freundlich_k, freundlich_n, surface_load, initial_states, material)


def solution(mesh):
    in_specs = (
        P("tm", "tile", None, None),
        P("tile", None, None),
        P(),
        P(),
        P(),
        P(),
        P("tile", None),
    )
    out_specs = P("tm", "tile", None, None)
    return jax.shard_map(shards, mesh=mesh, in_specs=in_specs, out_specs=out_specs, check_vma=False)
```

```python
import jax
import jax.numpy as jnp
from jax import lax
from jax.experimental import pallas as pl
from jax.experimental.pallas import tpu as pltpu
from jax.sharding import PartitionSpec as P

MESH = pl.DeviceIdType.MESH
F32 = jnp.float32
MATS = 12
TILES = 32
HALF = 128
FY = 64
CY = 32
PAD = 8
WIDE = 4


def lane(rows):
    return lax.broadcasted_iota(jnp.int32, (rows, HALF), 1)


def roll(value, shift):
    return pltpu.roll(value, shift, 1)


def gather(value, index):
    return jnp.take_along_axis(value, index, axis=1)


def update(um, u0, up, ym, yp, zm, zp, a, b, c, d, kn, n1):
    flux = a * ((up + zp) + (ym + yp)) + b * um + c * zm - d * u0
    power = jnp.exp2(n1 * jnp.log2(jnp.abs(u0) + 1.0))
    return u0 + flux / (1.0 + kn * power)


def squeeze_lanes(low, high):
    rows = low.shape[0]
    at = lane(rows)
    index = (2 * at) % HALF
    low = low + roll(low, HALF - 1)
    high = high + roll(high, HALF - 1)
    return jnp.where(at < HALF // 2, gather(low, index), gather(high, index))


def kernel(
    cond, disp, fk, fn, load, init, mat, out,
    U, M, C, L, LD, FL, GC, GU, GG, OWN, SEND, W, CF, CC, RD, GCB, FWB, OUT,
    LIN, TAB, RU, in_sem, small_sem, halo_send, halo_recv, relay_send, relay_recv, sib_send, sib_recv, cf_send, cf_recv, s_send, s_recv, fw_send, fw_recv,
):
    m = lax.axis_index("tm")
    t = lax.axis_index("tile")

    def device(tm, tile):
        return {"tm": tm, "tile": tile}

    def inside(tile):
        return jnp.logical_and(tile >= 0, tile < TILES)

    lead = jnp.logical_or(m == 3, m == 7)
    count = jnp.where(m == 3, 3, 4)
    first = jnp.where(m == 3, 0, 3)
    head = jnp.where(m < 3, 3, 7)
    place = jnp.where(m < 3, m, m - 3)
    width = head - m

    def coefs_from(e, d):
        far = jnp.abs(d)
        return jnp.where(
            e == 7,
            jnp.where(far == 1, 5, jnp.where(far == 2, 2, jnp.where(far == 3, 0, 1))),
            jnp.where(far == 1, 6, jnp.where(far == 2, 4, 5)),
        )

    def gives_coefs(e, d):
        far = jnp.abs(d)
        return jnp.logical_and(jnp.logical_and(far >= 1, far <= (4 if e == 7 else 3)), m == coefs_from(e, d))

    x = t % 4
    core = m % 2
    sibling = m + 1 - 2 * core
    far = (x == 0, x == 3)
    relays = (jnp.logical_and(x == 2, t + 2 < TILES), jnp.logical_and(x == 1, t >= 2))
    has = (t < TILES - 1, t > 0)

    loads = []
    for h in range(2):
        loads.append(pltpu.make_async_copy(mat.at[:, :, pl.ds(HALF * h, HALF)], M.at[pl.ds(2, 4), h], in_sem.at[h]))
    for h in range(2):
        loads.append(
            pltpu.make_async_copy(
                init.at[0, :, :, pl.ds(HALF * h, HALF)], U.at[0, pl.ds(3, 4), h, pl.ds(PAD, FY), :], in_sem.at[2 + h]
            )
        )
    small = [pltpu.make_async_copy(load, LIN, small_sem.at[0])]
    for i, ref in enumerate((cond, disp, fk, fn)):
        small.append(pltpu.make_async_copy(ref, TAB.at[i], small_sem.at[1 + i]))
    for copy in loads + small:
        copy.start()

    barrier = pltpu.get_barrier_semaphore()

    def greet(tm, tile, when):
        @pl.when(jnp.logical_and(when, inside(tile)))
        def _():
            pl.semaphore_signal(barrier, inc=1, device_id=device(tm, tile), device_id_type=MESH)

    def greet_all(i, carry):
        d = i - WIDE
        greet(m, t + d, jnp.abs(d) == 1)
        greet(coefs_from(m, d), t + d, jnp.logical_and(lead, jnp.logical_and(d != 0, jnp.abs(d) <= count)))
        for j in range(4):
            greet(first + j, t + d, jnp.logical_and(jnp.logical_and(lead, j < count), jnp.abs(d) <= count - j))
        return carry

    lax.fori_loop(0, 2 * WIDE + 1, greet_all, 0)
    greet(head, t, jnp.logical_and(jnp.logical_not(lead), m > 0))

    def span(reach):
        return jnp.minimum(t, reach) + jnp.minimum(TILES - 1 - t, reach)

    greet(sibling, t, m >= 0)

    def add_coefs(i, total):
        d = i - WIDE
        for e in (3, 7):
            total = total + jnp.where(jnp.logical_and(gives_coefs(e, d), inside(t + d)), 1, 0)
        return total

    expected = 1 + span(1) + jnp.where(m == 7, 0, span(width) + 1) + jnp.where(lead, count - 1, 0)
    for s in range(2):
        greet(m, t + 2 - 4 * s, relays[s])
        expected = expected + jnp.where(jnp.logical_and(far[s], (t > 0, t < TILES - 1)[s]), 1, 0)
    expected = expected + lax.fori_loop(0, 2 * WIDE + 1, add_coefs, 0)

    zero = jnp.zeros((PAD, HALF), F32)

    def blank_fine(i, carry):
        for h in range(2):
            U[i // 10, i % 10, h, pl.ds(0, PAD), :] = zero
            U[i // 10, i % 10, h, pl.ds(PAD + FY, PAD), :] = zero
        return carry

    lax.fori_loop(0, 50, blank_fine, 0)

    def blank_coarse(i, carry):
        for k in range(2):
            W[k, i, pl.ds(0, PAD), :] = zero
            W[k, i, pl.ds(PAD + CY, PAD), :] = zero
        return carry

    lax.fori_loop(0, 18, blank_coarse, 0)
    for k in range(2):
        for r in range(6):
            GU[k, r, pl.ds(0, PAD), :] = zero
            GU[k, r, pl.ds(PAD + CY, PAD), :] = zero
    for s in range(2):

        @pl.when(jnp.logical_not(has[s]))
        def _():
            def clear(i, carry):
                for h in range(2):
                    U[i // 3, 7 - 7 * s + i % 3, h, pl.ds(PAD, FY), :] = jnp.zeros((FY, HALF), F32)
                return carry

            lax.fori_loop(0, 12, clear, 0)
            for k in range(2):
                for r in range(2):
                    GU[k, 4 - 4 * s + r, pl.ds(PAD, CY), :] = jnp.zeros((CY, HALF), F32)

    @pl.when(lead)
    def _():
        def clear(i, carry):
            @pl.when(jnp.logical_not(inside(t + i // 2 - WIDE)))
            def _():
                for f in range(5):
                    CF[i, f] = jnp.zeros((CY, HALF), F32)
                for j in range(4):
                    RD[j, i] = jnp.zeros((CY, HALF), F32)

            return carry

        lax.fori_loop(0, 18, clear, 0)

    at = lane(8)
    tables = []
    for copy in small:
        copy.wait()
    for k in range(4):
        table = jnp.zeros((8, HALF), F32)
        for i in range(MATS):
            table = jnp.where(at == i, TAB[k, i], table)
        tables.append(table)
    t_cond, t_disp, t_k, t_n = tables
    t_a = t_disp * t_cond
    tables = [t_a, t_a + 0.5 * t_cond, t_a + 0.3 * t_cond, 6.0 * t_a + 0.8 * t_cond, t_k * t_n, t_n - 1.0, t_k]

    def look_up(r):
        for h in range(2):
            index = M[r, h]
            for f, table in enumerate(tables):
                value = gather(jnp.broadcast_to(table[0:1], (FY, HALF)), index)
                if f == 2 and h == 0:
                    value = jnp.where(lane(FY) == 0, 1.0, value)
                C[f, r, h] = value

    def spread_load(s, i, r):
        row = jnp.broadcast_to(L[s, i : i + 1, :], (FY, HALF))
        here = lax.broadcasted_iota(jnp.int32, (FY, HALF), 0) == lane(FY)
        total = jnp.sum(jnp.where(here, row, 0.0), axis=1, keepdims=True)
        LD[r] = jnp.broadcast_to(total, (FY, HALF))

    def coarse_load(s, i):
        row = jnp.broadcast_to(L[s, i : i + 1, :] + L[s, i + 1 : i + 2, :], (CY, HALF))
        here = lax.broadcasted_iota(jnp.int32, (CY, HALF), 0) == lane(CY) // 2
        total = jnp.sum(jnp.where(here, row, 0.0), axis=1, keepdims=True)
        return jnp.broadcast_to(0.25 * total, (CY, HALF))

    def fine_step(k, r):
        for y in (0, 32):
            rows = pl.ds(PAD + y, 32)
            here = pl.ds(y, 32)
            low, high = U[k, r, 0, rows, :], U[k, r, 1, rows, :]
            at = lane(32)
            back = (roll(low, 1), roll(high, 1))
            ahead = (roll(low, HALF - 1), roll(high, HALF - 1))
            zms = (jnp.where(at == 0, LD[r - 1, here], back[0]), jnp.where(at == 0, back[0], back[1]))
            zps = (jnp.where(at == HALF - 1, ahead[1], ahead[0]), jnp.where(at == HALF - 1, 0.0, ahead[1]))
            for h in range(2):
                U[k + 1, r, h, rows, :] = update(
                    U[k, r - 1, h, rows, :],
                    (low, high)[h],
                    U[k, r + 1, h, rows, :],
                    U[k, r, h, pl.ds(PAD + y - 1, 32), :],
                    U[k, r, h, pl.ds(PAD + y + 1, 32), :],
                    zms[h],
                    zps[h],
                    *[C[f, r - 1, h, here] for f in range(6)],
                )

    def mean_rows(k, r):
        halves = []
        for h in range(2):
            parts = [U[k, r + q, h, pl.ds(PAD + p, CY, stride=2), :] for q in range(2) for p in range(2)]
            halves.append((parts[0] + parts[1]) + (parts[2] + parts[3]))
        return 0.125 * squeeze_lanes(*halves)

    def mean_coefs(j):
        means = []
        for f in (0, 1, 6, 5):
            halves = []
            for h in range(2):
                parts = [C[f, 2 * j + q, h, pl.ds(p, CY, stride=2), :] for q in range(2) for p in range(2)]
                halves.append((parts[0] + parts[1]) + (parts[2] + parts[3]))
            means.append(0.125 * squeeze_lanes(*halves))
        FL[j, 0] = 0.5 * means[0]
        FL[j, 1] = 2.0 * (means[1] - means[0])
        FL[j, 2] = means[2] * (means[3] + 1.0)
        FL[j, 3] = means[3]

    def combine(src, dst, r):
        a, cond = src[r, 0], src[r, 1]
        dst[r, 0] = a
        dst[r, 1] = a + 0.5 * cond
        dst[r, 2] = jnp.where(lane(CY) == 0, 1.0, a + 0.3 * cond)
        dst[r, 3] = 6.0 * a + 0.8 * cond
        dst[r, 4] = src[r, 2]
        dst[r, 5] = src[r, 3]

    def coarse_step(src, k, r, coefs, fields, place):
        rows = pl.ds(PAD, CY)
        at = lane(CY)
        u0 = src[k, r, rows, :]
        return update(
            src[k, r - 1, rows, :],
            u0,
            src[k, r + 1, rows, :],
            src[k, r, pl.ds(PAD - 1, CY), :],
            src[k, r, pl.ds(PAD + 1, CY), :],
            jnp.where(at == 0, fields[place, 4], roll(u0, 1)),
            jnp.where(at == HALF - 1, 0.0, roll(u0, HALF - 1)),
            *[coefs[place, f] for f in range(6)],
        )

    L[1] = jnp.zeros((8, HALF), F32)
    L[1, 0:4, 0:FY] = LIN[...]
    for i in range(4):
        spread_load(1, i, 2 + i)
    loads[0].wait()
    loads[1].wait()

    def own_rows(r, carry):
        look_up(r)
        return carry

    lax.fori_loop(2, 6, own_rows, 0)
    loads[2].wait()
    loads[3].wait()

    def inner_rows(r, carry):
        fine_step(0, r)
        return carry

    lax.fori_loop(4, 6, inner_rows, 0)
    for j in range(2):
        GU[0, 2 + j, pl.ds(PAD, CY), :] = mean_rows(0, 3 + 2 * j)

    pl.semaphore_wait(barrier, expected)

    rows = pl.ds(PAD, FY)

    def halo(item, s, arriving):
        src, dst = (
            (U.at[0, 3 + 3 * s, :, rows, :], U.at[0, 7 - 5 * s, :, rows, :]),
            (M.at[2 + 3 * s + core * (1 - 2 * s)], M.at[6 - 5 * s + core * (1 - 2 * s)]),
            (L.at[1], L.at[2 - 2 * s]),
            (U.at[0, 4 + s, :, rows, :], U.at[0, 8 - 7 * s, :, rows, :]),
            (GU.at[0, 3 - s, pl.ds(PAD, CY), :], GU.at[0, 5 - 5 * s, pl.ds(PAD, CY), :]),
            (U.at[1, 4, :, rows, :], U.at[1, 8 - 8 * s, :, rows, :]),
            (U.at[1, 5, :, rows, :], U.at[1, 9 - 8 * s, :, rows, :]),
        )[item]
        toward = 2 * s - 1
        return pltpu.make_async_remote_copy(
            src_ref=src,
            dst_ref=dst,
            send_sem=halo_send.at[item, s],
            recv_sem=halo_recv.at[item, s],
            device_id=device(m, t - toward if arriving else t + toward),
            device_id_type=MESH,
        )

    def by_relay(item, s, step):
        toward = 2 * s - 1
        q = item - 5
        if step < 2:
            return pltpu.make_async_remote_copy(
                src_ref=U.at[1, 4 + q, :, rows, :],
                dst_ref=RU.at[q],
                send_sem=halo_send.at[item, s],
                recv_sem=relay_recv.at[q],
                device_id=device(m, t + 2 * toward if step == 0 else t - 2 * toward),
                device_id_type=MESH,
            )
        return pltpu.make_async_remote_copy(
            src_ref=RU.at[q],
            dst_ref=U.at[1, 8 - 8 * s + q, :, rows, :],
            send_sem=relay_send.at[q],
            recv_sem=halo_recv.at[item, s],
            device_id=device(m, t - toward),
            device_id_type=MESH,
        )

    def to_sibling(s, arriving):
        place = 6 - 5 * s + (1 - core if arriving else core) * (1 - 2 * s)
        return pltpu.make_async_remote_copy(
            src_ref=M.at[place],
            dst_ref=M.at[place],
            send_sem=sib_send.at[s],
            recv_sem=sib_recv.at[s],
            device_id=device(sibling, t),
            device_id_type=MESH,
        )

    sends = (t > 0, t < TILES - 1)

    def each_send(act):
        for s in range(2):

            @pl.when(jnp.logical_and(sends[s], far[s]))
            def _():
                for item in (5, 6):
                    act(by_relay(item, s, 0))
                for item in (1, 2, 4, 0, 3):
                    act(halo(item, s, False))

        for item in (1, 2, 4, 0, 3, 5, 6):
            for s in range(2):

                @pl.when(jnp.logical_and(sends[s], jnp.logical_not(far[s])))
                def _():
                    act(halo(item, s, False))

    each_send(lambda copy: copy.start())

    def arrive(items):
        for item in items:
            for s in range(2):

                @pl.when(has[s])
                def _():
                    halo(item, s, True).wait_recv()

    def both_sides(k, near):
        for s in range(2):
            r = 3 + (near if s == 1 else 3 - near)
            if near >= 0:
                fine_step(k, r)
            else:

                @pl.when(has[s])
                def _():
                    fine_step(k, r)

    for j in range(2):
        FL[1 + j, 4] = coarse_load(1, 2 * j)
        mean_coefs(1 + j)

    def coefs_copy(e, d, arriving):
        return pltpu.make_async_remote_copy(
            src_ref=FL.at[pl.ds(1, 2)],
            dst_ref=CF.at[pl.ds(2 * (WIDE + d if arriving else WIDE - d), 2)],
            send_sem=cf_send.at[e // 4, WIDE + d],
            recv_sem=cf_recv.at[WIDE + d if arriving else WIDE - d],
            device_id=device(coefs_from(m, d) if arriving else e, t + d),
            device_id_type=MESH,
        )

    def over_window(reach, act):
        def body(i, carry):
            d = i - WIDE

            @pl.when(jnp.logical_and(jnp.abs(d) <= reach, inside(t + d)))
            def _():
                act(d)

            return carry

        lax.fori_loop(0, 2 * WIDE + 1, body, 0)

    @pl.when(lead)
    def _():
        for q in range(2):
            CF[2 * WIDE + q] = FL[1 + q]

    def send_coefs(e, act):
        def body(i, carry):
            d = i - WIDE

            @pl.when(jnp.logical_and(gives_coefs(e, d), inside(t + d)))
            def _():
                act(coefs_copy(e, d, False))

            return carry

        lax.fori_loop(0, 2 * WIDE + 1, body, 0)

    arrive((1,))
    for s in range(2):

        @pl.when(has[s])
        def _():
            to_sibling(s, False).start()

    arrive((2,))

    for s in range(2):

        @pl.when(has[s])
        def _():
            to_sibling(s, True).wait_recv()

    for s in range(2):

        @pl.when(has[s])
        def _():
            for q in range(2):
                r = 6 - 6 * s + q
                look_up(r)
                spread_load(2 - 2 * s, q + 2 * s, r)
            FL[3 - 3 * s, 4] = coarse_load(2 - 2 * s, 2 * s)
            mean_coefs(3 - 3 * s)

    arrive((0,))
    send_coefs(3, lambda copy: copy.start())
    both_sides(0, 0)
    both_sides(1, 1)
    arrive((3,))
    both_sides(0, -1)
    both_sides(1, 0)
    both_sides(2, 1)
    for s in range(2):

        @pl.when(has[s])
        def _():
            GU[0, 4 - 3 * s, pl.ds(PAD, CY), :] = mean_rows(0, 7 - 6 * s)

    for s in range(2):

        @pl.when(relays[s])
        def _():
            for item in (5, 6):
                by_relay(item, s, 1).wait_recv()
                by_relay(item, s, 2).start()

    arrive((4,))
    for j in (1, 2):
        combine(FL, GC, j)
        GU[1, 1 + j, pl.ds(PAD, CY), :] = coarse_step(GU, 0, 1 + j, GC, FL, j)
    for s in range(2):

        @pl.when(has[s])
        def _():
            j = 3 - 3 * s
            combine(FL, GC, j)
            GU[1, 1 + j, pl.ds(PAD, CY), :] = coarse_step(GU, 0, 1 + j, GC, FL, j)

    for j in (1, 2):
        GG[j - 1] = coarse_step(GU, 1, 1 + j, GC, FL, j)

    arrive((5, 6))
    both_sides(1, -2)
    both_sides(1, -1)
    both_sides(2, -1)
    both_sides(2, 0)
    both_sides(3, 0)
    both_sides(3, 1)

    for j in range(2):
        mean = mean_rows(4, 3 + 2 * j)
        OWN[j] = jnp.where(m == 0, mean, mean - GG[j])

    def block_copy(src, tm, tile, j, slot, at):
        return pltpu.make_async_remote_copy(
            src_ref=src,
            dst_ref=RD.at[j, pl.ds(2 * slot, 2)],
            send_sem=s_send.at[at],
            recv_sem=s_recv.at[j, slot],
            device_id=device(tm, tile),
            device_id_type=MESH,
        )

    def send_block(src):
        over_window(width, lambda d: block_copy(src, head, t + d, place, WIDE - d, WIDE + d).start())

    def sent_block(src):
        over_window(width, lambda d: block_copy(src, head, t + d, place, WIDE - d, WIDE + d).wait_send())

    @pl.when(jnp.logical_not(lead))
    def _():
        send_block(OWN)

    send_coefs(7, lambda copy: copy.start())

    def forward(j, tm):
        return pltpu.make_async_remote_copy(
            src_ref=GCB.at[j],
            dst_ref=FWB,
            send_sem=fw_send.at[j],
            recv_sem=fw_recv.at[0],
            device_id=device(tm, t),
            device_id_type=MESH,
        )

    @pl.when(lead)
    def _():
        over_window(count, lambda d: pl.when(d != 0)(lambda: coefs_copy(0, d, True).wait_recv()))

        def prepare(r, carry):
            combine(CF, CC, r)
            return carry

        lax.fori_loop(2 * (WIDE - count), 2 * (WIDE + count + 1), prepare, 0)

        def chain(j, carry):
            def take(d):
                block_copy(OWN, first + j, t + d, j, WIDE + d, WIDE + d).wait_recv()

            over_window(count - j, take)
            w = count - 1 - j

            @pl.when(j == 0)
            def _():
                def lay(r, carry):
                    W[0, r, pl.ds(PAD, CY), :] = RD[0, r]
                    return carry

                lax.fori_loop(2 * (WIDE - count), 2 * (WIDE + count + 1), lay, 0)

            @pl.when(j > 0)
            def _():
                def add(r, carry):
                    W[0, r, pl.ds(PAD, CY), :] = W[0, r, pl.ds(PAD, CY), :] + RD[j, r]
                    return carry

                lax.fori_loop(2 * (WIDE - w - 1), 2 * (WIDE + w + 2), add, 0)

            def one(i, carry):
                for q in range(2):
                    r = 2 * (WIDE - w) - 1 + 2 * i + q
                    W[1, r, pl.ds(PAD, CY), :] = coarse_step(W, 0, r, CC, CF, r)
                return carry

            lax.fori_loop(0, 2 * w + 2, one, 0)

            def two(i, carry):
                for q in range(2):
                    r = 2 * (WIDE - w) + 2 * i + q
                    W[0, r, pl.ds(PAD, CY), :] = coarse_step(W, 1, r, CC, CF, r)
                return carry

            lax.fori_loop(0, 2 * w + 1, two, 0)
            for q in range(2):
                GCB[j, q] = W[0, 2 * WIDE + q, pl.ds(PAD, CY), :]
            return carry

        lax.fori_loop(0, count, chain, 0)

        @pl.when(m == 3)
        def _():
            for q in range(2):
                SEND[q] = GCB[2, q] + OWN[q]
            send_block(SEND)

        def hand_on(j, carry):
            forward(j, first + 1 + j).start()
            return carry

        lax.fori_loop(0, count - 1, hand_on, 0)
        for q in range(2):
            FWB[q] = GCB[count - 1, q]

    @pl.when(m == 0)
    def _():
        for q in range(2):
            FWB[q] = GG[q]

    @pl.when(jnp.logical_not(jnp.logical_or(lead, m == 0)))
    def _():
        forward(0, head).wait_recv()

    for j in range(2):
        shift = FWB[j] - GG[j]
        for h in range(2):
            wide = gather(shift, lane(CY) // 2 + 64 * h)
            for q in range(2):
                for p in range(2):
                    OUT[2 * j + q, h, pl.ds(p, CY, stride=2), :] = (
                        U[4, 3 + 2 * j + q, h, pl.ds(PAD + p, CY, stride=2), :] + wide
                    )
    stores = [
        pltpu.make_async_copy(OUT.at[:, h], out.at[0, :, :, pl.ds(HALF * h, HALF)], in_sem.at[h]) for h in range(2)
    ]
    for copy in stores:
        copy.start()

    each_send(lambda copy: copy.wait_send())
    for s in range(2):

        @pl.when(relays[s])
        def _():
            for item in (5, 6):
                by_relay(item, s, 2).wait_send()

        @pl.when(has[s])
        def _():
            to_sibling(s, False).wait_send()

    @pl.when(lead)
    def _():
        def handed(j, carry):
            forward(j, first + 1 + j).wait_send()
            return carry

        lax.fori_loop(0, count - 1, handed, 0)

    @pl.when(jnp.logical_not(lead))
    def _():
        sent_block(OWN)

    @pl.when(m == 3)
    def _():
        sent_block(SEND)

    send_coefs(3, lambda copy: copy.wait_send())
    send_coefs(7, lambda copy: copy.wait_send())
    for copy in stores:
        copy.wait()


def shards(initial_states, material, conductivity, dispersivity, freundlich_k, freundlich_n, surface_load):
    hbm = pl.BlockSpec(memory_space=pltpu.HBM)
    block = (CY, HALF)
    dma = pltpu.SemaphoreType.DMA
    return pl.pallas_call(
        kernel,
        out_shape=jax.ShapeDtypeStruct(initial_states.shape, F32),
        in_specs=[hbm] * 7,
        out_specs=hbm,
        scratch_shapes=[
            pltpu.VMEM((5, 10, 2, FY + 2 * PAD, HALF), F32),
            pltpu.VMEM((8, 2, FY, HALF), jnp.int32),
            pltpu.VMEM((7, 8, 2, FY, HALF), F32),
            pltpu.VMEM((3, 8, HALF), F32),
            pltpu.VMEM((8, FY, HALF), F32),
            pltpu.VMEM((4, 5) + block, F32),
            pltpu.VMEM((4, 6) + block, F32),
            pltpu.VMEM((2, 6, CY + 2 * PAD, HALF), F32),
            pltpu.VMEM((2,) + block, F32),
            pltpu.VMEM((2,) + block, F32),
            pltpu.VMEM((2,) + block, F32),
            pltpu.VMEM((2, 4 * WIDE + 2, CY + 2 * PAD, HALF), F32),
            pltpu.VMEM((4 * WIDE + 2, 5) + block, F32),
            pltpu.VMEM((4 * WIDE + 2, 6) + block, F32),
            pltpu.VMEM((4, 4 * WIDE + 2) + block, F32),
            pltpu.VMEM((4, 2) + block, F32),
            pltpu.VMEM((2,) + block, F32),
            pltpu.VMEM((4, 2, FY, HALF), F32),
            pltpu.VMEM((4, FY), F32),
            pltpu.SMEM((4, MATS), F32),
            pltpu.VMEM((2, 2, FY, HALF), F32),
            dma((4,)),
            dma((5,)),
            dma((7, 2)),
            dma((7, 2)),
            dma((2,)),
            dma((2,)),
            dma((2,)),
            dma((2,)),
            dma((2, 2 * WIDE + 1)),
            dma((2 * WIDE + 1,)),
            dma((2 * WIDE + 1,)),
            dma((4, 2 * WIDE + 1)),
            dma((4,)),
            dma((1,)),
        ],
        compiler_params=pltpu.CompilerParams(
            collective_id=0, has_side_effects=True, vmem_limit_bytes=63 * 1024 * 1024
        ),
    )(conductivity, dispersivity, freundlich_k, freundlich_n, surface_load, initial_states, material)


def solution(mesh):
    in_specs = (
        P("tm", "tile", None, None),
        P("tile", None, None),
        P(),
        P(),
        P(),
        P(),
        P("tile", None),
    )
    out_specs = P("tm", "tile", None, None)
    return jax.shard_map(shards, mesh=mesh, in_specs=in_specs, out_specs=out_specs, check_vma=False)
```

```python
import jax
import jax.numpy as jnp
from jax import lax
from jax.experimental import pallas as pl
from jax.experimental.pallas import tpu as pltpu
from jax.sharding import PartitionSpec as P

MESH = pl.DeviceIdType.MESH
F32 = jnp.float32
MATS = 12
TILES = 32
HALF = 128
FY = 64
CY = 32
PAD = 8
URGENT = 4
LAST = 7
BREAK = 2
LONGEST = max(BREAK, LAST - BREAK)
PAIRS = (LONGEST + 1) // 2
WIDE = 2 * PAIRS
SLOTS = 2 * WIDE + 2
COEFS_FROM = ((3, 5, 4, 4), (6, 4, 0, 1))


def lane(rows):
    return lax.broadcasted_iota(jnp.int32, (rows, HALF), 1)


def roll(value, shift):
    return pltpu.roll(value, shift, 1)


def gather(value, index):
    return jnp.take_along_axis(value, index, axis=1)


def update(um, u0, up, ym, yp, zm, zp, a, b, c, d, kn, n1):
    flux = a * ((up + zp) + (ym + yp)) + b * um + c * zm - d * u0
    power = jnp.exp2(n1 * jnp.log2(jnp.abs(u0) + 1.0))
    return u0 + flux / (1.0 + kn * power)


def squeeze_lanes(low, high):
    rows = low.shape[0]
    at = lane(rows)
    index = (2 * at) % HALF
    low = low + roll(low, HALF - 1)
    high = high + roll(high, HALF - 1)
    return jnp.where(at < HALF // 2, gather(low, index), gather(high, index))


def kernel(
    cond, disp, fk, fn, load, init, mat, out,
    U, M, C, L, LD, FL, GC, GL, GU, GG, OWN, CARRY, W, CF, CC, CL, RD, GCB, FWB, UP,
    LIN, TAB, in_sem, small_sem, halo_send, halo_recv, sib_send, sib_recv, cf_send, cf_recv, s_send, s_recv, c_send, c_recv, fw_send, fw_recv,
):
    m = lax.axis_index("tm")
    t = lax.axis_index("tile")

    def device(tm, tile):
        return {"tm": tm, "tile": tile}

    def inside(tile):
        return jnp.logical_and(tile >= 0, tile < TILES)

    base = t - t % 2

    def leader_of(base):
        return base + 1 - (base % 4) // 2

    head = jnp.where(m <= BREAK, BREAK, LAST)
    lead = jnp.logical_and(m == head, t == leader_of(base))
    first = jnp.where(m <= BREAK, 0, BREAK)
    count = head - first
    place = m - first
    width = head - m

    def both(a, b):
        return jnp.logical_and(a, b)

    def reaches(base, width):
        return both(both(base >= 0, base < TILES), both(base - width <= t, t <= base + 1 + width))

    def coefs_from(e, pairs):
        value = COEFS_FROM[e][PAIRS]
        for i in range(PAIRS):
            value = jnp.where(jnp.abs(pairs) == i, COEFS_FROM[e][i], value)
        return value

    def gives_coefs(e, pairs):
        to = base + 2 * pairs
        return both(both(reaches(to, (BREAK, LAST - BREAK)[e]), m == coefs_from(e, pairs)), t != leader_of(to))

    def gives_block(pairs):
        to = base + 2 * pairs
        return both(both(m < LAST, reaches(to, width)), jnp.logical_or(m < head, t != leader_of(to)))

    x = t % 4
    core = m % 2
    sibling = m + 1 - 2 * core
    far = (x == 0, x == 3)
    has = (t < TILES - 1, t > 0)

    loads = []
    for h in range(2):
        loads.append(pltpu.make_async_copy(mat.at[:, :, pl.ds(HALF * h, HALF)], M.at[pl.ds(2, 4), h], in_sem.at[h]))
    for h in range(2):
        loads.append(
            pltpu.make_async_copy(
                init.at[0, :, :, pl.ds(HALF * h, HALF)], U.at[0, pl.ds(3, 4), h, pl.ds(PAD, FY), :], in_sem.at[2 + h]
            )
        )
    small = [pltpu.make_async_copy(load, LIN, small_sem.at[0])]
    for i, ref in enumerate((cond, disp, fk, fn)):
        small.append(pltpu.make_async_copy(ref, TAB.at[i], small_sem.at[1 + i]))
    for copy in loads + small:
        copy.start()

    barrier = pltpu.get_barrier_semaphore()

    def greet(tm, tile, when):
        @pl.when(jnp.logical_and(when, inside(tile)))
        def _():
            pl.semaphore_signal(barrier, inc=1, device_id=device(tm, tile), device_id_type=MESH)

    greet(m, t - 1, m >= 0)
    greet(m, t + 1, m >= 0)
    greet(sibling, t, m >= 0)

    def needs(i, width):
        return both(i >= WIDE - width, i <= WIDE + 1 + width)

    @pl.when(lead)
    def _():
        def greet_slot(i, carry):
            tile = base - WIDE + i
            pairs = PAIRS - i // 2
            for e in range(2):
                greet(
                    coefs_from(e, pairs), tile, both(m == (BREAK, LAST)[e], both(needs(i, count), tile != t))
                )
            for j in range(LONGEST):
                exists = jnp.logical_or(both(m == BREAK, j <= BREAK), both(m == LAST, both(j > 0, j < count)))
                other = jnp.logical_or(first + j < m, tile != t)
                greet(first + j, tile, both(both(exists, other), needs(i, count - j)))
            return carry

        lax.fori_loop(0, SLOTS, greet_slot, 0)

        @pl.when(m == LAST)
        def _():
            def greet_pair(i, carry):
                to = base + 2 * (i - PAIRS)
                greet(BREAK, leader_of(to), inside(to))
                return carry

            lax.fori_loop(0, 2 * PAIRS + 1, greet_pair, 0)

    greet(head, leader_of(base), both(jnp.logical_not(lead), m > 0))

    def add_pair(i, total):
        pairs = i - PAIRS
        for e in range(2):
            total = total + jnp.where(gives_coefs(e, pairs), 1, 0)
        total = total + jnp.where(gives_block(pairs), 1, 0)
        return total + jnp.where(both(both(lead, m == BREAK), inside(base + 2 * pairs)), 1, 0)

    expected = 1 + jnp.where(t > 0, 1, 0) + jnp.where(t < TILES - 1, 1, 0) + jnp.where(lead, 2 * count - 1, 0)
    expected = expected + lax.fori_loop(0, 2 * PAIRS + 1, add_pair, 0)

    rows = pl.ds(PAD, FY)

    def halo(item, s, arriving):
        src, dst = (
            (U.at[0, 3 + 3 * s, :, rows, :], U.at[0, 7 - 5 * s, :, rows, :]),
            (M.at[2 + 3 * s + core * (1 - 2 * s)], M.at[6 - 5 * s + core * (1 - 2 * s)]),
            (L.at[1], L.at[2 - 2 * s]),
            (U.at[0, 4 + s, :, rows, :], U.at[0, 8 - 7 * s, :, rows, :]),
            (GU.at[0, 3 - s, pl.ds(PAD, CY), :], GU.at[0, 5 - 5 * s, pl.ds(PAD, CY), :]),
            (U.at[1, 4, :, rows, :], U.at[1, 8 - 8 * s, :, rows, :]),
            (U.at[1, 5, :, rows, :], U.at[1, 9 - 8 * s, :, rows, :]),
        )[item]
        toward = 2 * s - 1
        return pltpu.make_async_remote_copy(
            src_ref=src,
            dst_ref=dst,
            send_sem=halo_send.at[item, s],
            recv_sem=halo_recv.at[item, s],
            device_id=device(m, t - toward if arriving else t + toward),
            device_id_type=MESH,
        )

    def to_sibling(s, arriving):
        place = 6 - 5 * s + (1 - core if arriving else core) * (1 - 2 * s)
        return pltpu.make_async_remote_copy(
            src_ref=M.at[place],
            dst_ref=M.at[place],
            send_sem=sib_send.at[s],
            recv_sem=sib_recv.at[s],
            device_id=device(sibling, t),
            device_id_type=MESH,
        )

    sends = (t > 0, t < TILES - 1)

    def send_across(items, when, act):
        for s in range(2):

            @pl.when(jnp.logical_and(when, jnp.logical_and(sends[s], far[s])))
            def _():
                for item in items:
                    act(halo(item, s, False))

    def send_along(items, act):
        for item in items:
            for s in range(2):

                @pl.when(jnp.logical_and(sends[s], jnp.logical_not(far[s])))
                def _():
                    act(halo(item, s, False))

    every = (1, 2, 0, 3, 4, 5, 6)
    urgent = m < URGENT

    def arrive(items):
        for item in items:
            for s in range(2):

                @pl.when(has[s])
                def _():
                    halo(item, s, True).wait_recv()

    for copy in small[:1] + loads:
        copy.wait()
    L[1] = jnp.zeros((8, HALF), F32)
    L[1, 0:4, 0:FY] = LIN[...]
    pl.semaphore_wait(barrier, expected)
    send_across(every[:4], urgent, lambda copy: copy.start())
    send_along(every[:4], lambda copy: copy.start())

    zero = jnp.zeros((PAD, HALF), F32)

    def blank_fine(i, carry):
        for h in range(2):
            U[i // 10, i % 10, h, pl.ds(0, PAD), :] = zero
            U[i // 10, i % 10, h, pl.ds(PAD + FY, PAD), :] = zero
        return carry

    lax.fori_loop(0, 50, blank_fine, 0)

    def blank_coarse(i, carry):
        for k in range(2):
            W[k, i, pl.ds(0, PAD), :] = zero
            W[k, i, pl.ds(PAD + CY, PAD), :] = zero
        return carry

    lax.fori_loop(0, 2 * SLOTS, blank_coarse, 0)
    for k in range(2):
        for r in range(6):
            GU[k, r, pl.ds(0, PAD), :] = zero
            GU[k, r, pl.ds(PAD + CY, PAD), :] = zero
    for s in range(2):

        @pl.when(jnp.logical_not(has[s]))
        def _():
            def clear(i, carry):
                for h in range(2):
                    U[i // 3, 7 - 7 * s + i % 3, h, pl.ds(PAD, FY), :] = jnp.zeros((FY, HALF), F32)
                return carry

            lax.fori_loop(0, 12, clear, 0)
            for k in range(2):
                for r in range(2):
                    GU[k, 4 - 4 * s + r, pl.ds(PAD, CY), :] = jnp.zeros((CY, HALF), F32)

    @pl.when(lead)
    def _():
        def clear(i, carry):
            @pl.when(jnp.logical_not(inside(base + i - WIDE)))
            def _():
                for q in range(2):
                    for f in range(6):
                        CC[2 * i + q, f] = jnp.zeros((CY, HALF), F32)
                    CL[2 * i + q] = jnp.zeros((CY, HALF), F32)
                    for j in range(LONGEST):
                        RD[j, 2 * i + q] = jnp.zeros((CY, HALF), F32)

            return carry

        lax.fori_loop(0, SLOTS, clear, 0)

    at = lane(8)
    tables = []
    for copy in small[1:]:
        copy.wait()
    for k in range(4):
        table = jnp.zeros((8, HALF), F32)
        for i in range(MATS):
            table = jnp.where(at == i, TAB[k, i], table)
        tables.append(table)
    t_cond, t_disp, t_k, t_n = tables
    t_a = t_disp * t_cond
    tables = [t_a, t_a + 0.5 * t_cond, t_a + 0.3 * t_cond, 6.0 * t_a + 0.8 * t_cond, t_k * t_n, t_n - 1.0, t_k]

    def look_up(r):
        for h in range(2):
            index = M[r, h]
            for f, table in enumerate(tables):
                value = gather(jnp.broadcast_to(table[0:1], (FY, HALF)), index)
                if f == 2 and h == 0:
                    value = jnp.where(lane(FY) == 0, 1.0, value)
                C[f, r, h] = value

    def spread_load(s, i, r):
        row = jnp.broadcast_to(L[s, i : i + 1, :], (FY, HALF))
        here = lax.broadcasted_iota(jnp.int32, (FY, HALF), 0) == lane(FY)
        total = jnp.sum(jnp.where(here, row, 0.0), axis=1, keepdims=True)
        LD[r] = jnp.broadcast_to(total, (FY, HALF))

    def coarse_load(rows):
        row = jnp.broadcast_to(rows[0:1] + rows[1:2], (CY, HALF))
        here = lax.broadcasted_iota(jnp.int32, (CY, HALF), 0) == lane(CY) // 2
        total = jnp.sum(jnp.where(here, row, 0.0), axis=1, keepdims=True)
        return jnp.broadcast_to(0.25 * total, (CY, HALF))

    def fine_step(k, r):
        for y in (0, 32):
            rows = pl.ds(PAD + y, 32)
            here = pl.ds(y, 32)
            low, high = U[k, r, 0, rows, :], U[k, r, 1, rows, :]
            at = lane(32)
            back = (roll(low, 1), roll(high, 1))
            ahead = (roll(low, HALF - 1), roll(high, HALF - 1))
            zms = (jnp.where(at == 0, LD[r - 1, here], back[0]), jnp.where(at == 0, back[0], back[1]))
            zps = (jnp.where(at == HALF - 1, ahead[1], ahead[0]), jnp.where(at == HALF - 1, 0.0, ahead[1]))
            for h in range(2):
                U[k + 1, r, h, rows, :] = update(
                    U[k, r - 1, h, rows, :],
                    (low, high)[h],
                    U[k, r + 1, h, rows, :],
                    U[k, r, h, pl.ds(PAD + y - 1, 32), :],
                    U[k, r, h, pl.ds(PAD + y + 1, 32), :],
                    zms[h],
                    zps[h],
                    *[C[f, r - 1, h, here] for f in range(6)],
                )

    def mean_rows(k, r):
        halves = []
        for h in range(2):
            parts = [U[k, r + q, h, pl.ds(PAD + p, CY, stride=2), :] for q in range(2) for p in range(2)]
            halves.append((parts[0] + parts[1]) + (parts[2] + parts[3]))
        return 0.125 * squeeze_lanes(*halves)

    def mean_coefs(j):
        means = []
        for f in (0, 1, 6, 5):
            halves = []
            for h in range(2):
                parts = [C[f, 2 * j + q, h, pl.ds(p, CY, stride=2), :] for q in range(2) for p in range(2)]
                halves.append((parts[0] + parts[1]) + (parts[2] + parts[3]))
            means.append(0.125 * squeeze_lanes(*halves))
        return 0.5 * means[0], 2.0 * (means[1] - means[0]), means[2] * (means[3] + 1.0), means[3]

    def combine(fields, dst, r):
        a, cond, kn, n1 = fields
        dst[r, 0] = a
        dst[r, 1] = a + 0.5 * cond
        dst[r, 2] = jnp.where(lane(CY) == 0, 1.0, a + 0.3 * cond)
        dst[r, 3] = 6.0 * a + 0.8 * cond
        dst[r, 4] = kn
        dst[r, 5] = n1

    def coarse_step(src, k, r, coefs, inflow, place):
        rows = pl.ds(PAD, CY)
        at = lane(CY)
        u0 = src[k, r, rows, :]
        return update(
            src[k, r - 1, rows, :],
            u0,
            src[k, r + 1, rows, :],
            src[k, r, pl.ds(PAD - 1, CY), :],
            src[k, r, pl.ds(PAD + 1, CY), :],
            jnp.where(at == 0, inflow[place], roll(u0, 1)),
            jnp.where(at == HALF - 1, 0.0, roll(u0, HALF - 1)),
            *[coefs[place, f] for f in range(6)],
        )

    for i in range(4):
        spread_load(1, i, 2 + i)

    def own_rows(r, carry):
        look_up(r)
        return carry

    lax.fori_loop(2, 6, own_rows, 0)

    def inner_rows(r, carry):
        fine_step(0, r)
        return carry

    lax.fori_loop(4, 6, inner_rows, 0)
    for j in range(2):
        GU[0, 2 + j, pl.ds(PAD, CY), :] = mean_rows(0, 3 + 2 * j)
    send_across(every[4:], urgent, lambda copy: copy.start())
    send_along(every[4:], lambda copy: copy.start())

    def both_sides(k, near):
        for s in range(2):
            r = 3 + (near if s == 1 else 3 - near)
            if near >= 0:
                fine_step(k, r)
            else:

                @pl.when(has[s])
                def _():
                    fine_step(k, r)

    for q in range(2):
        fields = mean_coefs(1 + q)
        for f in range(4):
            FL[pl.ds((4 * q + f) * CY, CY), :] = fields[f]
        combine(fields, GC, 1 + q)
        GL[1 + q] = coarse_load(L[1, 2 * q : 2 * q + 2, :])
    FL[pl.ds(8 * CY, 8), :] = L[1]

    def coefs_copy(e, pairs):
        to = base + 2 * pairs
        slot = t - to + WIDE
        return pltpu.make_async_remote_copy(
            src_ref=FL,
            dst_ref=CF.at[slot],
            send_sem=cf_send.at[e, PAIRS + pairs],
            recv_sem=cf_recv.at[slot],
            device_id=device((BREAK, LAST)[e], leader_of(to)),
            device_id_type=MESH,
        )

    def coefs_arrive(slot):
        pltpu.make_async_remote_copy(
            src_ref=FL,
            dst_ref=CF.at[slot],
            send_sem=cf_send.at[0, 0],
            recv_sem=cf_recv.at[slot],
            device_id=device(sibling, t),
            device_id_type=MESH,
        ).wait_recv()

    def over_pairs(gives, act):
        def body(i, carry):
            @pl.when(gives(i - PAIRS))
            def _():
                act(i - PAIRS)

            return carry

        lax.fori_loop(0, 2 * PAIRS + 1, body, 0)

    def over_slots(width, act):
        def body(i, carry):
            @pl.when(inside(base - WIDE + i))
            def _():
                act(i)

            return carry

        lax.fori_loop(WIDE - width, WIDE + 2 + width, body, 0)

    def send_coefs(e, act):
        over_pairs(lambda pairs: gives_coefs(e, pairs), lambda pairs: act(coefs_copy(e, pairs)))

    send_coefs(0, lambda copy: copy.start())
    send_across(every, jnp.logical_not(urgent), lambda copy: copy.start())

    arrive((1,))
    for s in range(2):

        @pl.when(has[s])
        def _():
            to_sibling(s, False).start()

    arrive((2,))

    for s in range(2):

        @pl.when(has[s])
        def _():
            to_sibling(s, True).wait_recv()

    for s in range(2):

        @pl.when(has[s])
        def _():
            for q in range(2):
                r = 6 - 6 * s + q
                look_up(r)
                spread_load(2 - 2 * s, q + 2 * s, r)
            GL[3 - 3 * s] = coarse_load(L[2 - 2 * s, 2 * s : 2 * s + 2, :])
            combine(mean_coefs(3 - 3 * s), GC, 3 - 3 * s)

    arrive((0,))
    both_sides(0, 0)
    both_sides(1, 1)
    arrive((3,))
    send_coefs(1, lambda copy: copy.start())
    both_sides(0, -1)
    both_sides(1, 0)
    both_sides(2, 1)
    for s in range(2):

        @pl.when(has[s])
        def _():
            GU[0, 4 - 3 * s, pl.ds(PAD, CY), :] = mean_rows(0, 7 - 6 * s)

    arrive((4,))
    for j in (1, 2):
        GU[1, 1 + j, pl.ds(PAD, CY), :] = coarse_step(GU, 0, 1 + j, GC, GL, j)
    for s in range(2):

        @pl.when(has[s])
        def _():
            j = 3 - 3 * s
            GU[1, 1 + j, pl.ds(PAD, CY), :] = coarse_step(GU, 0, 1 + j, GC, GL, j)

    for j in (1, 2):
        GG[j - 1] = coarse_step(GU, 1, 1 + j, GC, GL, j)

    arrive((5, 6))
    both_sides(1, -2)
    both_sides(1, -1)
    both_sides(2, -1)
    both_sides(2, 0)
    both_sides(3, 0)
    both_sides(3, 1)

    for j in range(2):
        mean = mean_rows(4, 3 + 2 * j)
        OWN[j] = jnp.where(m == 0, mean, mean - GG[j])

    def block_copy(pairs):
        to = base + 2 * pairs
        slot = t - to + WIDE
        return pltpu.make_async_remote_copy(
            src_ref=OWN,
            dst_ref=RD.at[place, pl.ds(2 * slot, 2)],
            send_sem=s_send.at[PAIRS + pairs],
            recv_sem=s_recv.at[place, slot],
            device_id=device(head, leader_of(to)),
            device_id_type=MESH,
        )

    def block_arrives(j, slot):
        pltpu.make_async_remote_copy(
            src_ref=OWN,
            dst_ref=RD.at[j, pl.ds(2 * slot, 2)],
            send_sem=s_send.at[0],
            recv_sem=s_recv.at[j, slot],
            device_id=device(sibling, t),
            device_id_type=MESH,
        ).wait_recv()

    over_pairs(gives_block, lambda pairs: block_copy(pairs).start())

    def carry_copy(pairs):
        to = base + 2 * pairs
        return pltpu.make_async_remote_copy(
            src_ref=CARRY,
            dst_ref=RD.at[0, pl.ds(2 * (WIDE - 2 * pairs), 4)],
            send_sem=c_send.at[PAIRS + pairs],
            recv_sem=c_recv.at[PAIRS - pairs],
            device_id=device(LAST, leader_of(to)),
            device_id_type=MESH,
        )

    def carry_arrives(pairs):
        pltpu.make_async_remote_copy(
            src_ref=CARRY,
            dst_ref=RD.at[0, pl.ds(2 * (WIDE + 2 * pairs), 4)],
            send_sem=c_send.at[0],
            recv_sem=c_recv.at[PAIRS + pairs],
            device_id=device(sibling, t),
            device_id_type=MESH,
        ).wait_recv()

    def carry_pair(pairs):
        return inside(base + 2 * pairs)

    def forward(j, q):
        return pltpu.make_async_remote_copy(
            src_ref=GCB.at[j, pl.ds(2 * q, 2)],
            dst_ref=FWB,
            send_sem=fw_send.at[j, q],
            recv_sem=fw_recv.at[0],
            device_id=device(first + 1 + j, base + q),
            device_id_type=MESH,
        )

    def forwards(j, act):
        for q in range(2):

            @pl.when(jnp.logical_or(j < count - 1, base + q != t))
            def _():
                act(forward(j, q))

    @pl.when(lead)
    def _():
        def prepare(i):
            @pl.when(base - WIDE + i != t)
            def _():
                coefs_arrive(i)

            @pl.when(base - WIDE + i == t)
            def _():
                CF[i] = FL[...]

            for q in range(2):
                combine([CF[i, pl.ds((4 * q + f) * CY, CY), :] for f in range(4)], CC, 2 * i + q)
                CL[2 * i + q] = coarse_load(CF[i, pl.ds(8 * CY + 2 * q, 2), :])

        over_slots(count, prepare)

        def chain(j, carry):
            @pl.when(jnp.logical_or(m == BREAK, j > 0))
            def _():
                over_slots(count - j, lambda i: block_arrives(j, i))

            @pl.when(both(m == LAST, j == 0))
            def _():
                over_pairs(carry_pair, carry_arrives)

            w = count - 1 - j

            @pl.when(j == 0)
            def _():
                def lay(r, carry):
                    W[0, r, pl.ds(PAD, CY), :] = RD[0, r]
                    return carry

                lax.fori_loop(2 * (WIDE - count), 2 * (WIDE + count + 2), lay, 0)

            @pl.when(j > 0)
            def _():
                def add(r, carry):
                    W[0, r, pl.ds(PAD, CY), :] = W[0, r, pl.ds(PAD, CY), :] + RD[j, r]
                    return carry

                lax.fori_loop(2 * (WIDE - w - 1), 2 * (WIDE + w + 3), add, 0)

            def step(k, start, rows):
                for q in range(rows):
                    W[1 - k, start + q, pl.ds(PAD, CY), :] = coarse_step(W, k, start + q, CC, CL, start + q)

            def one(i, carry):
                step(0, 2 * (WIDE - w) - 1 + 4 * i, 4)
                return carry

            lax.fori_loop(0, w + 1, one, 0)
            step(0, 2 * (WIDE + w) + 3, 2)

            def two(i, carry):
                step(1, 2 * (WIDE - w) + 4 * i, 4)
                return carry

            lax.fori_loop(0, w + 1, two, 0)
            for q in range(4):
                GCB[j, q] = W[0, 2 * WIDE + q, pl.ds(PAD, CY), :]
            forwards(j, lambda copy: copy.start())
            return carry

        lax.fori_loop(0, count, chain, 0)

        own = t - base

        @pl.when(m == BREAK)
        def _():
            block_arrives(BREAK, WIDE + 1 - own)
            for q in range(2):
                RD[BREAK, 2 * WIDE + 2 * own + q] = OWN[q]
            for q in range(4):
                CARRY[q] = GCB[BREAK - 1, q] + RD[BREAK, 2 * WIDE + q]
            over_pairs(carry_pair, lambda pairs: carry_copy(pairs).start())

        for q in range(2):
            FWB[q] = GCB[count - 1, 2 * own + q]

    @pl.when(m == 0)
    def _():
        for q in range(2):
            FWB[q] = GG[q]

    @pl.when(jnp.logical_not(jnp.logical_or(lead, m == 0)))
    def _():
        forward(0, 0).wait_recv()

    for j in range(2):
        shift = FWB[j] - GG[j]
        for h in range(2):
            wide = gather(shift, lane(CY) // 2 + 64 * h)
            for p in range(2):
                UP[j, h, pl.ds(p, CY, stride=2), :] = wide
            for q in range(2):
                out[0, 2 * j + q, :, HALF * h : HALF * h + HALF] = U[4, 3 + 2 * j + q, h, rows, :] + UP[j, h]

    send_across(every, m >= 0, lambda copy: copy.wait_send())
    send_along(every, lambda copy: copy.wait_send())
    for s in range(2):

        @pl.when(has[s])
        def _():
            to_sibling(s, False).wait_send()

    @pl.when(lead)
    def _():
        def handed(j, carry):
            forwards(j, lambda copy: copy.wait_send())
            return carry

        lax.fori_loop(0, count, handed, 0)

        @pl.when(m == BREAK)
        def _():
            over_pairs(carry_pair, lambda pairs: carry_copy(pairs).wait_send())

    over_pairs(gives_block, lambda pairs: block_copy(pairs).wait_send())
    for e in range(2):
        send_coefs(e, lambda copy: copy.wait_send())


def shards(initial_states, material, conductivity, dispersivity, freundlich_k, freundlich_n, surface_load):
    hbm = pl.BlockSpec(memory_space=pltpu.HBM)
    block = (CY, HALF)
    dma = pltpu.SemaphoreType.DMA
    return pl.pallas_call(
        kernel,
        out_shape=pltpu.VMEM(initial_states.shape, F32),
        in_specs=[hbm] * 7,
        out_specs=pl.BlockSpec(memory_space=pltpu.VMEM),
        scratch_shapes=[
            pltpu.VMEM((5, 10, 2, FY + 2 * PAD, HALF), F32),
            pltpu.VMEM((8, 2, FY, HALF), jnp.int32),
            pltpu.VMEM((7, 8, 2, FY, HALF), F32),
            pltpu.VMEM((3, 8, HALF), F32),
            pltpu.VMEM((8, FY, HALF), F32),
            pltpu.VMEM((8 * CY + 8, HALF), F32),
            pltpu.VMEM((4, 6) + block, F32),
            pltpu.VMEM((4,) + block, F32),
            pltpu.VMEM((2, 6, CY + 2 * PAD, HALF), F32),
            pltpu.VMEM((2,) + block, F32),
            pltpu.VMEM((2,) + block, F32),
            pltpu.VMEM((4,) + block, F32),
            pltpu.VMEM((2, 2 * SLOTS, CY + 2 * PAD, HALF), F32),
            pltpu.VMEM((SLOTS, 8 * CY + 8, HALF), F32),
            pltpu.VMEM((2 * SLOTS, 6) + block, F32),
            pltpu.VMEM((2 * SLOTS,) + block, F32),
            pltpu.VMEM((LONGEST, 2 * SLOTS) + block, F32),
            pltpu.VMEM((LONGEST, 4) + block, F32),
            pltpu.VMEM((2,) + block, F32),
            pltpu.VMEM((2, 2, FY, HALF), F32),
            pltpu.VMEM((4, FY), F32),
            pltpu.SMEM((4, MATS), F32),
            dma((4,)),
            dma((5,)),
            dma((7, 2)),
            dma((7, 2)),
            dma((2,)),
            dma((2,)),
            dma((2, 2 * PAIRS + 1)),
            dma((SLOTS,)),
            dma((2 * PAIRS + 1,)),
            dma((LONGEST, SLOTS)),
            dma((2 * PAIRS + 1,)),
            dma((2 * PAIRS + 1,)),
            dma((LONGEST, 2)),
            dma((1,)),
        ],
        compiler_params=pltpu.CompilerParams(
            collective_id=0, has_side_effects=True, vmem_limit_bytes=63 * 1024 * 1024
        ),
    )(conductivity, dispersivity, freundlich_k, freundlich_n, surface_load, initial_states, material)


def solution(mesh):
    in_specs = (
        P("tm", "tile", None, None),
        P("tile", None, None),
        P(),
        P(),
        P(),
        P(),
        P("tile", None),
    )
    out_specs = P("tm", "tile", None, None)
    return jax.shard_map(shards, mesh=mesh, in_specs=in_specs, out_specs=out_specs, check_vma=False)
```

```python
import jax
import jax.numpy as jnp
from jax import lax
from jax.experimental import pallas as pl
from jax.experimental.pallas import tpu as pltpu
from jax.sharding import PartitionSpec as P

MESH = pl.DeviceIdType.MESH
F32 = jnp.float32
MATS = 12
TILES = 32
HALF = 128
FY = 64
CY = 32
PAD = 8
URGENT = 4
LAST = 7
BREAK = 3
LONGEST = max(BREAK, LAST - BREAK)
PAIRS = (LONGEST + 1) // 2
WIDE = 2 * PAIRS
SLOTS = 2 * WIDE + 2
COEFS_FROM = ((2, 5, 4), (6, 4, 1))


def lane(rows):
    return lax.broadcasted_iota(jnp.int32, (rows, HALF), 1)


def roll(value, shift):
    return pltpu.roll(value, shift, 1)


def gather(value, index):
    return jnp.take_along_axis(value, index, axis=1)


def update(um, u0, up, ym, yp, zm, zp, a, b, c, d, kn, n1):
    flux = a * ((up + zp) + (ym + yp)) + b * um + c * zm - d * u0
    power = jnp.exp2(n1 * jnp.log2(jnp.abs(u0) + 1.0))
    return u0 + flux / (1.0 + kn * power)


def squeeze_lanes(low, high):
    rows = low.shape[0]
    at = lane(rows)
    index = (2 * at) % HALF
    low = low + roll(low, HALF - 1)
    high = high + roll(high, HALF - 1)
    return jnp.where(at < HALF // 2, gather(low, index), gather(high, index))


def kernel(
    cond, disp, fk, fn, load, init, mat, out,
    U, M, C, L, LD, FL, GC, GL, GU, GG, OWN, CARRY, W, CF, CC, CL, RD, GCB, FWB, UP,
    LIN, TAB, in_sem, small_sem, halo_send, halo_recv, sib_send, sib_recv, cf_send, cf_recv, s_send, s_recv, c_send, c_recv, fw_send, fw_recv,
):
    m = lax.axis_index("tm")
    t = lax.axis_index("tile")

    def device(tm, tile):
        return {"tm": tm, "tile": tile}

    def inside(tile):
        return jnp.logical_and(tile >= 0, tile < TILES)

    base = t - t % 2

    def leader_of(base):
        return base + 1 - (base % 4) // 2

    head = jnp.where(m <= BREAK, BREAK, LAST)
    lead = jnp.logical_and(m == head, t == leader_of(base))
    first = jnp.where(m <= BREAK, 0, BREAK)
    count = head - first
    place = m - first
    width = head - m

    def both(a, b):
        return jnp.logical_and(a, b)

    def reaches(base, width):
        return both(both(base >= 0, base < TILES), both(base - width <= t, t <= base + 1 + width))

    def coefs_from(e, pairs):
        value = COEFS_FROM[e][PAIRS]
        for i in range(PAIRS):
            value = jnp.where(jnp.abs(pairs) == i, COEFS_FROM[e][i], value)
        return value

    def gives_coefs(e, pairs):
        to = base + 2 * pairs
        return both(both(reaches(to, (BREAK, LAST - BREAK)[e]), m == coefs_from(e, pairs)), t != leader_of(to))

    def gives_block(pairs):
        to = base + 2 * pairs
        return both(both(m < LAST, reaches(to, width)), jnp.logical_or(m < head, t != leader_of(to)))

    x = t % 4
    core = m % 2
    sibling = m + 1 - 2 * core
    far = (x == 0, x == 3)
    has = (t < TILES - 1, t > 0)

    loads = []
    for h in range(2):
        loads.append(pltpu.make_async_copy(mat.at[:, :, pl.ds(HALF * h, HALF)], M.at[pl.ds(2, 4), h], in_sem.at[h]))
    for h in range(2):
        loads.append(
            pltpu.make_async_copy(
                init.at[0, :, :, pl.ds(HALF * h, HALF)], U.at[0, pl.ds(3, 4), h, pl.ds(PAD, FY), :], in_sem.at[2 + h]
            )
        )
    small = [pltpu.make_async_copy(load, LIN, small_sem.at[0])]
    for i, ref in enumerate((cond, disp, fk, fn)):
        small.append(pltpu.make_async_copy(ref, TAB.at[i], small_sem.at[1 + i]))
    for copy in loads + small:
        copy.start()

    barrier = pltpu.get_barrier_semaphore()

    def greet(tm, tile, when):
        @pl.when(jnp.logical_and(when, inside(tile)))
        def _():
            pl.semaphore_signal(barrier, inc=1, device_id=device(tm, tile), device_id_type=MESH)

    greet(m, t - 1, m >= 0)
    greet(m, t + 1, m >= 0)
    greet(sibling, t, m >= 0)

    def needs(i, width):
        return both(i >= WIDE - width, i <= WIDE + 1 + width)

    @pl.when(lead)
    def _():
        def greet_slot(i, carry):
            tile = base - WIDE + i
            pairs = PAIRS - i // 2
            for e in range(2):
                greet(
                    coefs_from(e, pairs), tile, both(m == (BREAK, LAST)[e], both(needs(i, count), tile != t))
                )
            for j in range(LONGEST):
                exists = jnp.logical_or(both(m == BREAK, j <= BREAK), both(m == LAST, both(j > 0, j < count)))
                other = jnp.logical_or(first + j < m, tile != t)
                greet(first + j, tile, both(both(exists, other), needs(i, count - j)))
            return carry

        lax.fori_loop(0, SLOTS, greet_slot, 0)

        @pl.when(m == LAST)
        def _():
            def greet_pair(i, carry):
                to = base + 2 * (i - PAIRS)
                greet(BREAK, leader_of(to), inside(to))
                return carry

            lax.fori_loop(0, 2 * PAIRS + 1, greet_pair, 0)

    greet(head, leader_of(base), both(jnp.logical_not(lead), m > 0))

    def add_pair(i, total):
        pairs = i - PAIRS
        for e in range(2):
            total = total + jnp.where(gives_coefs(e, pairs), 1, 0)
        total = total + jnp.where(gives_block(pairs), 1, 0)
        return total + jnp.where(both(both(lead, m == BREAK), inside(base + 2 * pairs)), 1, 0)

    expected = 1 + jnp.where(t > 0, 1, 0) + jnp.where(t < TILES - 1, 1, 0) + jnp.where(lead, 2 * count - 1, 0)
    expected = expected + lax.fori_loop(0, 2 * PAIRS + 1, add_pair, 0)

    rows = pl.ds(PAD, FY)

    def halo(item, s, arriving):
        src, dst = (
            (U.at[0, 3 + 3 * s, :, rows, :], U.at[0, 7 - 5 * s, :, rows, :]),
            (M.at[2 + 3 * s + core * (1 - 2 * s)], M.at[6 - 5 * s + core * (1 - 2 * s)]),
            (L.at[1], L.at[2 - 2 * s]),
            (U.at[0, 4 + s, :, rows, :], U.at[0, 8 - 7 * s, :, rows, :]),
            (GU.at[0, 3 - s, pl.ds(PAD, CY), :], GU.at[0, 5 - 5 * s, pl.ds(PAD, CY), :]),
            (U.at[1, 4, :, rows, :], U.at[1, 8 - 8 * s, :, rows, :]),
            (U.at[1, 5, :, rows, :], U.at[1, 9 - 8 * s, :, rows, :]),
        )[item]
        toward = 2 * s - 1
        return pltpu.make_async_remote_copy(
            src_ref=src,
            dst_ref=dst,
            send_sem=halo_send.at[item, s],
            recv_sem=halo_recv.at[item, s],
            device_id=device(m, t - toward if arriving else t + toward),
            device_id_type=MESH,
        )

    def to_sibling(s, arriving):
        place = 6 - 5 * s + (1 - core if arriving else core) * (1 - 2 * s)
        return pltpu.make_async_remote_copy(
            src_ref=M.at[place],
            dst_ref=M.at[place],
            send_sem=sib_send.at[s],
            recv_sem=sib_recv.at[s],
            device_id=device(sibling, t),
            device_id_type=MESH,
        )

    sends = (t > 0, t < TILES - 1)

    def send_across(items, when, act):
        for s in range(2):

            @pl.when(jnp.logical_and(when, jnp.logical_and(sends[s], far[s])))
            def _():
                for item in items:
                    act(halo(item, s, False))

    def send_along(items, act):
        for item in items:
            for s in range(2):

                @pl.when(jnp.logical_and(sends[s], jnp.logical_not(far[s])))
                def _():
                    act(halo(item, s, False))

    every = (1, 2, 0, 3, 4, 5, 6)
    urgent = m < URGENT

    def arrive(items):
        for item in items:
            for s in range(2):

                @pl.when(has[s])
                def _():
                    halo(item, s, True).wait_recv()

    for copy in small[:1] + loads:
        copy.wait()
    L[1] = jnp.zeros((8, HALF), F32)
    L[1, 0:4, 0:FY] = LIN[...]
    pl.semaphore_wait(barrier, expected)
    send_across(every[:4], urgent, lambda copy: copy.start())
    send_along(every[:4], lambda copy: copy.start())

    zero = jnp.zeros((PAD, HALF), F32)

    def blank_fine(i, carry):
        for h in range(2):
            U[i // 10, i % 10, h, pl.ds(0, PAD), :] = zero
            U[i // 10, i % 10, h, pl.ds(PAD + FY, PAD), :] = zero
        return carry

    lax.fori_loop(0, 50, blank_fine, 0)

    def blank_coarse(i, carry):
        for k in range(2):
            W[k, i, pl.ds(0, PAD), :] = zero
            W[k, i, pl.ds(PAD + CY, PAD), :] = zero
        return carry

    lax.fori_loop(0, 2 * SLOTS, blank_coarse, 0)
    for k in range(2):
        for r in range(6):
            GU[k, r, pl.ds(0, PAD), :] = zero
            GU[k, r, pl.ds(PAD + CY, PAD), :] = zero
    for s in range(2):

        @pl.when(jnp.logical_not(has[s]))
        def _():
            def clear(i, carry):
                for h in range(2):
                    U[i // 3, 7 - 7 * s + i % 3, h, pl.ds(PAD, FY), :] = jnp.zeros((FY, HALF), F32)
                return carry

            lax.fori_loop(0, 12, clear, 0)
            for k in range(2):
                for r in range(2):
                    GU[k, 4 - 4 * s + r, pl.ds(PAD, CY), :] = jnp.zeros((CY, HALF), F32)

    @pl.when(lead)
    def _():
        def clear(i, carry):
            @pl.when(jnp.logical_not(inside(base + i - WIDE)))
            def _():
                for q in range(2):
                    for f in range(6):
                        CC[2 * i + q, f] = jnp.zeros((CY, HALF), F32)
                    CL[2 * i + q] = jnp.zeros((CY, HALF), F32)
                    for j in range(LONGEST):
                        RD[j, 2 * i + q] = jnp.zeros((CY, HALF), F32)

            return carry

        lax.fori_loop(0, SLOTS, clear, 0)

    at = lane(8)
    tables = []
    for copy in small[1:]:
        copy.wait()
    for k in range(4):
        table = jnp.zeros((8, HALF), F32)
        for i in range(MATS):
            table = jnp.where(at == i, TAB[k, i], table)
        tables.append(table)
    t_cond, t_disp, t_k, t_n = tables
    t_a = t_disp * t_cond
    tables = [t_a, t_a + 0.5 * t_cond, t_a + 0.3 * t_cond, 6.0 * t_a + 0.8 * t_cond, t_k * t_n, t_n - 1.0, t_k]

    def look_up(r):
        for h in range(2):
            index = M[r, h]
            for f, table in enumerate(tables):
                value = gather(jnp.broadcast_to(table[0:1], (FY, HALF)), index)
                if f == 2 and h == 0:
                    value = jnp.where(lane(FY) == 0, 1.0, value)
                C[f, r, h] = value

    def spread_load(s, i, r):
        row = jnp.broadcast_to(L[s, i : i + 1, :], (FY, HALF))
        here = lax.broadcasted_iota(jnp.int32, (FY, HALF), 0) == lane(FY)
        total = jnp.sum(jnp.where(here, row, 0.0), axis=1, keepdims=True)
        LD[r] = jnp.broadcast_to(total, (FY, HALF))

    def coarse_load(rows):
        row = jnp.broadcast_to(rows[0:1] + rows[1:2], (CY, HALF))
        here = lax.broadcasted_iota(jnp.int32, (CY, HALF), 0) == lane(CY) // 2
        total = jnp.sum(jnp.where(here, row, 0.0), axis=1, keepdims=True)
        return jnp.broadcast_to(0.25 * total, (CY, HALF))

    def fine_step(k, r):
        for y in (0, 32):
            rows = pl.ds(PAD + y, 32)
            here = pl.ds(y, 32)
            low, high = U[k, r, 0, rows, :], U[k, r, 1, rows, :]
            at = lane(32)
            back = (roll(low, 1), roll(high, 1))
            ahead = (roll(low, HALF - 1), roll(high, HALF - 1))
            zms = (jnp.where(at == 0, LD[r - 1, here], back[0]), jnp.where(at == 0, back[0], back[1]))
            zps = (jnp.where(at == HALF - 1, ahead[1], ahead[0]), jnp.where(at == HALF - 1, 0.0, ahead[1]))
            for h in range(2):
                U[k + 1, r, h, rows, :] = update(
                    U[k, r - 1, h, rows, :],
                    (low, high)[h],
                    U[k, r + 1, h, rows, :],
                    U[k, r, h, pl.ds(PAD + y - 1, 32), :],
                    U[k, r, h, pl.ds(PAD + y + 1, 32), :],
                    zms[h],
                    zps[h],
                    *[C[f, r - 1, h, here] for f in range(6)],
                )

    def mean_rows(k, r):
        halves = []
        for h in range(2):
            parts = [U[k, r + q, h, pl.ds(PAD + p, CY, stride=2), :] for q in range(2) for p in range(2)]
            halves.append((parts[0] + parts[1]) + (parts[2] + parts[3]))
        return 0.125 * squeeze_lanes(*halves)

    def mean_coefs(j):
        means = []
        for f in (0, 1, 6, 5):
            halves = []
            for h in range(2):
                parts = [C[f, 2 * j + q, h, pl.ds(p, CY, stride=2), :] for q in range(2) for p in range(2)]
                halves.append((parts[0] + parts[1]) + (parts[2] + parts[3]))
            means.append(0.125 * squeeze_lanes(*halves))
        return 0.5 * means[0], 2.0 * (means[1] - means[0]), means[2] * (means[3] + 1.0), means[3]

    def combine(fields, dst, r):
        a, cond, kn, n1 = fields
        dst[r, 0] = a
        dst[r, 1] = a + 0.5 * cond
        dst[r, 2] = jnp.where(lane(CY) == 0, 1.0, a + 0.3 * cond)
        dst[r, 3] = 6.0 * a + 0.8 * cond
        dst[r, 4] = kn
        dst[r, 5] = n1

    def coarse_step(src, k, r, coefs, inflow, place):
        rows = pl.ds(PAD, CY)
        at = lane(CY)
        u0 = src[k, r, rows, :]
        return update(
            src[k, r - 1, rows, :],
            u0,
            src[k, r + 1, rows, :],
            src[k, r, pl.ds(PAD - 1, CY), :],
            src[k, r, pl.ds(PAD + 1, CY), :],
            jnp.where(at == 0, inflow[place], roll(u0, 1)),
            jnp.where(at == HALF - 1, 0.0, roll(u0, HALF - 1)),
            *[coefs[place, f] for f in range(6)],
        )

    for i in range(4):
        spread_load(1, i, 2 + i)

    def own_rows(r, carry):
        look_up(r)
        return carry

    lax.fori_loop(2, 6, own_rows, 0)

    def inner_rows(r, carry):
        fine_step(0, r)
        return carry

    lax.fori_loop(4, 6, inner_rows, 0)
    for j in range(2):
        GU[0, 2 + j, pl.ds(PAD, CY), :] = mean_rows(0, 3 + 2 * j)
    send_across(every[4:], urgent, lambda copy: copy.start())
    send_along(every[4:], lambda copy: copy.start())

    def both_sides(k, near):
        for s in range(2):
            r = 3 + (near if s == 1 else 3 - near)
            if near >= 0:
                fine_step(k, r)
            else:

                @pl.when(has[s])
                def _():
                    fine_step(k, r)

    for q in range(2):
        fields = mean_coefs(1 + q)
        for f in range(4):
            FL[pl.ds((4 * q + f) * CY, CY), :] = fields[f]
        combine(fields, GC, 1 + q)
        GL[1 + q] = coarse_load(L[1, 2 * q : 2 * q + 2, :])
    FL[pl.ds(8 * CY, 8), :] = L[1]

    def coefs_copy(e, pairs):
        to = base + 2 * pairs
        slot = t - to + WIDE
        return pltpu.make_async_remote_copy(
            src_ref=FL,
            dst_ref=CF.at[slot],
            send_sem=cf_send.at[e, PAIRS + pairs],
            recv_sem=cf_recv.at[slot],
            device_id=device((BREAK, LAST)[e], leader_of(to)),
            device_id_type=MESH,
        )

    def coefs_arrive(slot):
        pltpu.make_async_remote_copy(
            src_ref=FL,
            dst_ref=CF.at[slot],
            send_sem=cf_send.at[0, 0],
            recv_sem=cf_recv.at[slot],
            device_id=device(sibling, t),
            device_id_type=MESH,
        ).wait_recv()

    def over_pairs(gives, act):
        def body(i, carry):
            @pl.when(gives(i - PAIRS))
            def _():
                act(i - PAIRS)

            return carry

        lax.fori_loop(0, 2 * PAIRS + 1, body, 0)

    def over_slots(width, act):
        def body(i, carry):
            @pl.when(inside(base - WIDE + i))
            def _():
                act(i)

            return carry

        lax.fori_loop(WIDE - width, WIDE + 2 + width, body, 0)

    def send_coefs(e, act):
        over_pairs(lambda pairs: gives_coefs(e, pairs), lambda pairs: act(coefs_copy(e, pairs)))

    send_coefs(0, lambda copy: copy.start())
    send_across(every, jnp.logical_not(urgent), lambda copy: copy.start())

    arrive((1,))
    for s in range(2):

        @pl.when(has[s])
        def _():
            to_sibling(s, False).start()

    arrive((2,))

    for s in range(2):

        @pl.when(has[s])
        def _():
            to_sibling(s, True).wait_recv()

    for s in range(2):

        @pl.when(has[s])
        def _():
            for q in range(2):
                r = 6 - 6 * s + q
                look_up(r)
                spread_load(2 - 2 * s, q + 2 * s, r)
            GL[3 - 3 * s] = coarse_load(L[2 - 2 * s, 2 * s : 2 * s + 2, :])
            combine(mean_coefs(3 - 3 * s), GC, 3 - 3 * s)

    arrive((0,))
    both_sides(0, 0)
    both_sides(1, 1)
    arrive((3,))
    send_coefs(1, lambda copy: copy.start())
    both_sides(0, -1)
    both_sides(1, 0)
    both_sides(2, 1)
    for s in range(2):

        @pl.when(has[s])
        def _():
            GU[0, 4 - 3 * s, pl.ds(PAD, CY), :] = mean_rows(0, 7 - 6 * s)

    arrive((4,))
    for j in (1, 2):
        GU[1, 1 + j, pl.ds(PAD, CY), :] = coarse_step(GU, 0, 1 + j, GC, GL, j)
    for s in range(2):

        @pl.when(has[s])
        def _():
            j = 3 - 3 * s
            GU[1, 1 + j, pl.ds(PAD, CY), :] = coarse_step(GU, 0, 1 + j, GC, GL, j)

    for j in (1, 2):
        GG[j - 1] = coarse_step(GU, 1, 1 + j, GC, GL, j)

    arrive((5, 6))
    both_sides(1, -2)
    both_sides(1, -1)
    both_sides(2, -1)
    both_sides(2, 0)
    both_sides(3, 0)
    both_sides(3, 1)

    for j in range(2):
        mean = mean_rows(4, 3 + 2 * j)
        OWN[j] = jnp.where(m == 0, mean, mean - GG[j])

    def block_copy(pairs):
        to = base + 2 * pairs
        slot = t - to + WIDE
        return pltpu.make_async_remote_copy(
            src_ref=OWN,
            dst_ref=RD.at[place, pl.ds(2 * slot, 2)],
            send_sem=s_send.at[PAIRS + pairs],
            recv_sem=s_recv.at[place, slot],
            device_id=device(head, leader_of(to)),
            device_id_type=MESH,
        )

    def block_arrives(j, slot):
        pltpu.make_async_remote_copy(
            src_ref=OWN,
            dst_ref=RD.at[j, pl.ds(2 * slot, 2)],
            send_sem=s_send.at[0],
            recv_sem=s_recv.at[j, slot],
            device_id=device(sibling, t),
            device_id_type=MESH,
        ).wait_recv()

    over_pairs(gives_block, lambda pairs: block_copy(pairs).start())

    def carry_copy(pairs):
        to = base + 2 * pairs
        return pltpu.make_async_remote_copy(
            src_ref=CARRY,
            dst_ref=RD.at[0, pl.ds(2 * (WIDE - 2 * pairs), 4)],
            send_sem=c_send.at[PAIRS + pairs],
            recv_sem=c_recv.at[PAIRS - pairs],
            device_id=device(LAST, leader_of(to)),
            device_id_type=MESH,
        )

    def carry_arrives(pairs):
        pltpu.make_async_remote_copy(
            src_ref=CARRY,
            dst_ref=RD.at[0, pl.ds(2 * (WIDE + 2 * pairs), 4)],
            send_sem=c_send.at[0],
            recv_sem=c_recv.at[PAIRS + pairs],
            device_id=device(sibling, t),
            device_id_type=MESH,
        ).wait_recv()

    def carry_pair(pairs):
        return inside(base + 2 * pairs)

    def forward(j, q):
        return pltpu.make_async_remote_copy(
            src_ref=GCB.at[j, pl.ds(2 * q, 2)],
            dst_ref=FWB,
            send_sem=fw_send.at[j, q],
            recv_sem=fw_recv.at[0],
            device_id=device(first + 1 + j, base + q),
            device_id_type=MESH,
        )

    def forwards(j, act):
        for q in range(2):

            @pl.when(jnp.logical_or(j < count - 1, base + q != t))
            def _():
                act(forward(j, q))

    @pl.when(lead)
    def _():
        def prepare(i):
            @pl.when(base - WIDE + i != t)
            def _():
                coefs_arrive(i)

            @pl.when(base - WIDE + i == t)
            def _():
                CF[i] = FL[...]

            for q in range(2):
                combine([CF[i, pl.ds((4 * q + f) * CY, CY), :] for f in range(4)], CC, 2 * i + q)
                CL[2 * i + q] = coarse_load(CF[i, pl.ds(8 * CY + 2 * q, 2), :])

        over_slots(count, prepare)

        def chain(j, carry):
            @pl.when(jnp.logical_or(m == BREAK, j > 0))
            def _():
                over_slots(count - j, lambda i: block_arrives(j, i))

            @pl.when(both(m == LAST, j == 0))
            def _():
                over_pairs(carry_pair, carry_arrives)

            w = count - 1 - j

            @pl.when(j == 0)
            def _():
                def lay(r, carry):
                    W[0, r, pl.ds(PAD, CY), :] = RD[0, r]
                    return carry

                lax.fori_loop(2 * (WIDE - count), 2 * (WIDE + count + 2), lay, 0)

            @pl.when(j > 0)
            def _():
                def add(r, carry):
                    W[0, r, pl.ds(PAD, CY), :] = W[0, r, pl.ds(PAD, CY), :] + RD[j, r]
                    return carry

                lax.fori_loop(2 * (WIDE - w - 1), 2 * (WIDE + w + 3), add, 0)

            def step(k, start, rows):
                for q in range(rows):
                    W[1 - k, start + q, pl.ds(PAD, CY), :] = coarse_step(W, k, start + q, CC, CL, start + q)

            def one(i, carry):
                step(0, 2 * (WIDE - w) - 1 + 4 * i, 4)
                return carry

            lax.fori_loop(0, w + 1, one, 0)
            step(0, 2 * (WIDE + w) + 3, 2)

            def two(i, carry):
                step(1, 2 * (WIDE - w) + 4 * i, 4)
                return carry

            lax.fori_loop(0, w + 1, two, 0)
            for q in range(4):
                GCB[j, q] = W[0, 2 * WIDE + q, pl.ds(PAD, CY), :]
            forwards(j, lambda copy: copy.start())
            return carry

        lax.fori_loop(0, count, chain, 0)

        own = t - base

        @pl.when(m == BREAK)
        def _():
            block_arrives(BREAK, WIDE + 1 - own)
            for q in range(2):
                RD[BREAK, 2 * WIDE + 2 * own + q] = OWN[q]
            for q in range(4):
                CARRY[q] = GCB[BREAK - 1, q] + RD[BREAK, 2 * WIDE + q]
            over_pairs(carry_pair, lambda pairs: carry_copy(pairs).start())

        for q in range(2):
            FWB[q] = GCB[count - 1, 2 * own + q]

    @pl.when(m == 0)
    def _():
        for q in range(2):
            FWB[q] = GG[q]

    @pl.when(jnp.logical_not(jnp.logical_or(lead, m == 0)))
    def _():
        forward(0, 0).wait_recv()

    for j in range(2):
        shift = FWB[j] - GG[j]
        for h in range(2):
            wide = gather(shift, lane(CY) // 2 + 64 * h)
            for p in range(2):
                UP[j, h, pl.ds(p, CY, stride=2), :] = wide
            for q in range(2):
                out[0, 2 * j + q, :, HALF * h : HALF * h + HALF] = U[4, 3 + 2 * j + q, h, rows, :] + UP[j, h]

    send_across(every, m >= 0, lambda copy: copy.wait_send())
    send_along(every, lambda copy: copy.wait_send())
    for s in range(2):

        @pl.when(has[s])
        def _():
            to_sibling(s, False).wait_send()

    @pl.when(lead)
    def _():
        def handed(j, carry):
            forwards(j, lambda copy: copy.wait_send())
            return carry

        lax.fori_loop(0, count, handed, 0)

        @pl.when(m == BREAK)
        def _():
            over_pairs(carry_pair, lambda pairs: carry_copy(pairs).wait_send())

    over_pairs(gives_block, lambda pairs: block_copy(pairs).wait_send())
    for e in range(2):
        send_coefs(e, lambda copy: copy.wait_send())


def shards(initial_states, material, conductivity, dispersivity, freundlich_k, freundlich_n, surface_load):
    hbm = pl.BlockSpec(memory_space=pltpu.HBM)
    block = (CY, HALF)
    dma = pltpu.SemaphoreType.DMA
    return pl.pallas_call(
        kernel,
        out_shape=pltpu.VMEM(initial_states.shape, F32),
        in_specs=[hbm] * 7,
        out_specs=pl.BlockSpec(memory_space=pltpu.VMEM),
        scratch_shapes=[
            pltpu.VMEM((5, 10, 2, FY + 2 * PAD, HALF), F32),
            pltpu.VMEM((8, 2, FY, HALF), jnp.int32),
            pltpu.VMEM((7, 8, 2, FY, HALF), F32),
            pltpu.VMEM((3, 8, HALF), F32),
            pltpu.VMEM((8, FY, HALF), F32),
            pltpu.VMEM((8 * CY + 8, HALF), F32),
            pltpu.VMEM((4, 6) + block, F32),
            pltpu.VMEM((4,) + block, F32),
            pltpu.VMEM((2, 6, CY + 2 * PAD, HALF), F32),
            pltpu.VMEM((2,) + block, F32),
            pltpu.VMEM((2,) + block, F32),
            pltpu.VMEM((4,) + block, F32),
            pltpu.VMEM((2, 2 * SLOTS, CY + 2 * PAD, HALF), F32),
            pltpu.VMEM((SLOTS, 8 * CY + 8, HALF), F32),
            pltpu.VMEM((2 * SLOTS, 6) + block, F32),
            pltpu.VMEM((2 * SLOTS,) + block, F32),
            pltpu.VMEM((LONGEST, 2 * SLOTS) + block, F32),
            pltpu.VMEM((LONGEST, 4) + block, F32),
            pltpu.VMEM((2,) + block, F32),
            pltpu.VMEM((2, 2, FY, HALF), F32),
            pltpu.VMEM((4, FY), F32),
            pltpu.SMEM((4, MATS), F32),
            dma((4,)),
            dma((5,)),
            dma((7, 2)),
            dma((7, 2)),
            dma((2,)),
            dma((2,)),
            dma((2, 2 * PAIRS + 1)),
            dma((SLOTS,)),
            dma((2 * PAIRS + 1,)),
            dma((LONGEST, SLOTS)),
            dma((2 * PAIRS + 1,)),
            dma((2 * PAIRS + 1,)),
            dma((LONGEST, 2)),
            dma((1,)),
        ],
        compiler_params=pltpu.CompilerParams(
            collective_id=0, has_side_effects=True, vmem_limit_bytes=63 * 1024 * 1024
        ),
    )(conductivity, dispersivity, freundlich_k, freundlich_n, surface_load, initial_states, material)


def solution(mesh):
    in_specs = (
        P("tm", "tile", None, None),
        P("tile", None, None),
        P(),
        P(),
        P(),
        P(),
        P("tile", None),
    )
    out_specs = P("tm", "tile", None, None)
    return jax.shard_map(shards, mesh=mesh, in_specs=in_specs, out_specs=out_specs, check_vma=False)
```

```python
import jax
import jax.numpy as jnp
from jax import lax
from jax.experimental import pallas as pl
from jax.experimental.pallas import tpu as pltpu
from jax.sharding import PartitionSpec as P

MESH = pl.DeviceIdType.MESH
F32 = jnp.float32
MATS = 12
TILES = 32
HALF = 128
FY = 64
CY = 32
PAD = 8
URGENT = 4
LAST = 7
BREAK = 3
LONGEST = max(BREAK, LAST - BREAK)
PAIRS = (LONGEST + 1) // 2
WIDE = 2 * PAIRS
SLOTS = 2 * WIDE + 2
COEFS_FROM = ((2, 5, 4), (6, 4, 1))


def lane(rows):
    return lax.broadcasted_iota(jnp.int32, (rows, HALF), 1)


def roll(value, shift):
    return pltpu.roll(value, shift, 1)


def gather(value, index):
    return jnp.take_along_axis(value, index, axis=1)


def update(um, u0, up, ym, yp, zm, zp, a, b, c, d, kn, n1):
    flux = a * ((up + zp) + (ym + yp)) + b * um + c * zm - d * u0
    power = jnp.exp2(n1 * jnp.log2(jnp.abs(u0) + 1.0))
    return u0 + flux / (1.0 + kn * power)


def squeeze_lanes(low, high):
    rows = low.shape[0]
    at = lane(rows)
    index = (2 * at) % HALF
    low = low + roll(low, HALF - 1)
    high = high + roll(high, HALF - 1)
    return jnp.where(at < HALF // 2, gather(low, index), gather(high, index))


def kernel(
    cond, disp, fk, fn, load, init, mat, out,
    U, M, C, L, LD, FL, GC, GL, GU, GG, OWN, CARRY, W, CF, CC, CL, RD, GCB, FWB, UP,
    LIN, TAB, in_sem, small_sem, halo_send, halo_recv, sib_send, sib_recv, cf_send, cf_recv, s_send, s_recv, c_send, c_recv, fw_send, fw_recv,
):
    m = lax.axis_index("tm")
    t = lax.axis_index("tile")

    def device(tm, tile):
        return {"tm": tm, "tile": tile}

    def inside(tile):
        return jnp.logical_and(tile >= 0, tile < TILES)

    base = t - t % 2

    def leader_of(base):
        return base + 1 - (base % 4) // 2

    head = jnp.where(m <= BREAK, BREAK, LAST)
    lead = jnp.logical_and(m == head, t == leader_of(base))
    first = jnp.where(m <= BREAK, 0, BREAK)
    count = head - first
    place = m - first
    width = head - m

    def both(a, b):
        return jnp.logical_and(a, b)

    def reaches(base, width):
        return both(both(base >= 0, base < TILES), both(base - width <= t, t <= base + 1 + width))

    def coefs_from(e, pairs):
        value = COEFS_FROM[e][PAIRS]
        for i in range(PAIRS):
            value = jnp.where(jnp.abs(pairs) == i, COEFS_FROM[e][i], value)
        return value

    def gives_coefs(e, pairs):
        to = base + 2 * pairs
        return both(both(reaches(to, (BREAK, LAST - BREAK)[e]), m == coefs_from(e, pairs)), t != leader_of(to))

    def gives_block(pairs):
        to = base + 2 * pairs
        return both(both(m < LAST, reaches(to, width)), jnp.logical_or(m < head, t != leader_of(to)))

    x = t % 4
    core = m % 2
    sibling = m + 1 - 2 * core
    far = (x == 0, x == 3)
    has = (t < TILES - 1, t > 0)

    loads = []
    for h in range(2):
        loads.append(pltpu.make_async_copy(mat.at[:, :, pl.ds(HALF * h, HALF)], M.at[pl.ds(2, 4), h], in_sem.at[h]))
    for h in range(2):
        loads.append(
            pltpu.make_async_copy(
                init.at[0, :, :, pl.ds(HALF * h, HALF)], U.at[0, pl.ds(3, 4), h, pl.ds(PAD, FY), :], in_sem.at[2 + h]
            )
        )
    small = [pltpu.make_async_copy(load, LIN, small_sem.at[0])]
    for i, ref in enumerate((cond, disp, fk, fn)):
        small.append(pltpu.make_async_copy(ref, TAB.at[i], small_sem.at[1 + i]))
    for copy in loads + small:
        copy.start()

    barrier = pltpu.get_barrier_semaphore()

    def greet(tm, tile, when):
        @pl.when(jnp.logical_and(when, inside(tile)))
        def _():
            pl.semaphore_signal(barrier, inc=1, device_id=device(tm, tile), device_id_type=MESH)

    greet(m, t - 1, m >= 0)
    greet(m, t + 1, m >= 0)
    greet(sibling, t, m >= 0)

    for e, (slice_, start) in enumerate(((BREAK, 0), (LAST, BREAK))):

        @pl.when(both(lead, m == slice_))
        def _():
            reach = slice_ - start
            for j in range(reach):
                if j == 0 and e == 1:

                    def greet_pair(i, carry):
                        to = base + 2 * (i - PAIRS)
                        greet(BREAK, leader_of(to), m >= 0)
                        return carry

                    lax.fori_loop(0, 2 * PAIRS + 1, greet_pair, 0)
                else:

                    def greet_tile(i, carry):
                        greet(start + j, base + i - (reach - j), m >= 0)
                        return carry

                    lax.fori_loop(0, 2 + 2 * (reach - j), greet_tile, 0)
            for pairs in range(-PAIRS, PAIRS + 1):
                for i in (2 * pairs, 2 * pairs + 1):
                    if -reach <= i <= 1 + reach:
                        greet(COEFS_FROM[e][abs(pairs)], base + i, base + i != t)
            if e == 0:
                greet(BREAK, 2 * base + 1 - t, m >= 0)

    greet(head, leader_of(base), both(jnp.logical_not(lead), m > 0))

    def add_pair(i, total):
        pairs = i - PAIRS
        for e in range(2):
            total = total + jnp.where(gives_coefs(e, pairs), 1, 0)
        total = total + jnp.where(gives_block(pairs), 1, 0)
        return total + jnp.where(both(both(lead, m == BREAK), inside(base + 2 * pairs)), 1, 0)

    expected = 1 + jnp.where(t > 0, 1, 0) + jnp.where(t < TILES - 1, 1, 0) + jnp.where(lead, 2 * count - 1, 0)
    expected = expected + lax.fori_loop(0, 2 * PAIRS + 1, add_pair, 0)

    rows = pl.ds(PAD, FY)

    def halo(item, s, arriving):
        src, dst = (
            (U.at[0, 3 + 3 * s, :, rows, :], U.at[0, 7 - 5 * s, :, rows, :]),
            (M.at[2 + 3 * s + core * (1 - 2 * s)], M.at[6 - 5 * s + core * (1 - 2 * s)]),
            (L.at[1], L.at[2 - 2 * s]),
            (U.at[0, 4 + s, :, rows, :], U.at[0, 8 - 7 * s, :, rows, :]),
            (GU.at[0, 3 - s, pl.ds(PAD, CY), :], GU.at[0, 5 - 5 * s, pl.ds(PAD, CY), :]),
            (U.at[1, 4, :, rows, :], U.at[1, 8 - 8 * s, :, rows, :]),
            (U.at[1, 5, :, rows, :], U.at[1, 9 - 8 * s, :, rows, :]),
        )[item]
        toward = 2 * s - 1
        return pltpu.make_async_remote_copy(
            src_ref=src,
            dst_ref=dst,
            send_sem=halo_send.at[item, s],
            recv_sem=halo_recv.at[item, s],
            device_id=device(m, t - toward if arriving else t + toward),
            device_id_type=MESH,
        )

    def to_sibling(s, arriving):
        place = 6 - 5 * s + (1 - core if arriving else core) * (1 - 2 * s)
        return pltpu.make_async_remote_copy(
            src_ref=M.at[place],
            dst_ref=M.at[place],
            send_sem=sib_send.at[s],
            recv_sem=sib_recv.at[s],
            device_id=device(sibling, t),
            device_id_type=MESH,
        )

    sends = (t > 0, t < TILES - 1)

    def send_across(items, when, act):
        for s in range(2):

            @pl.when(jnp.logical_and(when, jnp.logical_and(sends[s], far[s])))
            def _():
                for item in items:
                    act(halo(item, s, False))

    def send_along(items, act):
        for item in items:
            for s in range(2):

                @pl.when(jnp.logical_and(sends[s], jnp.logical_not(far[s])))
                def _():
                    act(halo(item, s, False))

    every = (1, 2, 0, 3, 4, 5, 6)
    urgent = m < URGENT

    def arrive(items):
        for item in items:
            for s in range(2):

                @pl.when(has[s])
                def _():
                    halo(item, s, True).wait_recv()

    for copy in small[:1] + loads:
        copy.wait()
    L[1] = jnp.zeros((8, HALF), F32)
    L[1, 0:4, 0:FY] = LIN[...]
    pl.semaphore_wait(barrier, expected)
    send_across(every[:2], m >= 0, lambda copy: copy.start())
    send_across(every[2:4], urgent, lambda copy: copy.start())
    send_along(every[:4], lambda copy: copy.start())

    zero = jnp.zeros((PAD, HALF), F32)

    def blank_fine(i, carry):
        for h in range(2):
            U[i // 10, i % 10, h, pl.ds(0, PAD), :] = zero
            U[i // 10, i % 10, h, pl.ds(PAD + FY, PAD), :] = zero
        return carry

    lax.fori_loop(0, 50, blank_fine, 0)

    def blank_coarse(i, carry):
        for k in range(2):
            W[k, i, pl.ds(0, PAD), :] = zero
            W[k, i, pl.ds(PAD + CY, PAD), :] = zero
        return carry

    lax.fori_loop(0, 2 * SLOTS, blank_coarse, 0)
    for k in range(2):
        for r in range(6):
            GU[k, r, pl.ds(0, PAD), :] = zero
            GU[k, r, pl.ds(PAD + CY, PAD), :] = zero
    for s in range(2):

        @pl.when(jnp.logical_not(has[s]))
        def _():
            def clear(i, carry):
                for h in range(2):
                    U[i // 3, 7 - 7 * s + i % 3, h, pl.ds(PAD, FY), :] = jnp.zeros((FY, HALF), F32)
                return carry

            lax.fori_loop(0, 12, clear, 0)
            for k in range(2):
                for r in range(2):
                    GU[k, 4 - 4 * s + r, pl.ds(PAD, CY), :] = jnp.zeros((CY, HALF), F32)

    @pl.when(lead)
    def _():
        def clear(i, carry):
            @pl.when(jnp.logical_not(inside(base + i - WIDE)))
            def _():
                for q in range(2):
                    for f in range(6):
                        CC[2 * i + q, f] = jnp.zeros((CY, HALF), F32)
                    CL[2 * i + q] = jnp.zeros((CY, HALF), F32)
                    W[0, 2 * i + q, pl.ds(PAD, CY), :] = jnp.zeros((CY, HALF), F32)
                    for j in range(LONGEST):
                        RD[j, 2 * i + q] = jnp.zeros((CY, HALF), F32)

            return carry

        lax.fori_loop(0, SLOTS, clear, 0)

    at = lane(8)
    tables = []
    for copy in small[1:]:
        copy.wait()
    for k in range(4):
        table = jnp.zeros((8, HALF), F32)
        for i in range(MATS):
            table = jnp.where(at == i, TAB[k, i], table)
        tables.append(table)
    t_cond, t_disp, t_k, t_n = tables
    t_a = t_disp * t_cond
    tables = [t_a, t_a + 0.5 * t_cond, t_a + 0.3 * t_cond, 6.0 * t_a + 0.8 * t_cond, t_k * t_n, t_n - 1.0, t_k]

    def look_up(r):
        for h in range(2):
            index = M[r, h]
            for f, table in enumerate(tables):
                value = gather(jnp.broadcast_to(table[0:1], (FY, HALF)), index)
                if f == 2 and h == 0:
                    value = jnp.where(lane(FY) == 0, 1.0, value)
                C[f, r, h] = value

    def spread_load(s, i, r):
        row = jnp.broadcast_to(L[s, i : i + 1, :], (FY, HALF))
        here = lax.broadcasted_iota(jnp.int32, (FY, HALF), 0) == lane(FY)
        total = jnp.sum(jnp.where(here, row, 0.0), axis=1, keepdims=True)
        LD[r] = jnp.broadcast_to(total, (FY, HALF))

    def coarse_load(rows):
        row = jnp.broadcast_to(rows[0:1] + rows[1:2], (CY, HALF))
        here = lax.broadcasted_iota(jnp.int32, (CY, HALF), 0) == lane(CY) // 2
        total = jnp.sum(jnp.where(here, row, 0.0), axis=1, keepdims=True)
        return jnp.broadcast_to(0.25 * total, (CY, HALF))

    def fine_step(k, r):
        for y in (0, 32):
            rows = pl.ds(PAD + y, 32)
            here = pl.ds(y, 32)
            low, high = U[k, r, 0, rows, :], U[k, r, 1, rows, :]
            at = lane(32)
            back = (roll(low, 1), roll(high, 1))
            ahead = (roll(low, HALF - 1), roll(high, HALF - 1))
            zms = (jnp.where(at == 0, LD[r - 1, here], back[0]), jnp.where(at == 0, back[0], back[1]))
            zps = (jnp.where(at == HALF - 1, ahead[1], ahead[0]), jnp.where(at == HALF - 1, 0.0, ahead[1]))
            for h in range(2):
                U[k + 1, r, h, rows, :] = update(
                    U[k, r - 1, h, rows, :],
                    (low, high)[h],
                    U[k, r + 1, h, rows, :],
                    U[k, r, h, pl.ds(PAD + y - 1, 32), :],
                    U[k, r, h, pl.ds(PAD + y + 1, 32), :],
                    zms[h],
                    zps[h],
                    *[C[f, r - 1, h, here] for f in range(6)],
                )

    def mean_rows(k, r):
        halves = []
        for h in range(2):
            parts = [U[k, r + q, h, pl.ds(PAD + p, CY, stride=2), :] for q in range(2) for p in range(2)]
            halves.append((parts[0] + parts[1]) + (parts[2] + parts[3]))
        return 0.125 * squeeze_lanes(*halves)

    def mean_coefs(j):
        means = []
        for f in (0, 1, 6, 5):
            halves = []
            for h in range(2):
                parts = [C[f, 2 * j + q, h, pl.ds(p, CY, stride=2), :] for q in range(2) for p in range(2)]
                halves.append((parts[0] + parts[1]) + (parts[2] + parts[3]))
            means.append(0.125 * squeeze_lanes(*halves))
        return 0.5 * means[0], 2.0 * (means[1] - means[0]), means[2] * (means[3] + 1.0), means[3]

    def combine(fields, dst, r):
        a, cond, kn, n1 = fields
        dst[r, 0] = a
        dst[r, 1] = a + 0.5 * cond
        dst[r, 2] = jnp.where(lane(CY) == 0, 1.0, a + 0.3 * cond)
        dst[r, 3] = 6.0 * a + 0.8 * cond
        dst[r, 4] = kn
        dst[r, 5] = n1

    def coarse_step(src, k, r, coefs, inflow, place):
        rows = pl.ds(PAD, CY)
        at = lane(CY)
        u0 = src[k, r, rows, :]
        return update(
            src[k, r - 1, rows, :],
            u0,
            src[k, r + 1, rows, :],
            src[k, r, pl.ds(PAD - 1, CY), :],
            src[k, r, pl.ds(PAD + 1, CY), :],
            jnp.where(at == 0, inflow[place], roll(u0, 1)),
            jnp.where(at == HALF - 1, 0.0, roll(u0, HALF - 1)),
            *[coefs[place, f] for f in range(6)],
        )

    for i in range(4):
        spread_load(1, i, 2 + i)

    def own_rows(r, carry):
        look_up(r)
        return carry

    lax.fori_loop(2, 6, own_rows, 0)

    def inner_rows(r, carry):
        fine_step(0, r)
        return carry

    lax.fori_loop(4, 6, inner_rows, 0)
    for j in range(2):
        GU[0, 2 + j, pl.ds(PAD, CY), :] = mean_rows(0, 3 + 2 * j)
    send_across(every[4:], urgent, lambda copy: copy.start())
    send_along(every[4:], lambda copy: copy.start())

    def both_sides(k, near):
        for s in range(2):
            r = 3 + (near if s == 1 else 3 - near)
            if near >= 0:
                fine_step(k, r)
            else:

                @pl.when(has[s])
                def _():
                    fine_step(k, r)

    for q in range(2):
        fields = mean_coefs(1 + q)
        for f in range(4):
            FL[pl.ds((4 * q + f) * CY, CY), :] = fields[f]
        combine(fields, GC, 1 + q)
        GL[1 + q] = coarse_load(L[1, 2 * q : 2 * q + 2, :])
    FL[pl.ds(8 * CY, 8), :] = L[1]

    def coefs_copy(e, pairs):
        to = base + 2 * pairs
        slot = t - to + WIDE
        return pltpu.make_async_remote_copy(
            src_ref=FL,
            dst_ref=CF.at[slot],
            send_sem=cf_send.at[e, PAIRS + pairs],
            recv_sem=cf_recv.at[slot],
            device_id=device((BREAK, LAST)[e], leader_of(to)),
            device_id_type=MESH,
        )

    def coefs_arrive(slot):
        pltpu.make_async_remote_copy(
            src_ref=FL,
            dst_ref=CF.at[slot],
            send_sem=cf_send.at[0, 0],
            recv_sem=cf_recv.at[slot],
            device_id=device(sibling, t),
            device_id_type=MESH,
        ).wait_recv()

    def over_pairs(gives, act):
        def body(i, carry):
            @pl.when(gives(i - PAIRS))
            def _():
                act(i - PAIRS)

            return carry

        lax.fori_loop(0, 2 * PAIRS + 1, body, 0)

    def over_slots(width, act):
        def body(i, carry):
            @pl.when(inside(base - WIDE + i))
            def _():
                act(i)

            return carry

        lax.fori_loop(WIDE - width, WIDE + 2 + width, body, 0)

    def send_coefs(e, act):
        over_pairs(lambda pairs: gives_coefs(e, pairs), lambda pairs: act(coefs_copy(e, pairs)))

    send_coefs(0, lambda copy: copy.start())

    arrive((1,))
    for s in range(2):

        @pl.when(has[s])
        def _():
            to_sibling(s, False).start()

    arrive((2,))

    send_across(every[2:], jnp.logical_not(urgent), lambda copy: copy.start())
    for s in range(2):

        @pl.when(has[s])
        def _():
            to_sibling(s, True).wait_recv()

    for s in range(2):

        @pl.when(has[s])
        def _():
            for q in range(2):
                r = 6 - 6 * s + q
                look_up(r)
                spread_load(2 - 2 * s, q + 2 * s, r)
            GL[3 - 3 * s] = coarse_load(L[2 - 2 * s, 2 * s : 2 * s + 2, :])
            combine(mean_coefs(3 - 3 * s), GC, 3 - 3 * s)

    arrive((0,))
    both_sides(0, 0)
    both_sides(1, 1)
    arrive((3,))
    send_coefs(1, lambda copy: copy.start())
    both_sides(0, -1)
    both_sides(1, 0)
    both_sides(2, 1)
    for s in range(2):

        @pl.when(has[s])
        def _():
            GU[0, 4 - 3 * s, pl.ds(PAD, CY), :] = mean_rows(0, 7 - 6 * s)

    arrive((4,))
    for j in (1, 2):
        GU[1, 1 + j, pl.ds(PAD, CY), :] = coarse_step(GU, 0, 1 + j, GC, GL, j)
    for s in range(2):

        @pl.when(has[s])
        def _():
            j = 3 - 3 * s
            GU[1, 1 + j, pl.ds(PAD, CY), :] = coarse_step(GU, 0, 1 + j, GC, GL, j)

    for j in (1, 2):
        GG[j - 1] = coarse_step(GU, 1, 1 + j, GC, GL, j)

    arrive((5, 6))
    both_sides(1, -2)
    both_sides(1, -1)
    both_sides(2, -1)
    both_sides(2, 0)
    both_sides(3, 0)
    both_sides(3, 1)

    for j in range(2):
        mean = mean_rows(4, 3 + 2 * j)
        OWN[j] = jnp.where(m == 0, mean, mean - GG[j])

    def block_copy(pairs, initial):
        to = base + 2 * pairs
        slot = t - to + WIDE
        dst = W.at[0, pl.ds(2 * slot, 2), pl.ds(PAD, CY), :] if initial else RD.at[place, pl.ds(2 * slot, 2)]
        return pltpu.make_async_remote_copy(
            src_ref=OWN,
            dst_ref=dst,
            send_sem=s_send.at[PAIRS + pairs],
            recv_sem=s_recv.at[place, slot],
            device_id=device(head, leader_of(to)),
            device_id_type=MESH,
        )

    def block_arrives(j, slot, initial):
        pltpu.make_async_remote_copy(
            src_ref=OWN,
            dst_ref=W.at[0, pl.ds(2 * slot, 2), pl.ds(PAD, CY), :] if initial else RD.at[j, pl.ds(2 * slot, 2)],
            send_sem=s_send.at[0],
            recv_sem=s_recv.at[j, slot],
            device_id=device(sibling, t),
            device_id_type=MESH,
        ).wait_recv()

    def each_block(act):
        @pl.when(m == 0)
        def _():
            over_pairs(gives_block, lambda pairs: act(block_copy(pairs, True)))

        @pl.when(m > 0)
        def _():
            over_pairs(gives_block, lambda pairs: act(block_copy(pairs, False)))

    each_block(lambda copy: copy.start())

    def carry_copy(pairs):
        to = base + 2 * pairs
        return pltpu.make_async_remote_copy(
            src_ref=CARRY,
            dst_ref=W.at[0, pl.ds(2 * (WIDE - 2 * pairs), 4), pl.ds(PAD, CY), :],
            send_sem=c_send.at[PAIRS + pairs],
            recv_sem=c_recv.at[PAIRS - pairs],
            device_id=device(LAST, leader_of(to)),
            device_id_type=MESH,
        )

    def carry_arrives(pairs):
        pltpu.make_async_remote_copy(
            src_ref=CARRY,
            dst_ref=W.at[0, pl.ds(2 * (WIDE + 2 * pairs), 4), pl.ds(PAD, CY), :],
            send_sem=c_send.at[0],
            recv_sem=c_recv.at[PAIRS + pairs],
            device_id=device(sibling, t),
            device_id_type=MESH,
        ).wait_recv()

    def carry_pair(pairs):
        return inside(base + 2 * pairs)

    def forward(j, q):
        return pltpu.make_async_remote_copy(
            src_ref=GCB.at[j, pl.ds(2 * q, 2)],
            dst_ref=FWB,
            send_sem=fw_send.at[j, q],
            recv_sem=fw_recv.at[0],
            device_id=device(first + 1 + j, base + q),
            device_id_type=MESH,
        )

    def forwards(j, act):
        for q in range(2):

            @pl.when(jnp.logical_or(j < count - 1, base + q != t))
            def _():
                act(forward(j, q))

    send_across(every, m >= 0, lambda copy: copy.wait_send())
    send_along(every, lambda copy: copy.wait_send())
    for s in range(2):

        @pl.when(has[s])
        def _():
            to_sibling(s, False).wait_send()
    each_block(lambda copy: copy.wait_send())
    for e in range(2):
        send_coefs(e, lambda copy: copy.wait_send())

    @pl.when(lead)
    def _():
        def prepare(i):
            @pl.when(base - WIDE + i != t)
            def _():
                coefs_arrive(i)

            @pl.when(base - WIDE + i == t)
            def _():
                CF[i] = FL[...]

            for q in range(2):
                combine([CF[i, pl.ds((4 * q + f) * CY, CY), :] for f in range(4)], CC, 2 * i + q)
                CL[2 * i + q] = coarse_load(CF[i, pl.ds(8 * CY + 2 * q, 2), :])

        over_slots(count, prepare)

        def chain(j, carry):
            @pl.when(both(m == BREAK, j == 0))
            def _():
                over_slots(count, lambda i: block_arrives(0, i, True))

            @pl.when(j > 0)
            def _():
                over_slots(count - j, lambda i: block_arrives(j, i, False))

            @pl.when(both(m == LAST, j == 0))
            def _():
                over_pairs(carry_pair, carry_arrives)

            w = count - 1 - j

            @pl.when(j > 0)
            def _():
                def add(i, carry):
                    for q in range(4):
                        r = 2 * (WIDE - w - 1) + 4 * i + q
                        W[0, r, pl.ds(PAD, CY), :] = W[0, r, pl.ds(PAD, CY), :] + RD[j, r]
                    return carry

                lax.fori_loop(0, w + 2, add, 0)

            def step(k, start, rows):
                for q in range(rows):
                    W[1 - k, start + q, pl.ds(PAD, CY), :] = coarse_step(W, k, start + q, CC, CL, start + q)

            def sweep(k, start):
                def eight(i, carry):
                    step(k, start + 8 * i, 8)
                    return carry

                lax.fori_loop(0, jnp.where(w == 3, 2, jnp.where(w == 0, 0, 1)), eight, 0)

                @pl.when(jnp.logical_or(w == 0, w == 2))
                def _():
                    step(k, start + 4 * w, 4)

            sweep(0, 2 * (WIDE - w) - 1)
            step(0, 2 * (WIDE + w) + 3, 2)
            sweep(1, 2 * (WIDE - w))
            for q in range(4):
                GCB[j, q] = W[0, 2 * WIDE + q, pl.ds(PAD, CY), :]
            forwards(j, lambda copy: copy.start())
            return carry

        lax.fori_loop(0, count, chain, 0)

        own = t - base

        @pl.when(m == BREAK)
        def _():
            block_arrives(BREAK, WIDE + 1 - own, False)
            for q in range(2):
                RD[BREAK, 2 * WIDE + 2 * own + q] = OWN[q]
            for q in range(4):
                CARRY[q] = GCB[BREAK - 1, q] + RD[BREAK, 2 * WIDE + q]
            over_pairs(carry_pair, lambda pairs: carry_copy(pairs).start())

        for q in range(2):
            FWB[q] = GCB[count - 1, 2 * own + q]

    @pl.when(m == 0)
    def _():
        for q in range(2):
            FWB[q] = GG[q]

    @pl.when(jnp.logical_not(jnp.logical_or(lead, m == 0)))
    def _():
        forward(0, 0).wait_recv()

    for j in range(2):
        shift = FWB[j] - GG[j]
        for h in range(2):
            wide = gather(shift, lane(CY) // 2 + 64 * h)
            for p in range(2):
                UP[j, h, pl.ds(p, CY, stride=2), :] = wide
            for q in range(2):
                out[0, 2 * j + q, :, HALF * h : HALF * h + HALF] = U[4, 3 + 2 * j + q, h, rows, :] + UP[j, h]

    @pl.when(lead)
    def _():
        def handed(j, carry):
            forwards(j, lambda copy: copy.wait_send())
            return carry

        lax.fori_loop(0, count, handed, 0)

        @pl.when(m == BREAK)
        def _():
            over_pairs(carry_pair, lambda pairs: carry_copy(pairs).wait_send())


def shards(initial_states, material, conductivity, dispersivity, freundlich_k, freundlich_n, surface_load):
    hbm = pl.BlockSpec(memory_space=pltpu.HBM)
    block = (CY, HALF)
    dma = pltpu.SemaphoreType.DMA
    return pl.pallas_call(
        kernel,
        out_shape=pltpu.VMEM(initial_states.shape, F32),
        in_specs=[hbm] * 7,
        out_specs=pl.BlockSpec(memory_space=pltpu.VMEM),
        scratch_shapes=[
            pltpu.VMEM((5, 10, 2, FY + 2 * PAD, HALF), F32),
            pltpu.VMEM((8, 2, FY, HALF), jnp.int32),
            pltpu.VMEM((7, 8, 2, FY, HALF), F32),
            pltpu.VMEM((3, 8, HALF), F32),
            pltpu.VMEM((8, FY, HALF), F32),
            pltpu.VMEM((8 * CY + 8, HALF), F32),
            pltpu.VMEM((4, 6) + block, F32),
            pltpu.VMEM((4,) + block, F32),
            pltpu.VMEM((2, 6, CY + 2 * PAD, HALF), F32),
            pltpu.VMEM((2,) + block, F32),
            pltpu.VMEM((2,) + block, F32),
            pltpu.VMEM((4,) + block, F32),
            pltpu.VMEM((2, 2 * SLOTS, CY + 2 * PAD, HALF), F32),
            pltpu.VMEM((SLOTS, 8 * CY + 8, HALF), F32),
            pltpu.VMEM((2 * SLOTS, 6) + block, F32),
            pltpu.VMEM((2 * SLOTS,) + block, F32),
            pltpu.VMEM((LONGEST, 2 * SLOTS) + block, F32),
            pltpu.VMEM((LONGEST, 4) + block, F32),
            pltpu.VMEM((2,) + block, F32),
            pltpu.VMEM((2, 2, FY, HALF), F32),
            pltpu.VMEM((4, FY), F32),
            pltpu.SMEM((4, MATS), F32),
            dma((4,)),
            dma((5,)),
            dma((7, 2)),
            dma((7, 2)),
            dma((2,)),
            dma((2,)),
            dma((2, 2 * PAIRS + 1)),
            dma((SLOTS,)),
            dma((2 * PAIRS + 1,)),
            dma((LONGEST, SLOTS)),
            dma((2 * PAIRS + 1,)),
            dma((2 * PAIRS + 1,)),
            dma((LONGEST, 2)),
            dma((1,)),
        ],
        compiler_params=pltpu.CompilerParams(
            collective_id=0, has_side_effects=True, vmem_limit_bytes=63 * 1024 * 1024
        ),
    )(conductivity, dispersivity, freundlich_k, freundlich_n, surface_load, initial_states, material)


def solution(mesh):
    in_specs = (
        P("tm", "tile", None, None),
        P("tile", None, None),
        P(),
        P(),
        P(),
        P(),
        P("tile", None),
    )
    out_specs = P("tm", "tile", None, None)
    return jax.shard_map(shards, mesh=mesh, in_specs=in_specs, out_specs=out_specs, check_vma=False)
```

```python
import jax
import jax.numpy as jnp
from jax import lax
from jax.experimental import pallas as pl
from jax.experimental.pallas import tpu as pltpu
from jax.sharding import PartitionSpec as P

MESH = pl.DeviceIdType.MESH
F32 = jnp.float32
MATS = 12
TILES = 32
HALF = 128
FY = 64
CY = 32
PAD = 8
URGENT = 3
LAST = 7
BREAK = 3
LONGEST = max(BREAK, LAST - BREAK)
PAIRS = (LONGEST + 1) // 2
WIDE = 2 * PAIRS
SLOTS = 2 * WIDE + 2
COEFS_FROM = ((2, 5, 4), (6, 4, 1))


def lane(rows):
    return lax.broadcasted_iota(jnp.int32, (rows, HALF), 1)


def roll(value, shift):
    return pltpu.roll(value, shift, 1)


def gather(value, index):
    return jnp.take_along_axis(value, index, axis=1)


def update(um, u0, up, ym, yp, zm, zp, a, b, c, d, kn, n1):
    flux = a * ((up + zp) + (ym + yp)) + b * um + c * zm - d * u0
    power = jnp.exp2(n1 * jnp.log2(jnp.abs(u0) + 1.0))
    return u0 + flux / (1.0 + kn * power)


def squeeze_lanes(low, high):
    rows = low.shape[0]
    at = lane(rows)
    index = (2 * at) % HALF
    low = low + roll(low, HALF - 1)
    high = high + roll(high, HALF - 1)
    return jnp.where(at < HALF // 2, gather(low, index), gather(high, index))


def kernel(
    cond, disp, fk, fn, load, init, mat, out,
    U, M, C, L, LD, FL, GC, GL, GU, GG, OWN, CARRY, W, CF, CC, CL, RD, GCB, FWB, UP,
    LIN, TAB, in_sem, small_sem, halo_send, halo_recv, sib_send, sib_recv, cf_send, cf_recv, s_send, s_recv, c_send, c_recv, fw_send, fw_recv,
):
    m = lax.axis_index("tm")
    t = lax.axis_index("tile")

    def device(tm, tile):
        return {"tm": tm, "tile": tile}

    def inside(tile):
        return jnp.logical_and(tile >= 0, tile < TILES)

    base = t - t % 2

    def leader_of(base):
        return base + 1 - (base % 4) // 2

    head = jnp.where(m <= BREAK, BREAK, LAST)
    lead = jnp.logical_and(m == head, t == leader_of(base))
    first = jnp.where(m <= BREAK, 0, BREAK)
    count = head - first
    place = m - first
    width = head - m

    def both(a, b):
        return jnp.logical_and(a, b)

    def reaches(base, width):
        return both(both(base >= 0, base < TILES), both(base - width <= t, t <= base + 1 + width))

    def coefs_from(e, pairs):
        value = COEFS_FROM[e][PAIRS]
        for i in range(PAIRS):
            value = jnp.where(jnp.abs(pairs) == i, COEFS_FROM[e][i], value)
        return value

    def gives_coefs(e, pairs):
        to = base + 2 * pairs
        return both(both(reaches(to, (BREAK, LAST - BREAK)[e]), m == coefs_from(e, pairs)), t != leader_of(to))

    def gives_block(pairs):
        to = base + 2 * pairs
        return both(both(m < LAST, reaches(to, width)), jnp.logical_or(m < head, t != leader_of(to)))

    x = t % 4
    core = m % 2
    sibling = m + 1 - 2 * core
    far = (x == 0, x == 3)
    has = (t < TILES - 1, t > 0)

    loads = []
    for h in range(2):
        loads.append(pltpu.make_async_copy(mat.at[:, :, pl.ds(HALF * h, HALF)], M.at[pl.ds(2, 4), h], in_sem.at[h]))
    for h in range(2):
        loads.append(
            pltpu.make_async_copy(
                init.at[0, :, :, pl.ds(HALF * h, HALF)], U.at[0, pl.ds(3, 4), h, pl.ds(PAD, FY), :], in_sem.at[2 + h]
            )
        )
    small = [pltpu.make_async_copy(load, LIN, small_sem.at[0])]
    for i, ref in enumerate((cond, disp, fk, fn)):
        small.append(pltpu.make_async_copy(ref, TAB.at[i], small_sem.at[1 + i]))
    for copy in loads + small:
        copy.start()

    barrier = pltpu.get_barrier_semaphore()

    def greet(tm, tile, when):
        @pl.when(jnp.logical_and(when, inside(tile)))
        def _():
            pl.semaphore_signal(barrier, inc=1, device_id=device(tm, tile), device_id_type=MESH)

    greet(m, t - 1, m >= 0)
    greet(m, t + 1, m >= 0)
    greet(sibling, t, m >= 0)

    for e, (slice_, start) in enumerate(((BREAK, 0), (LAST, BREAK))):

        @pl.when(both(lead, m == slice_))
        def _():
            reach = slice_ - start
            for j in range(reach):
                if j == 0 and e == 1:

                    def greet_pair(i, carry):
                        to = base + 2 * (i - PAIRS)
                        greet(BREAK, leader_of(to), m >= 0)
                        return carry

                    lax.fori_loop(0, 2 * PAIRS + 1, greet_pair, 0)
                else:

                    def greet_tile(i, carry):
                        greet(start + j, base + i - (reach - j), m >= 0)
                        return carry

                    lax.fori_loop(0, 2 + 2 * (reach - j), greet_tile, 0)
            for pairs in range(-PAIRS, PAIRS + 1):
                for i in (2 * pairs, 2 * pairs + 1):
                    if -reach <= i <= 1 + reach:
                        greet(COEFS_FROM[e][abs(pairs)], base + i, base + i != t)
            if e == 0:
                greet(BREAK, 2 * base + 1 - t, m >= 0)

    greet(head, leader_of(base), both(jnp.logical_not(lead), m > 0))

    def add_pair(i, total):
        pairs = i - PAIRS
        for e in range(2):
            total = total + jnp.where(gives_coefs(e, pairs), 1, 0)
        total = total + jnp.where(gives_block(pairs), 1, 0)
        return total + jnp.where(both(both(lead, m == BREAK), inside(base + 2 * pairs)), 1, 0)

    expected = 1 + jnp.where(t > 0, 1, 0) + jnp.where(t < TILES - 1, 1, 0) + jnp.where(lead, 2 * count - 1, 0)
    expected = expected + lax.fori_loop(0, 2 * PAIRS + 1, add_pair, 0)

    rows = pl.ds(PAD, FY)

    def halo(item, s, arriving):
        src, dst = (
            (U.at[0, 3 + 3 * s, :, rows, :], U.at[0, 7 - 5 * s, :, rows, :]),
            (M.at[pl.ds(2 + 2 * s, 2)], M.at[pl.ds(6 - 6 * s, 2)]),
            (L.at[1], L.at[2 - 2 * s]),
            (U.at[0, 4 + s, :, rows, :], U.at[0, 8 - 7 * s, :, rows, :]),
            (GU.at[0, 3 - s, pl.ds(PAD, CY), :], GU.at[0, 5 - 5 * s, pl.ds(PAD, CY), :]),
            (U.at[1, 4, :, rows, :], U.at[1, 8 - 8 * s, :, rows, :]),
            (U.at[1, 5, :, rows, :], U.at[1, 9 - 8 * s, :, rows, :]),
        )[item]
        toward = 2 * s - 1
        return pltpu.make_async_remote_copy(
            src_ref=src,
            dst_ref=dst,
            send_sem=halo_send.at[item, s],
            recv_sem=halo_recv.at[item, s],
            device_id=device(m, t - toward if arriving else t + toward),
            device_id_type=MESH,
        )

    def to_sibling(s):
        rows = pl.ds(6 - 6 * s, 2)
        return pltpu.make_async_remote_copy(
            src_ref=M.at[rows],
            dst_ref=M.at[rows],
            send_sem=sib_send.at[s],
            recv_sem=sib_recv.at[s],
            device_id=device(sibling, t),
            device_id_type=MESH,
        )

    sends = (t > 0, t < TILES - 1)

    def send_across(items, when, act):
        for s in range(2):

            @pl.when(jnp.logical_and(when, jnp.logical_and(sends[s], far[s])))
            def _():
                for item in items:
                    if item == 1:

                        @pl.when(core == 1)
                        def _():
                            act(halo(item, s, False))

                    else:
                        act(halo(item, s, False))

    def send_along(items, act):
        for item in items:
            for s in range(2):

                @pl.when(both(both(sends[s], jnp.logical_not(far[s])), jnp.logical_or(item != 1, core == 1)))
                def _():
                    act(halo(item, s, False))

    every = (1, 2, 0, 3, 4, 5, 6)
    urgent = m < URGENT

    def arrive(items):
        for item in items:
            for s in range(2):

                @pl.when(both(has[s], jnp.logical_or(item != 1, core == 1)))
                def _():
                    halo(item, s, True).wait_recv()

    for copy in small[:1] + loads:
        copy.wait()
    L[1] = jnp.zeros((8, HALF), F32)
    L[1, 0:4, 0:FY] = LIN[...]
    pl.semaphore_wait(barrier, expected)
    send_across(every[:2], m >= 0, lambda copy: copy.start())
    send_across(every[2:4], urgent, lambda copy: copy.start())
    send_along(every[:4], lambda copy: copy.start())

    zero = jnp.zeros((PAD, HALF), F32)

    def blank_fine(i, carry):
        for h in range(2):
            U[i // 10, i % 10, h, pl.ds(0, PAD), :] = zero
            U[i // 10, i % 10, h, pl.ds(PAD + FY, PAD), :] = zero
        return carry

    lax.fori_loop(3, 7, blank_fine, 0)

    at = lane(8)
    tables = []
    for copy in small[1:]:
        copy.wait()
    for k in range(4):
        table = jnp.zeros((8, HALF), F32)
        for i in range(MATS):
            table = jnp.where(at == i, TAB[k, i], table)
        tables.append(table)
    t_cond, t_disp, t_k, t_n = tables
    t_a = t_disp * t_cond
    tables = [t_a, t_a + 0.5 * t_cond, t_a + 0.3 * t_cond, 6.0 * t_a + 0.8 * t_cond, t_k * t_n, t_n - 1.0, t_k]

    def look_up(r):
        for h in range(2):
            index = M[r, h]
            for f, table in enumerate(tables):
                value = gather(jnp.broadcast_to(table[0:1], (FY, HALF)), index)
                if f == 2 and h == 0:
                    value = jnp.where(lane(FY) == 0, 1.0, value)
                C[f, r, h] = value

    def spread_load(s, i, r):
        row = jnp.broadcast_to(L[s, i : i + 1, :], (FY, HALF))
        here = lax.broadcasted_iota(jnp.int32, (FY, HALF), 0) == lane(FY)
        total = jnp.sum(jnp.where(here, row, 0.0), axis=1, keepdims=True)
        LD[r] = jnp.broadcast_to(total, (FY, HALF))

    def coarse_load(rows):
        row = jnp.broadcast_to(rows[0:1] + rows[1:2], (CY, HALF))
        here = lax.broadcasted_iota(jnp.int32, (CY, HALF), 0) == lane(CY) // 2
        total = jnp.sum(jnp.where(here, row, 0.0), axis=1, keepdims=True)
        return jnp.broadcast_to(0.25 * total, (CY, HALF))

    def fine_step(k, r):
        for y in (0, 32):
            rows = pl.ds(PAD + y, 32)
            here = pl.ds(y, 32)
            low, high = U[k, r, 0, rows, :], U[k, r, 1, rows, :]
            at = lane(32)
            back = (roll(low, 1), roll(high, 1))
            ahead = (roll(low, HALF - 1), roll(high, HALF - 1))
            zms = (jnp.where(at == 0, LD[r - 1, here], back[0]), jnp.where(at == 0, back[0], back[1]))
            zps = (jnp.where(at == HALF - 1, ahead[1], ahead[0]), jnp.where(at == HALF - 1, 0.0, ahead[1]))
            for h in range(2):
                U[k + 1, r, h, rows, :] = update(
                    U[k, r - 1, h, rows, :],
                    (low, high)[h],
                    U[k, r + 1, h, rows, :],
                    U[k, r, h, pl.ds(PAD + y - 1, 32), :],
                    U[k, r, h, pl.ds(PAD + y + 1, 32), :],
                    zms[h],
                    zps[h],
                    *[C[f, r - 1, h, here] for f in range(6)],
                )

    def mean_rows(k, r):
        halves = []
        for h in range(2):
            parts = [U[k, r + q, h, pl.ds(PAD + p, CY, stride=2), :] for q in range(2) for p in range(2)]
            halves.append((parts[0] + parts[1]) + (parts[2] + parts[3]))
        return 0.125 * squeeze_lanes(*halves)

    def mean_coefs(j):
        means = []
        for f in (0, 1, 6, 5):
            halves = []
            for h in range(2):
                parts = [C[f, 2 * j + q, h, pl.ds(p, CY, stride=2), :] for q in range(2) for p in range(2)]
                halves.append((parts[0] + parts[1]) + (parts[2] + parts[3]))
            means.append(0.125 * squeeze_lanes(*halves))
        return 0.5 * means[0], 2.0 * (means[1] - means[0]), means[2] * (means[3] + 1.0), means[3]

    def combine(fields, dst, r):
        a, cond, kn, n1 = fields
        dst[r, 0] = a
        dst[r, 1] = a + 0.5 * cond
        dst[r, 2] = jnp.where(lane(CY) == 0, 1.0, a + 0.3 * cond)
        dst[r, 3] = 6.0 * a + 0.8 * cond
        dst[r, 4] = kn
        dst[r, 5] = n1

    def coarse_step(src, k, r, coefs, inflow, place):
        rows = pl.ds(PAD, CY)
        at = lane(CY)
        u0 = src[k, r, rows, :]
        return update(
            src[k, r - 1, rows, :],
            u0,
            src[k, r + 1, rows, :],
            src[k, r, pl.ds(PAD - 1, CY), :],
            src[k, r, pl.ds(PAD + 1, CY), :],
            jnp.where(at == 0, inflow[place], roll(u0, 1)),
            jnp.where(at == HALF - 1, 0.0, roll(u0, HALF - 1)),
            *[coefs[place, f] for f in range(6)],
        )

    for i in range(4):
        spread_load(1, i, 2 + i)

    def own_rows(r, carry):
        look_up(r)
        return carry

    lax.fori_loop(3, 5, own_rows, 0)

    def inner_rows(r, carry):
        fine_step(0, r)
        return carry

    lax.fori_loop(4, 6, inner_rows, 0)
    for j in range(2):
        GU[0, 2 + j, pl.ds(PAD, CY), :] = mean_rows(0, 3 + 2 * j)
    send_across(every[4:], urgent, lambda copy: copy.start())
    send_along(every[4:], lambda copy: copy.start())

    def both_sides(k, near):
        for s in range(2):
            r = 3 + (near if s == 1 else 3 - near)
            if near >= 0:
                fine_step(k, r)
            else:

                @pl.when(has[s])
                def _():
                    fine_step(k, r)

    lax.fori_loop(0, 50, blank_fine, 0)

    def blank_coarse(i, carry):
        for k in range(2):
            W[k, i, pl.ds(0, PAD), :] = zero
            W[k, i, pl.ds(PAD + CY, PAD), :] = zero
        return carry

    lax.fori_loop(0, 2 * SLOTS, blank_coarse, 0)
    for k in range(2):
        for r in range(6):
            GU[k, r, pl.ds(0, PAD), :] = zero
            GU[k, r, pl.ds(PAD + CY, PAD), :] = zero
    for s in range(2):

        @pl.when(jnp.logical_not(has[s]))
        def _():
            def clear(i, carry):
                for h in range(2):
                    U[i // 3, 7 - 7 * s + i % 3, h, pl.ds(PAD, FY), :] = jnp.zeros((FY, HALF), F32)
                return carry

            lax.fori_loop(0, 12, clear, 0)
            for k in range(2):
                for r in range(2):
                    GU[k, 4 - 4 * s + r, pl.ds(PAD, CY), :] = jnp.zeros((CY, HALF), F32)

    @pl.when(lead)
    def _():
        def clear(i, carry):
            @pl.when(jnp.logical_not(inside(base + i - WIDE)))
            def _():
                for q in range(2):
                    for f in range(6):
                        CC[2 * i + q, f] = jnp.zeros((CY, HALF), F32)
                    CL[2 * i + q] = jnp.zeros((CY, HALF), F32)
                    W[0, 2 * i + q, pl.ds(PAD, CY), :] = jnp.zeros((CY, HALF), F32)
                    for j in range(LONGEST):
                        RD[j, 2 * i + q] = jnp.zeros((CY, HALF), F32)

            return carry

        lax.fori_loop(0, SLOTS, clear, 0)

    look_up(2)
    look_up(5)
    for q in range(2):
        fields = mean_coefs(1 + q)
        for f in range(4):
            FL[pl.ds((4 * q + f) * CY, CY), :] = fields[f]
        combine(fields, GC, 1 + q)
        GL[1 + q] = coarse_load(L[1, 2 * q : 2 * q + 2, :])
    FL[pl.ds(8 * CY, 8), :] = L[1]

    def coefs_copy(e, pairs):
        to = base + 2 * pairs
        slot = t - to + WIDE
        return pltpu.make_async_remote_copy(
            src_ref=FL,
            dst_ref=CF.at[slot],
            send_sem=cf_send.at[e, PAIRS + pairs],
            recv_sem=cf_recv.at[slot],
            device_id=device((BREAK, LAST)[e], leader_of(to)),
            device_id_type=MESH,
        )

    def coefs_arrive(slot):
        pltpu.make_async_remote_copy(
            src_ref=FL,
            dst_ref=CF.at[slot],
            send_sem=cf_send.at[0, 0],
            recv_sem=cf_recv.at[slot],
            device_id=device(sibling, t),
            device_id_type=MESH,
        ).wait_recv()

    def over_pairs(gives, act):
        def body(i, carry):
            @pl.when(gives(i - PAIRS))
            def _():
                act(i - PAIRS)

            return carry

        lax.fori_loop(0, 2 * PAIRS + 1, body, 0)

    def over_slots(width, act):
        def body(i, carry):
            @pl.when(inside(base - WIDE + i))
            def _():
                act(i)

            return carry

        lax.fori_loop(WIDE - width, WIDE + 2 + width, body, 0)

    def send_coefs(e, act):
        over_pairs(lambda pairs: gives_coefs(e, pairs), lambda pairs: act(coefs_copy(e, pairs)))

    send_coefs(0, lambda copy: copy.start())

    arrive((1,))
    for s in range(2):

        @pl.when(both(has[s], core == 1))
        def _():
            to_sibling(s).start()

    arrive((2,))

    send_across(every[2:], jnp.logical_not(urgent), lambda copy: copy.start())
    for s in range(2):

        @pl.when(both(has[s], core == 0))
        def _():
            to_sibling(s).wait_recv()

    for s in range(2):

        @pl.when(has[s])
        def _():
            for q in range(2):
                r = 6 - 6 * s + q
                look_up(r)
                spread_load(2 - 2 * s, q + 2 * s, r)
            GL[3 - 3 * s] = coarse_load(L[2 - 2 * s, 2 * s : 2 * s + 2, :])
            combine(mean_coefs(3 - 3 * s), GC, 3 - 3 * s)

    arrive((0,))
    both_sides(0, 0)
    both_sides(1, 1)
    arrive((3,))
    @pl.when(m > 1)
    def _():
        send_coefs(1, lambda copy: copy.start())

    both_sides(0, -1)
    both_sides(1, 0)
    both_sides(2, 1)
    for s in range(2):

        @pl.when(has[s])
        def _():
            GU[0, 4 - 3 * s, pl.ds(PAD, CY), :] = mean_rows(0, 7 - 6 * s)

    arrive((4,))
    for j in (1, 2):
        GU[1, 1 + j, pl.ds(PAD, CY), :] = coarse_step(GU, 0, 1 + j, GC, GL, j)
    for s in range(2):

        @pl.when(has[s])
        def _():
            j = 3 - 3 * s
            GU[1, 1 + j, pl.ds(PAD, CY), :] = coarse_step(GU, 0, 1 + j, GC, GL, j)

    for j in (1, 2):
        GG[j - 1] = coarse_step(GU, 1, 1 + j, GC, GL, j)

    arrive((5, 6))
    both_sides(1, -2)
    both_sides(1, -1)
    both_sides(2, -1)
    both_sides(2, 0)
    both_sides(3, 0)
    both_sides(3, 1)

    for j in range(2):
        mean = mean_rows(4, 3 + 2 * j)
        OWN[j] = jnp.where(m == 0, mean, mean - GG[j])

    def block_copy(pairs, initial):
        to = base + 2 * pairs
        slot = t - to + WIDE
        dst = W.at[0, pl.ds(2 * slot, 2), pl.ds(PAD, CY), :] if initial else RD.at[place, pl.ds(2 * slot, 2)]
        return pltpu.make_async_remote_copy(
            src_ref=OWN,
            dst_ref=dst,
            send_sem=s_send.at[PAIRS + pairs],
            recv_sem=s_recv.at[place, slot],
            device_id=device(head, leader_of(to)),
            device_id_type=MESH,
        )

    def block_arrives(j, slot, initial):
        pltpu.make_async_remote_copy(
            src_ref=OWN,
            dst_ref=W.at[0, pl.ds(2 * slot, 2), pl.ds(PAD, CY), :] if initial else RD.at[j, pl.ds(2 * slot, 2)],
            send_sem=s_send.at[0],
            recv_sem=s_recv.at[j, slot],
            device_id=device(sibling, t),
            device_id_type=MESH,
        ).wait_recv()

    def each_block(act):
        @pl.when(m == 0)
        def _():
            over_pairs(gives_block, lambda pairs: act(block_copy(pairs, True)))

        @pl.when(m > 0)
        def _():
            over_pairs(gives_block, lambda pairs: act(block_copy(pairs, False)))

    each_block(lambda copy: copy.start())

    @pl.when(m == 1)
    def _():
        send_coefs(1, lambda copy: copy.start())


    def carry_copy(pairs):
        to = base + 2 * pairs
        return pltpu.make_async_remote_copy(
            src_ref=CARRY,
            dst_ref=W.at[0, pl.ds(2 * (WIDE - 2 * pairs), 4), pl.ds(PAD, CY), :],
            send_sem=c_send.at[PAIRS + pairs],
            recv_sem=c_recv.at[PAIRS - pairs],
            device_id=device(LAST, leader_of(to)),
            device_id_type=MESH,
        )

    def carry_arrives(pairs):
        pltpu.make_async_remote_copy(
            src_ref=CARRY,
            dst_ref=W.at[0, pl.ds(2 * (WIDE + 2 * pairs), 4), pl.ds(PAD, CY), :],
            send_sem=c_send.at[0],
            recv_sem=c_recv.at[PAIRS + pairs],
            device_id=device(sibling, t),
            device_id_type=MESH,
        ).wait_recv()

    def carry_pair(pairs):
        return inside(base + 2 * pairs)

    def forward(j, q):
        return pltpu.make_async_remote_copy(
            src_ref=GCB.at[j, pl.ds(2 * q, 2)],
            dst_ref=FWB,
            send_sem=fw_send.at[j, q],
            recv_sem=fw_recv.at[0],
            device_id=device(first + 1 + j, base + q),
            device_id_type=MESH,
        )

    def forwards(j, act):
        for q in range(2):

            @pl.when(jnp.logical_or(j < count - 1, base + q != t))
            def _():
                act(forward(j, q))

    send_across(every, m >= 0, lambda copy: copy.wait_send())
    send_along(every, lambda copy: copy.wait_send())
    for s in range(2):

        @pl.when(both(has[s], core == 1))
        def _():
            to_sibling(s).wait_send()
    each_block(lambda copy: copy.wait_send())
    for e in range(2):
        send_coefs(e, lambda copy: copy.wait_send())

    @pl.when(lead)
    def _():
        def prepare(i):
            @pl.when(base - WIDE + i != t)
            def _():
                coefs_arrive(i)

            @pl.when(base - WIDE + i == t)
            def _():
                CF[i] = FL[...]

            for q in range(2):
                combine([CF[i, pl.ds((4 * q + f) * CY, CY), :] for f in range(4)], CC, 2 * i + q)
                CL[2 * i + q] = coarse_load(CF[i, pl.ds(8 * CY + 2 * q, 2), :])

        over_slots(count, prepare)

        def chain(j, carry):
            @pl.when(both(m == BREAK, j == 0))
            def _():
                over_slots(count, lambda i: block_arrives(0, i, True))

            @pl.when(j > 0)
            def _():
                over_slots(count - j, lambda i: block_arrives(j, i, False))

            @pl.when(both(m == LAST, j == 0))
            def _():
                over_pairs(carry_pair, carry_arrives)

            w = count - 1 - j

            @pl.when(j > 0)
            def _():
                def add(i, carry):
                    for q in range(4):
                        r = 2 * (WIDE - w - 1) + 4 * i + q
                        W[0, r, pl.ds(PAD, CY), :] = W[0, r, pl.ds(PAD, CY), :] + RD[j, r]
                    return carry

                lax.fori_loop(0, w + 2, add, 0)

            def step(k, start, rows):
                for q in range(rows):
                    W[1 - k, start + q, pl.ds(PAD, CY), :] = coarse_step(W, k, start + q, CC, CL, start + q)

            def sweep(k, start):
                def eight(i, carry):
                    step(k, start + 8 * i, 8)
                    return carry

                lax.fori_loop(0, jnp.where(w == 3, 2, jnp.where(w == 0, 0, 1)), eight, 0)

                @pl.when(jnp.logical_or(w == 0, w == 2))
                def _():
                    step(k, start + 4 * w, 4)

            sweep(0, 2 * (WIDE - w) - 1)
            step(0, 2 * (WIDE + w) + 3, 2)
            sweep(1, 2 * (WIDE - w))
            for q in range(4):
                GCB[j, q] = W[0, 2 * WIDE + q, pl.ds(PAD, CY), :]
            forwards(j, lambda copy: copy.start())
            return carry

        lax.fori_loop(0, count, chain, 0)

        own = t - base

        @pl.when(m == BREAK)
        def _():
            block_arrives(BREAK, WIDE + 1 - own, False)
            for q in range(2):
                RD[BREAK, 2 * WIDE + 2 * own + q] = OWN[q]
            for q in range(4):
                CARRY[q] = GCB[BREAK - 1, q] + RD[BREAK, 2 * WIDE + q]
            over_pairs(carry_pair, lambda pairs: carry_copy(pairs).start())

        for q in range(2):
            FWB[q] = GCB[count - 1, 2 * own + q]

    @pl.when(m == 0)
    def _():
        for q in range(2):
            FWB[q] = GG[q]

    @pl.when(jnp.logical_not(jnp.logical_or(lead, m == 0)))
    def _():
        forward(0, 0).wait_recv()

    for j in range(2):
        shift = FWB[j] - GG[j]
        for h in range(2):
            wide = gather(shift, lane(CY) // 2 + 64 * h)
            for p in range(2):
                UP[j, h, pl.ds(p, CY, stride=2), :] = wide
            for q in range(2):
                out[0, 2 * j + q, :, HALF * h : HALF * h + HALF] = U[4, 3 + 2 * j + q, h, rows, :] + UP[j, h]

    @pl.when(lead)
    def _():
        def handed(j, carry):
            forwards(j, lambda copy: copy.wait_send())
            return carry

        lax.fori_loop(0, count, handed, 0)

        @pl.when(m == BREAK)
        def _():
            over_pairs(carry_pair, lambda pairs: carry_copy(pairs).wait_send())


def shards(initial_states, material, conductivity, dispersivity, freundlich_k, freundlich_n, surface_load):
    hbm = pl.BlockSpec(memory_space=pltpu.HBM)
    block = (CY, HALF)
    dma = pltpu.SemaphoreType.DMA
    return pl.pallas_call(
        kernel,
        out_shape=pltpu.VMEM(initial_states.shape, F32),
        in_specs=[hbm] * 7,
        out_specs=pl.BlockSpec(memory_space=pltpu.VMEM),
        scratch_shapes=[
            pltpu.VMEM((5, 10, 2, FY + 2 * PAD, HALF), F32),
            pltpu.VMEM((8, 2, FY, HALF), jnp.int32),
            pltpu.VMEM((7, 8, 2, FY, HALF), F32),
            pltpu.VMEM((3, 8, HALF), F32),
            pltpu.VMEM((8, FY, HALF), F32),
            pltpu.VMEM((8 * CY + 8, HALF), F32),
            pltpu.VMEM((4, 6) + block, F32),
            pltpu.VMEM((4,) + block, F32),
            pltpu.VMEM((2, 6, CY + 2 * PAD, HALF), F32),
            pltpu.VMEM((2,) + block, F32),
            pltpu.VMEM((2,) + block, F32),
            pltpu.VMEM((4,) + block, F32),
            pltpu.VMEM((2, 2 * SLOTS, CY + 2 * PAD, HALF), F32),
            pltpu.VMEM((SLOTS, 8 * CY + 8, HALF), F32),
            pltpu.VMEM((2 * SLOTS, 6) + block, F32),
            pltpu.VMEM((2 * SLOTS,) + block, F32),
            pltpu.VMEM((LONGEST, 2 * SLOTS) + block, F32),
            pltpu.VMEM((LONGEST, 4) + block, F32),
            pltpu.VMEM((2,) + block, F32),
            pltpu.VMEM((2, 2, FY, HALF), F32),
            pltpu.VMEM((4, FY), F32),
            pltpu.SMEM((4, MATS), F32),
            dma((4,)),
            dma((5,)),
            dma((7, 2)),
            dma((7, 2)),
            dma((2,)),
            dma((2,)),
            dma((2, 2 * PAIRS + 1)),
            dma((SLOTS,)),
            dma((2 * PAIRS + 1,)),
            dma((LONGEST, SLOTS)),
            dma((2 * PAIRS + 1,)),
            dma((2 * PAIRS + 1,)),
            dma((LONGEST, 2)),
            dma((1,)),
        ],
        compiler_params=pltpu.CompilerParams(
            collective_id=0, has_side_effects=True, vmem_limit_bytes=63 * 1024 * 1024
        ),
    )(conductivity, dispersivity, freundlich_k, freundlich_n, surface_load, initial_states, material)


def solution(mesh):
    in_specs = (
        P("tm", "tile", None, None),
        P("tile", None, None),
        P(),
        P(),
        P(),
        P(),
        P("tile", None),
    )
    out_specs = P("tm", "tile", None, None)
    return jax.shard_map(shards, mesh=mesh, in_specs=in_specs, out_specs=out_specs, check_vma=False)
```

```python
import jax
import jax.numpy as jnp
from jax import lax
from jax.experimental import pallas as pl
from jax.experimental.pallas import tpu as pltpu
from jax.sharding import PartitionSpec as P

MESH = pl.DeviceIdType.MESH
F32 = jnp.float32
MATS = 12
TILES = 32
HALF = 128
FY = 64
CY = 32
PAD = 8
URGENT = 3
LAST = 7
BREAK = 3
LONGEST = max(BREAK, LAST - BREAK)
PAIRS = (LONGEST + 1) // 2
WIDE = 2 * PAIRS
SLOTS = 2 * WIDE + 2
COEFS_FROM = ((2, 5, 4), (6, 4, 1))


def lane(rows):
    return lax.broadcasted_iota(jnp.int32, (rows, HALF), 1)


def roll(value, shift):
    return pltpu.roll(value, shift, 1)


def gather(value, index):
    return jnp.take_along_axis(value, index, axis=1)


def update(um, u0, up, ym, yp, zm, zp, a, b, c, d, kn, n1):
    flux = a * ((up + zp) + (ym + yp)) + b * um + c * zm - d * u0
    power = jnp.exp2(n1 * jnp.log2(jnp.abs(u0) + 1.0))
    return u0 + flux / (1.0 + kn * power)


def squeeze_lanes(low, high):
    rows = low.shape[0]
    at = lane(rows)
    index = (2 * at) % HALF
    low = low + roll(low, HALF - 1)
    high = high + roll(high, HALF - 1)
    return jnp.where(at < HALF // 2, gather(low, index), gather(high, index))


def kernel(
    cond, disp, fk, fn, load, init, mat, out,
    U, M, C, L, LD, FL, GC, GL, GU, GG, OWN, CARRY, W, CF, CC, CL, RD, GCB, FWB, UP,
    LIN, TAB, in_sem, small_sem, halo_send, halo_recv, sib_send, sib_recv, cf_send, cf_recv, s_send, s_recv, c_send, c_recv, fw_send, fw_recv,
):
    m = lax.axis_index("tm")
    t = lax.axis_index("tile")

    def device(tm, tile):
        return {"tm": tm, "tile": tile}

    def inside(tile):
        return jnp.logical_and(tile >= 0, tile < TILES)

    base = t - t % 2

    def leader_of(base):
        return base + 1 - (base % 4) // 2

    head = jnp.where(m <= BREAK, BREAK, LAST)
    lead = jnp.logical_and(m == head, t == leader_of(base))
    first = jnp.where(m <= BREAK, 0, BREAK)
    count = head - first
    place = m - first
    width = head - m

    def both(a, b):
        return jnp.logical_and(a, b)

    def reaches(base, width):
        return both(both(base >= 0, base < TILES), both(base - width <= t, t <= base + 1 + width))

    def coefs_from(e, pairs):
        value = COEFS_FROM[e][PAIRS]
        for i in range(PAIRS):
            value = jnp.where(jnp.abs(pairs) == i, COEFS_FROM[e][i], value)
        return value

    def gives_coefs(e, pairs):
        to = base + 2 * pairs
        return both(both(reaches(to, (BREAK, LAST - BREAK)[e]), m == coefs_from(e, pairs)), t != leader_of(to))

    def gives_block(pairs):
        to = base + 2 * pairs
        return both(both(m < LAST, reaches(to, width)), jnp.logical_or(m < head, t != leader_of(to)))

    x = t % 4
    core = m % 2
    sibling = m + 1 - 2 * core
    far = (x == 0, x == 3)
    has = (t < TILES - 1, t > 0)

    loads = []
    for h in range(2):
        loads.append(pltpu.make_async_copy(mat.at[:, :, pl.ds(HALF * h, HALF)], M.at[pl.ds(2, 4), h], in_sem.at[h]))
    for h in range(2):
        loads.append(
            pltpu.make_async_copy(
                init.at[0, :, :, pl.ds(HALF * h, HALF)], U.at[0, pl.ds(3, 4), h, pl.ds(PAD, FY), :], in_sem.at[2 + h]
            )
        )
    small = [pltpu.make_async_copy(load, LIN, small_sem.at[0])]
    for i, ref in enumerate((cond, disp, fk, fn)):
        small.append(pltpu.make_async_copy(ref, TAB.at[i], small_sem.at[1 + i]))
    for copy in loads + small:
        copy.start()

    barrier = pltpu.get_barrier_semaphore()

    def greet(tm, tile, when):
        @pl.when(jnp.logical_and(when, inside(tile)))
        def _():
            pl.semaphore_signal(barrier, inc=1, device_id=device(tm, tile), device_id_type=MESH)

    greet(m, t - 1, m >= 0)
    greet(m, t + 1, m >= 0)
    greet(sibling, t, m >= 0)

    for e, (slice_, start) in enumerate(((BREAK, 0), (LAST, BREAK))):

        @pl.when(both(lead, m == slice_))
        def _():
            reach = slice_ - start
            for j in range(reach):
                if j == 0 and e == 1:

                    def greet_pair(i, carry):
                        to = base + 2 * (i - PAIRS)
                        greet(BREAK, leader_of(to), m >= 0)
                        return carry

                    lax.fori_loop(0, 2 * PAIRS + 1, greet_pair, 0)
                else:

                    def greet_tile(i, carry):
                        greet(start + j, base + i - (reach - j), m >= 0)
                        return carry

                    lax.fori_loop(0, 2 + 2 * (reach - j), greet_tile, 0)
            for pairs in range(-PAIRS, PAIRS + 1):
                for i in (2 * pairs, 2 * pairs + 1):
                    if -reach <= i <= 1 + reach:
                        greet(COEFS_FROM[e][abs(pairs)], base + i, base + i != t)
            if e == 0:
                greet(BREAK, 2 * base + 1 - t, m >= 0)

    greet(head, leader_of(base), both(jnp.logical_not(lead), m > 0))

    def add_pair(i, total):
        pairs = i - PAIRS
        for e in range(2):
            total = total + jnp.where(gives_coefs(e, pairs), 1, 0)
        total = total + jnp.where(gives_block(pairs), 1, 0)
        return total + jnp.where(both(both(lead, m == BREAK), inside(base + 2 * pairs)), 1, 0)

    expected = 1 + jnp.where(t > 0, 1, 0) + jnp.where(t < TILES - 1, 1, 0) + jnp.where(lead, 2 * count - 1, 0)
    expected = expected + lax.fori_loop(0, 2 * PAIRS + 1, add_pair, 0)

    rows = pl.ds(PAD, FY)

    def halo(item, s, arriving):
        src, dst = (
            (U.at[0, 3 + 3 * s, :, rows, :], U.at[0, 7 - 5 * s, :, rows, :]),
            (M.at[pl.ds(2 + 2 * s, 2)], M.at[pl.ds(6 - 6 * s, 2)]),
            (L.at[1], L.at[2 - 2 * s]),
            (U.at[0, 4 + s, :, rows, :], U.at[0, 8 - 7 * s, :, rows, :]),
            (GU.at[0, 3 - s, pl.ds(PAD, CY), :], GU.at[0, 5 - 5 * s, pl.ds(PAD, CY), :]),
            (U.at[1, 4, :, rows, :], U.at[1, 8 - 8 * s, :, rows, :]),
            (U.at[1, 5, :, rows, :], U.at[1, 9 - 8 * s, :, rows, :]),
        )[item]
        toward = 2 * s - 1
        return pltpu.make_async_remote_copy(
            src_ref=src,
            dst_ref=dst,
            send_sem=halo_send.at[item, s],
            recv_sem=halo_recv.at[item, s],
            device_id=device(m, t - toward if arriving else t + toward),
            device_id_type=MESH,
        )

    def to_sibling(s):
        rows = pl.ds(6 - 6 * s, 2)
        return pltpu.make_async_remote_copy(
            src_ref=M.at[rows],
            dst_ref=M.at[rows],
            send_sem=sib_send.at[s],
            recv_sem=sib_recv.at[s],
            device_id=device(sibling, t),
            device_id_type=MESH,
        )

    sends = (t > 0, t < TILES - 1)

    def send_across(items, when, act):
        for s in range(2):

            @pl.when(jnp.logical_and(when, jnp.logical_and(sends[s], far[s])))
            def _():
                for item in items:
                    if item == 1:

                        @pl.when(core == 1)
                        def _():
                            act(halo(item, s, False))

                    else:
                        act(halo(item, s, False))

    def send_along(items, act):
        for item in items:
            for s in range(2):

                @pl.when(both(both(sends[s], jnp.logical_not(far[s])), jnp.logical_or(item != 1, core == 1)))
                def _():
                    act(halo(item, s, False))

    every = (1, 2, 0, 3, 4, 5, 6)
    urgent = m < URGENT

    def arrive(items):
        for item in items:
            for s in range(2):

                @pl.when(both(has[s], jnp.logical_or(item != 1, core == 1)))
                def _():
                    halo(item, s, True).wait_recv()

    for copy in small[:1] + loads:
        copy.wait()
    L[1] = jnp.zeros((8, HALF), F32)
    L[1, 0:4, 0:FY] = LIN[...]
    pl.semaphore_wait(barrier, expected)
    send_across(every[:2], m >= 0, lambda copy: copy.start())
    send_across(every[2:4], urgent, lambda copy: copy.start())
    send_along(every[:4], lambda copy: copy.start())

    zero = jnp.zeros((PAD, HALF), F32)

    def blank_fine(i, carry):
        for h in range(2):
            U[i // 10, i % 10, h, pl.ds(0, PAD), :] = zero
            U[i // 10, i % 10, h, pl.ds(PAD + FY, PAD), :] = zero
        return carry

    lax.fori_loop(3, 7, blank_fine, 0)

    at = lane(8)
    tables = []
    for copy in small[1:]:
        copy.wait()
    for k in range(4):
        table = jnp.zeros((8, HALF), F32)
        for i in range(MATS):
            table = jnp.where(at == i, TAB[k, i], table)
        tables.append(table)
    t_cond, t_disp, t_k, t_n = tables
    t_a = t_disp * t_cond
    tables = [t_a, t_a + 0.5 * t_cond, t_a + 0.3 * t_cond, 6.0 * t_a + 0.8 * t_cond, t_k * t_n, t_n - 1.0, t_k]

    def look_up(r):
        for h in range(2):
            index = M[r, h]
            for f, table in enumerate(tables):
                value = gather(jnp.broadcast_to(table[0:1], (FY, HALF)), index)
                if f == 2 and h == 0:
                    value = jnp.where(lane(FY) == 0, 1.0, value)
                C[f, r, h] = value

    def spread_load(s, i, r):
        row = jnp.broadcast_to(L[s, i : i + 1, :], (FY, HALF))
        here = lax.broadcasted_iota(jnp.int32, (FY, HALF), 0) == lane(FY)
        total = jnp.sum(jnp.where(here, row, 0.0), axis=1, keepdims=True)
        LD[r] = jnp.broadcast_to(total, (FY, HALF))

    def coarse_load(rows):
        row = jnp.broadcast_to(rows[0:1] + rows[1:2], (CY, HALF))
        here = lax.broadcasted_iota(jnp.int32, (CY, HALF), 0) == lane(CY) // 2
        total = jnp.sum(jnp.where(here, row, 0.0), axis=1, keepdims=True)
        return jnp.broadcast_to(0.25 * total, (CY, HALF))

    def fine_step(k, r):
        for y in (0, 32):
            rows = pl.ds(PAD + y, 32)
            here = pl.ds(y, 32)
            low, high = U[k, r, 0, rows, :], U[k, r, 1, rows, :]
            at = lane(32)
            back = (roll(low, 1), roll(high, 1))
            ahead = (roll(low, HALF - 1), roll(high, HALF - 1))
            zms = (jnp.where(at == 0, LD[r - 1, here], back[0]), jnp.where(at == 0, back[0], back[1]))
            zps = (jnp.where(at == HALF - 1, ahead[1], ahead[0]), jnp.where(at == HALF - 1, 0.0, ahead[1]))
            for h in range(2):
                U[k + 1, r, h, rows, :] = update(
                    U[k, r - 1, h, rows, :],
                    (low, high)[h],
                    U[k, r + 1, h, rows, :],
                    U[k, r, h, pl.ds(PAD + y - 1, 32), :],
                    U[k, r, h, pl.ds(PAD + y + 1, 32), :],
                    zms[h],
                    zps[h],
                    *[C[f, r - 1, h, here] for f in range(6)],
                )

    def mean_rows(k, r):
        halves = []
        for h in range(2):
            parts = [U[k, r + q, h, pl.ds(PAD + p, CY, stride=2), :] for q in range(2) for p in range(2)]
            halves.append((parts[0] + parts[1]) + (parts[2] + parts[3]))
        return 0.125 * squeeze_lanes(*halves)

    def mean_coefs(j):
        means = []
        for f in (0, 1, 6, 5):
            halves = []
            for h in range(2):
                parts = [C[f, 2 * j + q, h, pl.ds(p, CY, stride=2), :] for q in range(2) for p in range(2)]
                halves.append((parts[0] + parts[1]) + (parts[2] + parts[3]))
            means.append(0.125 * squeeze_lanes(*halves))
        return 0.5 * means[0], 2.0 * (means[1] - means[0]), means[2] * (means[3] + 1.0), means[3]

    def combine(fields, dst, r):
        a, cond, kn, n1 = fields
        dst[r, 0] = a
        dst[r, 1] = a + 0.5 * cond
        dst[r, 2] = jnp.where(lane(CY) == 0, 1.0, a + 0.3 * cond)
        dst[r, 3] = 6.0 * a + 0.8 * cond
        dst[r, 4] = kn
        dst[r, 5] = n1

    def coarse_step(src, k, r, coefs, inflow, place):
        rows = pl.ds(PAD, CY)
        at = lane(CY)
        u0 = src[k, r, rows, :]
        return update(
            src[k, r - 1, rows, :],
            u0,
            src[k, r + 1, rows, :],
            src[k, r, pl.ds(PAD - 1, CY), :],
            src[k, r, pl.ds(PAD + 1, CY), :],
            jnp.where(at == 0, inflow[place], roll(u0, 1)),
            jnp.where(at == HALF - 1, 0.0, roll(u0, HALF - 1)),
            *[coefs[place, f] for f in range(6)],
        )

    for i in range(4):
        spread_load(1, i, 2 + i)

    def own_rows(r, carry):
        look_up(r)
        return carry

    lax.fori_loop(3, 5, own_rows, 0)

    def inner_rows(r, carry):
        fine_step(0, r)
        return carry

    lax.fori_loop(4, 6, inner_rows, 0)
    for j in range(2):
        GU[0, 2 + j, pl.ds(PAD, CY), :] = mean_rows(0, 3 + 2 * j)
    send_across(every[4:], urgent, lambda copy: copy.start())
    send_along(every[4:], lambda copy: copy.start())

    def both_sides(k, near):
        for s in range(2):
            r = 3 + (near if s == 1 else 3 - near)
            if near >= 0:
                fine_step(k, r)
            else:

                @pl.when(has[s])
                def _():
                    fine_step(k, r)

    lax.fori_loop(0, 50, blank_fine, 0)

    def blank_coarse(i, carry):
        for k in range(2):
            W[k, i, pl.ds(0, PAD), :] = zero
            W[k, i, pl.ds(PAD + CY, PAD), :] = zero
        return carry

    lax.fori_loop(0, 2 * SLOTS, blank_coarse, 0)
    for k in range(2):
        for r in range(6):
            GU[k, r, pl.ds(0, PAD), :] = zero
            GU[k, r, pl.ds(PAD + CY, PAD), :] = zero
    for s in range(2):

        @pl.when(jnp.logical_not(has[s]))
        def _():
            def clear(i, carry):
                for h in range(2):
                    U[i // 3, 7 - 7 * s + i % 3, h, pl.ds(PAD, FY), :] = jnp.zeros((FY, HALF), F32)
                return carry

            lax.fori_loop(0, 12, clear, 0)
            for k in range(2):
                for r in range(2):
                    GU[k, 4 - 4 * s + r, pl.ds(PAD, CY), :] = jnp.zeros((CY, HALF), F32)

    @pl.when(lead)
    def _():
        def clear(i, carry):
            @pl.when(jnp.logical_not(inside(base + i - WIDE)))
            def _():
                for q in range(2):
                    for f in range(6):
                        CC[2 * i + q, f] = jnp.zeros((CY, HALF), F32)
                    CL[2 * i + q] = jnp.zeros((CY, HALF), F32)
                    W[0, 2 * i + q, pl.ds(PAD, CY), :] = jnp.zeros((CY, HALF), F32)
                    for j in range(LONGEST):
                        RD[j, 2 * i + q] = jnp.zeros((CY, HALF), F32)

            return carry

        lax.fori_loop(0, SLOTS, clear, 0)

    look_up(2)
    look_up(5)
    for q in range(2):
        fields = mean_coefs(1 + q)
        for f in range(4):
            FL[pl.ds((4 * q + f) * CY, CY), :] = fields[f]
        combine(fields, GC, 1 + q)
        GL[1 + q] = coarse_load(L[1, 2 * q : 2 * q + 2, :])
    FL[pl.ds(8 * CY, 8), :] = L[1]

    def coefs_copy(e, pairs):
        to = base + 2 * pairs
        slot = t - to + WIDE
        return pltpu.make_async_remote_copy(
            src_ref=FL,
            dst_ref=CF.at[slot],
            send_sem=cf_send.at[e, PAIRS + pairs],
            recv_sem=cf_recv.at[slot],
            device_id=device((BREAK, LAST)[e], leader_of(to)),
            device_id_type=MESH,
        )

    def coefs_arrive(slot):
        pltpu.make_async_remote_copy(
            src_ref=FL,
            dst_ref=CF.at[slot],
            send_sem=cf_send.at[0, 0],
            recv_sem=cf_recv.at[slot],
            device_id=device(sibling, t),
            device_id_type=MESH,
        ).wait_recv()

    def over_pairs(gives, act):
        def body(i, carry):
            @pl.when(gives(i - PAIRS))
            def _():
                act(i - PAIRS)

            return carry

        lax.fori_loop(0, 2 * PAIRS + 1, body, 0)

    def over_slots(width, act):
        def body(i, carry):
            @pl.when(inside(base - WIDE + i))
            def _():
                act(i)

            return carry

        lax.fori_loop(WIDE - width, WIDE + 2 + width, body, 0)

    def send_coefs(e, act):
        over_pairs(lambda pairs: gives_coefs(e, pairs), lambda pairs: act(coefs_copy(e, pairs)))

    send_coefs(0, lambda copy: copy.start())

    @pl.when(m == 6)
    def _():
        send_coefs(1, lambda copy: copy.start())


    arrive((1,))
    for s in range(2):

        @pl.when(both(has[s], core == 1))
        def _():
            to_sibling(s).start()

    arrive((2,))

    send_across(every[2:], jnp.logical_not(urgent), lambda copy: copy.start())
    for s in range(2):

        @pl.when(both(has[s], core == 0))
        def _():
            to_sibling(s).wait_recv()

    for s in range(2):

        @pl.when(has[s])
        def _():
            for q in range(2):
                r = 6 - 6 * s + q
                look_up(r)
                spread_load(2 - 2 * s, q + 2 * s, r)
            GL[3 - 3 * s] = coarse_load(L[2 - 2 * s, 2 * s : 2 * s + 2, :])
            combine(mean_coefs(3 - 3 * s), GC, 3 - 3 * s)

    arrive((0,))
    both_sides(0, 0)
    both_sides(1, 1)
    arrive((3,))
    @pl.when(m == 4)
    def _():
        send_coefs(1, lambda copy: copy.start())

    both_sides(0, -1)
    both_sides(1, 0)
    both_sides(2, 1)
    for s in range(2):

        @pl.when(has[s])
        def _():
            GU[0, 4 - 3 * s, pl.ds(PAD, CY), :] = mean_rows(0, 7 - 6 * s)

    arrive((4,))
    for j in (1, 2):
        GU[1, 1 + j, pl.ds(PAD, CY), :] = coarse_step(GU, 0, 1 + j, GC, GL, j)
    for s in range(2):

        @pl.when(has[s])
        def _():
            j = 3 - 3 * s
            GU[1, 1 + j, pl.ds(PAD, CY), :] = coarse_step(GU, 0, 1 + j, GC, GL, j)

    for j in (1, 2):
        GG[j - 1] = coarse_step(GU, 1, 1 + j, GC, GL, j)

    arrive((5, 6))
    both_sides(1, -2)
    both_sides(1, -1)
    both_sides(2, -1)
    both_sides(2, 0)
    both_sides(3, 0)
    both_sides(3, 1)

    for j in range(2):
        mean = mean_rows(4, 3 + 2 * j)
        OWN[j] = jnp.where(m == 0, mean, mean - GG[j])

    def block_copy(pairs, initial):
        to = base + 2 * pairs
        slot = t - to + WIDE
        dst = W.at[0, pl.ds(2 * slot, 2), pl.ds(PAD, CY), :] if initial else RD.at[place, pl.ds(2 * slot, 2)]
        return pltpu.make_async_remote_copy(
            src_ref=OWN,
            dst_ref=dst,
            send_sem=s_send.at[PAIRS + pairs],
            recv_sem=s_recv.at[place, slot],
            device_id=device(head, leader_of(to)),
            device_id_type=MESH,
        )

    def block_arrives(j, slot, initial):
        pltpu.make_async_remote_copy(
            src_ref=OWN,
            dst_ref=W.at[0, pl.ds(2 * slot, 2), pl.ds(PAD, CY), :] if initial else RD.at[j, pl.ds(2 * slot, 2)],
            send_sem=s_send.at[0],
            recv_sem=s_recv.at[j, slot],
            device_id=device(sibling, t),
            device_id_type=MESH,
        ).wait_recv()

    def each_block(act):
        @pl.when(m == 0)
        def _():
            over_pairs(gives_block, lambda pairs: act(block_copy(pairs, True)))

        @pl.when(m > 0)
        def _():
            over_pairs(gives_block, lambda pairs: act(block_copy(pairs, False)))

    each_block(lambda copy: copy.start())

    @pl.when(m == 1)
    def _():
        send_coefs(1, lambda copy: copy.start())


    def carry_copy(pairs):
        to = base + 2 * pairs
        return pltpu.make_async_remote_copy(
            src_ref=CARRY,
            dst_ref=W.at[0, pl.ds(2 * (WIDE - 2 * pairs), 4), pl.ds(PAD, CY), :],
            send_sem=c_send.at[PAIRS + pairs],
            recv_sem=c_recv.at[PAIRS - pairs],
            device_id=device(LAST, leader_of(to)),
            device_id_type=MESH,
        )

    def carry_arrives(pairs):
        pltpu.make_async_remote_copy(
            src_ref=CARRY,
            dst_ref=W.at[0, pl.ds(2 * (WIDE + 2 * pairs), 4), pl.ds(PAD, CY), :],
            send_sem=c_send.at[0],
            recv_sem=c_recv.at[PAIRS + pairs],
            device_id=device(sibling, t),
            device_id_type=MESH,
        ).wait_recv()

    def carry_pair(pairs):
        return inside(base + 2 * pairs)

    def forward(j, q):
        return pltpu.make_async_remote_copy(
            src_ref=GCB.at[j, pl.ds(2 * q, 2)],
            dst_ref=FWB,
            send_sem=fw_send.at[j, q],
            recv_sem=fw_recv.at[0],
            device_id=device(first + 1 + j, base + q),
            device_id_type=MESH,
        )

    def forwards(j, act):
        for q in range(2):

            @pl.when(jnp.logical_or(j < count - 1, base + q != t))
            def _():
                act(forward(j, q))

    send_across(every, m >= 0, lambda copy: copy.wait_send())
    send_along(every, lambda copy: copy.wait_send())
    for s in range(2):

        @pl.when(both(has[s], core == 1))
        def _():
            to_sibling(s).wait_send()
    each_block(lambda copy: copy.wait_send())
    for e in range(2):
        send_coefs(e, lambda copy: copy.wait_send())

    @pl.when(lead)
    def _():
        def prepare(i):
            @pl.when(base - WIDE + i != t)
            def _():
                coefs_arrive(i)

            @pl.when(base - WIDE + i == t)
            def _():
                CF[i] = FL[...]

            for q in range(2):
                combine([CF[i, pl.ds((4 * q + f) * CY, CY), :] for f in range(4)], CC, 2 * i + q)
                CL[2 * i + q] = coarse_load(CF[i, pl.ds(8 * CY + 2 * q, 2), :])

        over_slots(count, prepare)

        def chain(j, carry):
            @pl.when(both(m == BREAK, j == 0))
            def _():
                over_slots(count, lambda i: block_arrives(0, i, True))

            @pl.when(j > 0)
            def _():
                over_slots(count - j, lambda i: block_arrives(j, i, False))

            @pl.when(both(m == LAST, j == 0))
            def _():
                over_pairs(carry_pair, carry_arrives)

            w = count - 1 - j

            @pl.when(j > 0)
            def _():
                def add(i, carry):
                    for q in range(4):
                        r = 2 * (WIDE - w - 1) + 4 * i + q
                        W[0, r, pl.ds(PAD, CY), :] = W[0, r, pl.ds(PAD, CY), :] + RD[j, r]
                    return carry

                lax.fori_loop(0, w + 2, add, 0)

            def step(k, start, rows):
                for q in range(rows):
                    W[1 - k, start + q, pl.ds(PAD, CY), :] = coarse_step(W, k, start + q, CC, CL, start + q)

            def sweep(k, start):
                def eight(i, carry):
                    step(k, start + 8 * i, 8)
                    return carry

                lax.fori_loop(0, jnp.where(w == 3, 2, jnp.where(w == 0, 0, 1)), eight, 0)

                @pl.when(jnp.logical_or(w == 0, w == 2))
                def _():
                    step(k, start + 4 * w, 4)

            sweep(0, 2 * (WIDE - w) - 1)
            step(0, 2 * (WIDE + w) + 3, 2)
            sweep(1, 2 * (WIDE - w))
            for q in range(4):
                GCB[j, q] = W[0, 2 * WIDE + q, pl.ds(PAD, CY), :]
            forwards(j, lambda copy: copy.start())
            return carry

        lax.fori_loop(0, count, chain, 0)

        own = t - base

        @pl.when(m == BREAK)
        def _():
            block_arrives(BREAK, WIDE + 1 - own, False)
            for q in range(2):
                RD[BREAK, 2 * WIDE + 2 * own + q] = OWN[q]
            for q in range(4):
                CARRY[q] = GCB[BREAK - 1, q] + RD[BREAK, 2 * WIDE + q]
            over_pairs(carry_pair, lambda pairs: carry_copy(pairs).start())

        for q in range(2):
            FWB[q] = GCB[count - 1, 2 * own + q]

    @pl.when(m == 0)
    def _():
        for q in range(2):
            FWB[q] = GG[q]

    @pl.when(jnp.logical_not(jnp.logical_or(lead, m == 0)))
    def _():
        forward(0, 0).wait_recv()

    for j in range(2):
        shift = FWB[j] - GG[j]
        for h in range(2):
            wide = gather(shift, lane(CY) // 2 + 64 * h)
            for p in range(2):
                UP[j, h, pl.ds(p, CY, stride=2), :] = wide
            for q in range(2):
                out[0, 2 * j + q, :, HALF * h : HALF * h + HALF] = U[4, 3 + 2 * j + q, h, rows, :] + UP[j, h]

    @pl.when(lead)
    def _():
        def handed(j, carry):
            forwards(j, lambda copy: copy.wait_send())
            return carry

        lax.fori_loop(0, count, handed, 0)

        @pl.when(m == BREAK)
        def _():
            over_pairs(carry_pair, lambda pairs: carry_copy(pairs).wait_send())


def shards(initial_states, material, conductivity, dispersivity, freundlich_k, freundlich_n, surface_load):
    hbm = pl.BlockSpec(memory_space=pltpu.HBM)
    block = (CY, HALF)
    dma = pltpu.SemaphoreType.DMA
    return pl.pallas_call(
        kernel,
        out_shape=pltpu.VMEM(initial_states.shape, F32),
        in_specs=[hbm] * 7,
        out_specs=pl.BlockSpec(memory_space=pltpu.VMEM),
        scratch_shapes=[
            pltpu.VMEM((5, 10, 2, FY + 2 * PAD, HALF), F32),
            pltpu.VMEM((8, 2, FY, HALF), jnp.int32),
            pltpu.VMEM((7, 8, 2, FY, HALF), F32),
            pltpu.VMEM((3, 8, HALF), F32),
            pltpu.VMEM((8, FY, HALF), F32),
            pltpu.VMEM((8 * CY + 8, HALF), F32),
            pltpu.VMEM((4, 6) + block, F32),
            pltpu.VMEM((4,) + block, F32),
            pltpu.VMEM((2, 6, CY + 2 * PAD, HALF), F32),
            pltpu.VMEM((2,) + block, F32),
            pltpu.VMEM((2,) + block, F32),
            pltpu.VMEM((4,) + block, F32),
            pltpu.VMEM((2, 2 * SLOTS, CY + 2 * PAD, HALF), F32),
            pltpu.VMEM((SLOTS, 8 * CY + 8, HALF), F32),
            pltpu.VMEM((2 * SLOTS, 6) + block, F32),
            pltpu.VMEM((2 * SLOTS,) + block, F32),
            pltpu.VMEM((LONGEST, 2 * SLOTS) + block, F32),
            pltpu.VMEM((LONGEST, 4) + block, F32),
            pltpu.VMEM((2,) + block, F32),
            pltpu.VMEM((2, 2, FY, HALF), F32),
            pltpu.VMEM((4, FY), F32),
            pltpu.SMEM((4, MATS), F32),
            dma((4,)),
            dma((5,)),
            dma((7, 2)),
            dma((7, 2)),
            dma((2,)),
            dma((2,)),
            dma((2, 2 * PAIRS + 1)),
            dma((SLOTS,)),
            dma((2 * PAIRS + 1,)),
            dma((LONGEST, SLOTS)),
            dma((2 * PAIRS + 1,)),
            dma((2 * PAIRS + 1,)),
            dma((LONGEST, 2)),
            dma((1,)),
        ],
        compiler_params=pltpu.CompilerParams(
            collective_id=0, has_side_effects=True, vmem_limit_bytes=63 * 1024 * 1024
        ),
    )(conductivity, dispersivity, freundlich_k, freundlich_n, surface_load, initial_states, material)


def solution(mesh):
    in_specs = (
        P("tm", "tile", None, None),
        P("tile", None, None),
        P(),
        P(),
        P(),
        P(),
        P("tile", None),
    )
    out_specs = P("tm", "tile", None, None)
    return jax.shard_map(shards, mesh=mesh, in_specs=in_specs, out_specs=out_specs, check_vma=False)
```

```python
import jax
import jax.numpy as jnp
from jax import lax
from jax.experimental import pallas as pl
from jax.experimental.pallas import tpu as pltpu
from jax.sharding import PartitionSpec as P

MESH = pl.DeviceIdType.MESH
F32 = jnp.float32
MATS = 12
TILES = 32
HALF = 128
FY = 64
CY = 32
PAD = 8
URGENT = 3
LAST = 7
BREAK = 3
LONGEST = max(BREAK, LAST - BREAK)
PAIRS = (LONGEST + 1) // 2
WIDE = 2 * PAIRS
SLOTS = 2 * WIDE + 2
COEFS_FROM = ((2, 5, 4), (6, 4, 1))


def lane(rows):
    return lax.broadcasted_iota(jnp.int32, (rows, HALF), 1)


def roll(value, shift):
    return pltpu.roll(value, shift, 1)


def gather(value, index):
    return jnp.take_along_axis(value, index, axis=1)


def update(um, u0, up, ym, yp, zm, zp, a, b, c, d, kn, n1):
    flux = a * ((up + zp) + (ym + yp)) + b * um + c * zm - d * u0
    power = jnp.exp2(n1 * jnp.log2(jnp.abs(u0) + 1.0))
    return u0 + flux / (1.0 + kn * power)


def squeeze_lanes(low, high):
    rows = low.shape[0]
    at = lane(rows)
    index = (2 * at) % HALF
    low = low + roll(low, HALF - 1)
    high = high + roll(high, HALF - 1)
    return jnp.where(at < HALF // 2, gather(low, index), gather(high, index))


def kernel(
    cond, disp, fk, fn, load, init, mat, out,
    U, M, C, L, LD, FL, GC, GL, GU, GG, OWN, CARRY, W, CF, CC, CL, RD, GCB, FWB, UP,
    LIN, TAB, in_sem, small_sem, halo_send, halo_recv, sib_send, sib_recv, cf_send, cf_recv, s_send, s_recv, c_send, c_recv, fw_send, fw_recv,
):
    m = lax.axis_index("tm")
    t = lax.axis_index("tile")

    def device(tm, tile):
        return {"tm": tm, "tile": tile}

    def inside(tile):
        return jnp.logical_and(tile >= 0, tile < TILES)

    base = t - t % 2

    def leader_of(base):
        return base + 1 - (base % 4) // 2

    head = jnp.where(m <= BREAK, BREAK, LAST)
    lead = jnp.logical_and(m == head, t == leader_of(base))
    first = jnp.where(m <= BREAK, 0, BREAK)
    count = head - first
    place = m - first
    width = head - m

    def both(a, b):
        return jnp.logical_and(a, b)

    def reaches(base, width):
        return both(both(base >= 0, base < TILES), both(base - width <= t, t <= base + 1 + width))

    def coefs_from(e, pairs):
        value = COEFS_FROM[e][PAIRS]
        for i in range(PAIRS):
            value = jnp.where(jnp.abs(pairs) == i, COEFS_FROM[e][i], value)
        return value

    def gives_coefs(e, pairs):
        to = base + 2 * pairs
        return both(both(reaches(to, (BREAK, LAST - BREAK)[e]), m == coefs_from(e, pairs)), t != leader_of(to))

    def gives_block(pairs):
        to = base + 2 * pairs
        return both(both(m < LAST, reaches(to, width)), jnp.logical_or(m < head, t != leader_of(to)))

    x = t % 4
    core = m % 2
    sibling = m + 1 - 2 * core
    far = (x == 0, x == 3)
    has = (t < TILES - 1, t > 0)

    loads = []
    for h in range(2):
        loads.append(pltpu.make_async_copy(mat.at[:, :, pl.ds(HALF * h, HALF)], M.at[pl.ds(2, 4), h], in_sem.at[h]))
    for h in range(2):
        loads.append(
            pltpu.make_async_copy(
                init.at[0, :, :, pl.ds(HALF * h, HALF)], U.at[0, pl.ds(3, 4), h, pl.ds(PAD, FY), :], in_sem.at[2 + h]
            )
        )
    small = [pltpu.make_async_copy(load, LIN, small_sem.at[0])]
    for i, ref in enumerate((cond, disp, fk, fn)):
        small.append(pltpu.make_async_copy(ref, TAB.at[i], small_sem.at[1 + i]))
    for copy in loads + small:
        copy.start()

    barrier = pltpu.get_barrier_semaphore()

    def greet(tm, tile, when):
        @pl.when(jnp.logical_and(when, inside(tile)))
        def _():
            pl.semaphore_signal(barrier, inc=1, device_id=device(tm, tile), device_id_type=MESH)

    greet(m, t - 1, m >= 0)
    greet(m, t + 1, m >= 0)
    greet(sibling, t, m >= 0)

    for e, (slice_, start) in enumerate(((BREAK, 0), (LAST, BREAK))):

        @pl.when(both(lead, m == slice_))
        def _():
            reach = slice_ - start
            for j in range(reach):
                if j == 0 and e == 1:

                    def greet_pair(i, carry):
                        to = base + 2 * (i - PAIRS)
                        greet(BREAK, leader_of(to), m >= 0)
                        return carry

                    lax.fori_loop(0, 2 * PAIRS + 1, greet_pair, 0)
                else:

                    def greet_tile(i, carry):
                        greet(start + j, base + i - (reach - j), m >= 0)
                        return carry

                    lax.fori_loop(0, 2 + 2 * (reach - j), greet_tile, 0)
            for pairs in range(-PAIRS, PAIRS + 1):
                for i in (2 * pairs, 2 * pairs + 1):
                    if -reach <= i <= 1 + reach:
                        greet(COEFS_FROM[e][abs(pairs)], base + i, base + i != t)
            if e == 0:
                greet(BREAK, 2 * base + 1 - t, m >= 0)

    greet(head, leader_of(base), both(jnp.logical_not(lead), m > 0))

    def add_pair(i, total):
        pairs = i - PAIRS
        for e in range(2):
            total = total + jnp.where(gives_coefs(e, pairs), 1, 0)
        total = total + jnp.where(gives_block(pairs), 1, 0)
        return total + jnp.where(both(both(lead, m == BREAK), inside(base + 2 * pairs)), 1, 0)

    expected = 1 + jnp.where(t > 0, 1, 0) + jnp.where(t < TILES - 1, 1, 0) + jnp.where(lead, 2 * count - 1, 0)
    expected = expected + lax.fori_loop(0, 2 * PAIRS + 1, add_pair, 0)

    rows = pl.ds(PAD, FY)

    def halo(item, s, arriving):
        src, dst = (
            (U.at[0, 3 + 3 * s, :, rows, :], U.at[0, 7 - 5 * s, :, rows, :]),
            (M.at[pl.ds(2 + 2 * s, 2)], M.at[pl.ds(6 - 6 * s, 2)]),
            (L.at[1], L.at[2 - 2 * s]),
            (U.at[0, 4 + s, :, rows, :], U.at[0, 8 - 7 * s, :, rows, :]),
            (GU.at[0, 3 - s, pl.ds(PAD, CY), :], GU.at[0, 5 - 5 * s, pl.ds(PAD, CY), :]),
            (U.at[1, 4, :, rows, :], U.at[1, 8 - 8 * s, :, rows, :]),
            (U.at[1, 5, :, rows, :], U.at[1, 9 - 8 * s, :, rows, :]),
        )[item]
        toward = 2 * s - 1
        return pltpu.make_async_remote_copy(
            src_ref=src,
            dst_ref=dst,
            send_sem=halo_send.at[item, s],
            recv_sem=halo_recv.at[item, s],
            device_id=device(m, t - toward if arriving else t + toward),
            device_id_type=MESH,
        )

    def to_sibling(s):
        rows = pl.ds(6 - 6 * s, 2)
        return pltpu.make_async_remote_copy(
            src_ref=M.at[rows],
            dst_ref=M.at[rows],
            send_sem=sib_send.at[s],
            recv_sem=sib_recv.at[s],
            device_id=device(sibling, t),
            device_id_type=MESH,
        )

    sends = (t > 0, t < TILES - 1)

    def send_across(items, when, act):
        for s in range(2):

            @pl.when(jnp.logical_and(when, jnp.logical_and(sends[s], far[s])))
            def _():
                for item in items:
                    if item == 1:

                        @pl.when(core == 1)
                        def _():
                            act(halo(item, s, False))

                    else:
                        act(halo(item, s, False))

    def send_along(items, act):
        for item in items:
            for s in range(2):

                @pl.when(both(both(sends[s], jnp.logical_not(far[s])), jnp.logical_or(item != 1, core == 1)))
                def _():
                    act(halo(item, s, False))

    every = (1, 2, 0, 3, 4, 5, 6)
    urgent = m < URGENT

    def arrive(items):
        for item in items:
            for s in range(2):

                @pl.when(both(has[s], jnp.logical_or(item != 1, core == 1)))
                def _():
                    halo(item, s, True).wait_recv()

    for copy in small[:1] + loads:
        copy.wait()
    L[1] = jnp.zeros((8, HALF), F32)
    L[1, 0:4, 0:FY] = LIN[...]
    pl.semaphore_wait(barrier, expected)
    send_across(every[:2], m >= 0, lambda copy: copy.start())
    send_across(every[2:4], urgent, lambda copy: copy.start())
    send_along(every[:4], lambda copy: copy.start())

    zero = jnp.zeros((PAD, HALF), F32)

    def blank_fine(i, carry):
        for h in range(2):
            U[i // 10, i % 10, h, pl.ds(0, PAD), :] = zero
            U[i // 10, i % 10, h, pl.ds(PAD + FY, PAD), :] = zero
        return carry

    lax.fori_loop(3, 7, blank_fine, 0)

    at = lane(8)
    tables = []
    for copy in small[1:]:
        copy.wait()
    for k in range(4):
        table = jnp.zeros((8, HALF), F32)
        for i in range(MATS):
            table = jnp.where(at == i, TAB[k, i], table)
        tables.append(table)
    t_cond, t_disp, t_k, t_n = tables
    t_a = t_disp * t_cond
    tables = [t_a, t_a + 0.5 * t_cond, t_a + 0.3 * t_cond, 6.0 * t_a + 0.8 * t_cond, t_k * t_n, t_n - 1.0, t_k]

    def look_up(r):
        for h in range(2):
            index = M[r, h]
            for f, table in enumerate(tables):
                value = gather(jnp.broadcast_to(table[0:1], (FY, HALF)), index)
                if f == 2 and h == 0:
                    value = jnp.where(lane(FY) == 0, 1.0, value)
                C[f, r, h] = value

    def spread_load(s, i, r):
        row = jnp.broadcast_to(L[s, i : i + 1, :], (FY, HALF))
        here = lax.broadcasted_iota(jnp.int32, (FY, HALF), 0) == lane(FY)
        total = jnp.sum(jnp.where(here, row, 0.0), axis=1, keepdims=True)
        LD[r] = jnp.broadcast_to(total, (FY, HALF))

    def coarse_load(rows):
        row = jnp.broadcast_to(rows[0:1] + rows[1:2], (CY, HALF))
        here = lax.broadcasted_iota(jnp.int32, (CY, HALF), 0) == lane(CY) // 2
        total = jnp.sum(jnp.where(here, row, 0.0), axis=1, keepdims=True)
        return jnp.broadcast_to(0.25 * total, (CY, HALF))

    def fine_step(k, r):
        for y in (0, 32):
            rows = pl.ds(PAD + y, 32)
            here = pl.ds(y, 32)
            low, high = U[k, r, 0, rows, :], U[k, r, 1, rows, :]
            at = lane(32)
            back = (roll(low, 1), roll(high, 1))
            ahead = (roll(low, HALF - 1), roll(high, HALF - 1))
            zms = (jnp.where(at == 0, LD[r - 1, here], back[0]), jnp.where(at == 0, back[0], back[1]))
            zps = (jnp.where(at == HALF - 1, ahead[1], ahead[0]), jnp.where(at == HALF - 1, 0.0, ahead[1]))
            for h in range(2):
                U[k + 1, r, h, rows, :] = update(
                    U[k, r - 1, h, rows, :],
                    (low, high)[h],
                    U[k, r + 1, h, rows, :],
                    U[k, r, h, pl.ds(PAD + y - 1, 32), :],
                    U[k, r, h, pl.ds(PAD + y + 1, 32), :],
                    zms[h],
                    zps[h],
                    *[C[f, r - 1, h, here] for f in range(6)],
                )

    def mean_rows(k, r):
        halves = []
        for h in range(2):
            parts = [U[k, r + q, h, pl.ds(PAD + p, CY, stride=2), :] for q in range(2) for p in range(2)]
            halves.append((parts[0] + parts[1]) + (parts[2] + parts[3]))
        return 0.125 * squeeze_lanes(*halves)

    def mean_coefs(j):
        means = []
        for f in (0, 1, 6, 5):
            halves = []
            for h in range(2):
                parts = [C[f, 2 * j + q, h, pl.ds(p, CY, stride=2), :] for q in range(2) for p in range(2)]
                halves.append((parts[0] + parts[1]) + (parts[2] + parts[3]))
            means.append(0.125 * squeeze_lanes(*halves))
        return 0.5 * means[0], 2.0 * (means[1] - means[0]), means[2] * (means[3] + 1.0), means[3]

    def combine(fields, dst, r):
        a, cond, kn, n1 = fields
        dst[r, 0] = a
        dst[r, 1] = a + 0.5 * cond
        dst[r, 2] = jnp.where(lane(CY) == 0, 1.0, a + 0.3 * cond)
        dst[r, 3] = 6.0 * a + 0.8 * cond
        dst[r, 4] = kn
        dst[r, 5] = n1

    def coarse_step(src, k, r, coefs, inflow, place):
        rows = pl.ds(PAD, CY)
        at = lane(CY)
        u0 = src[k, r, rows, :]
        return update(
            src[k, r - 1, rows, :],
            u0,
            src[k, r + 1, rows, :],
            src[k, r, pl.ds(PAD - 1, CY), :],
            src[k, r, pl.ds(PAD + 1, CY), :],
            jnp.where(at == 0, inflow[place], roll(u0, 1)),
            jnp.where(at == HALF - 1, 0.0, roll(u0, HALF - 1)),
            *[coefs[place, f] for f in range(6)],
        )

    for i in range(4):
        spread_load(1, i, 2 + i)

    def own_rows(r, carry):
        look_up(r)
        return carry

    lax.fori_loop(3, 5, own_rows, 0)

    def inner_rows(r, carry):
        fine_step(0, r)
        return carry

    lax.fori_loop(4, 6, inner_rows, 0)
    for j in range(2):
        GU[0, 2 + j, pl.ds(PAD, CY), :] = mean_rows(0, 3 + 2 * j)
    send_across(every[4:], urgent, lambda copy: copy.start())
    send_along(every[4:], lambda copy: copy.start())

    def both_sides(k, near):
        for s in range(2):
            r = 3 + (near if s == 1 else 3 - near)
            if near >= 0:
                fine_step(k, r)
            else:

                @pl.when(has[s])
                def _():
                    fine_step(k, r)

    lax.fori_loop(0, 50, blank_fine, 0)

    def blank_coarse(i, carry):
        for k in range(2):
            W[k, i, pl.ds(0, PAD), :] = zero
            W[k, i, pl.ds(PAD + CY, PAD), :] = zero
        return carry

    lax.fori_loop(0, 2 * SLOTS, blank_coarse, 0)
    for k in range(2):
        for r in range(6):
            GU[k, r, pl.ds(0, PAD), :] = zero
            GU[k, r, pl.ds(PAD + CY, PAD), :] = zero
    for s in range(2):

        @pl.when(jnp.logical_not(has[s]))
        def _():
            def clear(i, carry):
                for h in range(2):
                    U[i // 3, 7 - 7 * s + i % 3, h, pl.ds(PAD, FY), :] = jnp.zeros((FY, HALF), F32)
                return carry

            lax.fori_loop(0, 12, clear, 0)
            for k in range(2):
                for r in range(2):
                    GU[k, 4 - 4 * s + r, pl.ds(PAD, CY), :] = jnp.zeros((CY, HALF), F32)

    @pl.when(lead)
    def _():
        def clear(i, carry):
            @pl.when(jnp.logical_not(inside(base + i - WIDE)))
            def _():
                for q in range(2):
                    for f in range(6):
                        CC[2 * i + q, f] = jnp.zeros((CY, HALF), F32)
                    CL[2 * i + q] = jnp.zeros((CY, HALF), F32)
                    W[0, 2 * i + q, pl.ds(PAD, CY), :] = jnp.zeros((CY, HALF), F32)
                    for j in range(LONGEST):
                        RD[j, 2 * i + q] = jnp.zeros((CY, HALF), F32)

            return carry

        lax.fori_loop(0, SLOTS, clear, 0)

    look_up(2)
    look_up(5)
    for q in range(2):
        fields = mean_coefs(1 + q)
        for f in range(4):
            FL[pl.ds((4 * q + f) * CY, CY), :] = fields[f]
        combine(fields, GC, 1 + q)
        GL[1 + q] = coarse_load(L[1, 2 * q : 2 * q + 2, :])
    FL[pl.ds(8 * CY, 8), :] = L[1]

    def coefs_copy(e, pairs):
        to = base + 2 * pairs
        slot = t - to + WIDE
        return pltpu.make_async_remote_copy(
            src_ref=FL,
            dst_ref=CF.at[slot],
            send_sem=cf_send.at[e, PAIRS + pairs],
            recv_sem=cf_recv.at[slot],
            device_id=device((BREAK, LAST)[e], leader_of(to)),
            device_id_type=MESH,
        )

    def coefs_arrive(slot):
        pltpu.make_async_remote_copy(
            src_ref=FL,
            dst_ref=CF.at[slot],
            send_sem=cf_send.at[0, 0],
            recv_sem=cf_recv.at[slot],
            device_id=device(sibling, t),
            device_id_type=MESH,
        ).wait_recv()

    def over_pairs(gives, act):
        def body(i, carry):
            @pl.when(gives(i - PAIRS))
            def _():
                act(i - PAIRS)

            return carry

        lax.fori_loop(0, 2 * PAIRS + 1, body, 0)

    def over_slots(width, act):
        def body(i, carry):
            @pl.when(inside(base - WIDE + i))
            def _():
                act(i)

            return carry

        lax.fori_loop(WIDE - width, WIDE + 2 + width, body, 0)

    def send_coefs(e, act):
        over_pairs(lambda pairs: gives_coefs(e, pairs), lambda pairs: act(coefs_copy(e, pairs)))

    send_coefs(0, lambda copy: copy.start())

    @pl.when(m == 6)
    def _():
        send_coefs(1, lambda copy: copy.start())


    arrive((1,))
    for s in range(2):

        @pl.when(both(has[s], core == 1))
        def _():
            to_sibling(s).start()

    arrive((2,))

    send_across(every[2:], jnp.logical_not(urgent), lambda copy: copy.start())
    for s in range(2):

        @pl.when(both(has[s], core == 0))
        def _():
            to_sibling(s).wait_recv()

    for s in range(2):

        @pl.when(has[s])
        def _():
            for q in range(2):
                r = 6 - 6 * s + q
                look_up(r)
                spread_load(2 - 2 * s, q + 2 * s, r)
            GL[3 - 3 * s] = coarse_load(L[2 - 2 * s, 2 * s : 2 * s + 2, :])
            combine(mean_coefs(3 - 3 * s), GC, 3 - 3 * s)

    arrive((0,))
    both_sides(0, 0)
    both_sides(1, 1)
    arrive((3,))
    @pl.when(m == 4)
    def _():
        send_coefs(1, lambda copy: copy.start())

    both_sides(0, -1)
    both_sides(1, 0)
    both_sides(2, 1)
    for s in range(2):

        @pl.when(has[s])
        def _():
            GU[0, 4 - 3 * s, pl.ds(PAD, CY), :] = mean_rows(0, 7 - 6 * s)

    arrive((4,))
    for j in (1, 2):
        GU[1, 1 + j, pl.ds(PAD, CY), :] = coarse_step(GU, 0, 1 + j, GC, GL, j)
    for s in range(2):

        @pl.when(has[s])
        def _():
            j = 3 - 3 * s
            GU[1, 1 + j, pl.ds(PAD, CY), :] = coarse_step(GU, 0, 1 + j, GC, GL, j)

    for j in (1, 2):
        GG[j - 1] = coarse_step(GU, 1, 1 + j, GC, GL, j)

    arrive((5, 6))
    both_sides(1, -2)
    both_sides(1, -1)
    both_sides(2, -1)
    both_sides(2, 0)
    both_sides(3, 0)
    both_sides(3, 1)

    for j in range(2):
        mean = mean_rows(4, 3 + 2 * j)
        OWN[j] = jnp.where(m == 0, mean, mean - GG[j])

    def block_copy(pairs, initial):
        to = base + 2 * pairs
        slot = t - to + WIDE
        dst = W.at[0, pl.ds(2 * slot, 2), pl.ds(PAD, CY), :] if initial else RD.at[place, pl.ds(2 * slot, 2)]
        return pltpu.make_async_remote_copy(
            src_ref=OWN,
            dst_ref=dst,
            send_sem=s_send.at[PAIRS + pairs],
            recv_sem=s_recv.at[place, slot],
            device_id=device(head, leader_of(to)),
            device_id_type=MESH,
        )

    def block_arrives(j, slot, initial):
        pltpu.make_async_remote_copy(
            src_ref=OWN,
            dst_ref=W.at[0, pl.ds(2 * slot, 2), pl.ds(PAD, CY), :] if initial else RD.at[j, pl.ds(2 * slot, 2)],
            send_sem=s_send.at[0],
            recv_sem=s_recv.at[j, slot],
            device_id=device(sibling, t),
            device_id_type=MESH,
        ).wait_recv()

    def each_block(act):
        @pl.when(m == 0)
        def _():
            over_pairs(gives_block, lambda pairs: act(block_copy(pairs, True)))

        @pl.when(m > 0)
        def _():
            over_pairs(gives_block, lambda pairs: act(block_copy(pairs, False)))

    each_block(lambda copy: copy.start())

    @pl.when(m == 1)
    def _():
        send_coefs(1, lambda copy: copy.start())


    def carry_copy(pairs):
        to = base + 2 * pairs
        return pltpu.make_async_remote_copy(
            src_ref=CARRY,
            dst_ref=W.at[0, pl.ds(2 * (WIDE - 2 * pairs), 4), pl.ds(PAD, CY), :],
            send_sem=c_send.at[PAIRS + pairs],
            recv_sem=c_recv.at[PAIRS - pairs],
            device_id=device(LAST, leader_of(to)),
            device_id_type=MESH,
        )

    def carry_arrives(pairs):
        pltpu.make_async_remote_copy(
            src_ref=CARRY,
            dst_ref=W.at[0, pl.ds(2 * (WIDE + 2 * pairs), 4), pl.ds(PAD, CY), :],
            send_sem=c_send.at[0],
            recv_sem=c_recv.at[PAIRS + pairs],
            device_id=device(sibling, t),
            device_id_type=MESH,
        ).wait_recv()

    def carry_pair(pairs):
        return inside(base + 2 * pairs)

    def forward(j, q):
        return pltpu.make_async_remote_copy(
            src_ref=GCB.at[j, pl.ds(2 * q, 2)],
            dst_ref=FWB,
            send_sem=fw_send.at[j, q],
            recv_sem=fw_recv.at[0],
            device_id=device(first + 1 + j, base + q),
            device_id_type=MESH,
        )

    def forwards(j, act):
        for q in range(2):

            @pl.when(jnp.logical_or(j < count - 1, base + q != t))
            def _():
                act(forward(j, q))

    send_across(every, m >= 0, lambda copy: copy.wait_send())
    send_along(every, lambda copy: copy.wait_send())
    for s in range(2):

        @pl.when(both(has[s], core == 1))
        def _():
            to_sibling(s).wait_send()
    each_block(lambda copy: copy.wait_send())
    for e in range(2):
        send_coefs(e, lambda copy: copy.wait_send())

    @pl.when(lead)
    def _():
        def prepare(i):
            @pl.when(base - WIDE + i != t)
            def _():
                coefs_arrive(i)

            @pl.when(base - WIDE + i == t)
            def _():
                CF[i] = FL[...]

            for q in range(2):
                combine([CF[i, pl.ds((4 * q + f) * CY, CY), :] for f in range(4)], CC, 2 * i + q)
                CL[2 * i + q] = coarse_load(CF[i, pl.ds(8 * CY + 2 * q, 2), :])

        over_slots(count, prepare)

        def chain(j, carry):
            @pl.when(both(m == BREAK, j == 0))
            def _():
                over_slots(count, lambda i: block_arrives(0, i, True))

            @pl.when(j > 0)
            def _():
                over_slots(count - j, lambda i: block_arrives(j, i, False))

            @pl.when(both(m == LAST, j == 0))
            def _():
                over_pairs(carry_pair, carry_arrives)

            w = count - 1 - j

            @pl.when(j > 0)
            def _():
                def add(i, carry):
                    for q in range(4):
                        r = 2 * (WIDE - w - 1) + 4 * i + q
                        W[0, r, pl.ds(PAD, CY), :] = W[0, r, pl.ds(PAD, CY), :] + RD[j, r]
                    return carry

                lax.fori_loop(0, w + 2, add, 0)

            def step(k, start, rows):
                for q in range(rows):
                    W[1 - k, start + q, pl.ds(PAD, CY), :] = coarse_step(W, k, start + q, CC, CL, start + q)

            def sweep(k, start, more):
                tail = start + jnp.where(w >= 2, 8, 0)

                @pl.when(w >= 2)
                def _():
                    step(k, start, 8)

                @pl.when(jnp.logical_or(w == 0, w == 2))
                def _():
                    step(k, tail, 4 + more)

                @pl.when(jnp.logical_or(w == 1, w == 3))
                def _():
                    step(k, tail, 8 + more)

            sweep(0, 2 * (WIDE - w) - 1, 2)
            sweep(1, 2 * (WIDE - w), 0)
            for q in range(4):
                GCB[j, q] = W[0, 2 * WIDE + q, pl.ds(PAD, CY), :]
            forwards(j, lambda copy: copy.start())
            return carry

        lax.fori_loop(0, count, chain, 0)

        own = t - base

        @pl.when(m == BREAK)
        def _():
            block_arrives(BREAK, WIDE + 1 - own, False)
            for q in range(2):
                RD[BREAK, 2 * WIDE + 2 * own + q] = OWN[q]
            for q in range(4):
                CARRY[q] = GCB[BREAK - 1, q] + RD[BREAK, 2 * WIDE + q]
            over_pairs(carry_pair, lambda pairs: carry_copy(pairs).start())

        for q in range(2):
            FWB[q] = GCB[count - 1, 2 * own + q]

    @pl.when(m == 0)
    def _():
        for q in range(2):
            FWB[q] = GG[q]

    @pl.when(jnp.logical_not(jnp.logical_or(lead, m == 0)))
    def _():
        forward(0, 0).wait_recv()

    for j in range(2):
        shift = FWB[j] - GG[j]
        for h in range(2):
            wide = gather(shift, lane(CY) // 2 + 64 * h)
            for p in range(2):
                UP[j, h, pl.ds(p, CY, stride=2), :] = wide
            for q in range(2):
                out[0, 2 * j + q, :, HALF * h : HALF * h + HALF] = U[4, 3 + 2 * j + q, h, rows, :] + UP[j, h]

    @pl.when(lead)
    def _():
        def handed(j, carry):
            forwards(j, lambda copy: copy.wait_send())
            return carry

        lax.fori_loop(0, count, handed, 0)

        @pl.when(m == BREAK)
        def _():
            over_pairs(carry_pair, lambda pairs: carry_copy(pairs).wait_send())


def shards(initial_states, material, conductivity, dispersivity, freundlich_k, freundlich_n, surface_load):
    hbm = pl.BlockSpec(memory_space=pltpu.HBM)
    block = (CY, HALF)
    dma = pltpu.SemaphoreType.DMA
    return pl.pallas_call(
        kernel,
        out_shape=pltpu.VMEM(initial_states.shape, F32),
        in_specs=[hbm] * 7,
        out_specs=pl.BlockSpec(memory_space=pltpu.VMEM),
        scratch_shapes=[
            pltpu.VMEM((5, 10, 2, FY + 2 * PAD, HALF), F32),
            pltpu.VMEM((8, 2, FY, HALF), jnp.int32),
            pltpu.VMEM((7, 8, 2, FY, HALF), F32),
            pltpu.VMEM((3, 8, HALF), F32),
            pltpu.VMEM((8, FY, HALF), F32),
            pltpu.VMEM((8 * CY + 8, HALF), F32),
            pltpu.VMEM((4, 6) + block, F32),
            pltpu.VMEM((4,) + block, F32),
            pltpu.VMEM((2, 6, CY + 2 * PAD, HALF), F32),
            pltpu.VMEM((2,) + block, F32),
            pltpu.VMEM((2,) + block, F32),
            pltpu.VMEM((4,) + block, F32),
            pltpu.VMEM((2, 2 * SLOTS, CY + 2 * PAD, HALF), F32),
            pltpu.VMEM((SLOTS, 8 * CY + 8, HALF), F32),
            pltpu.VMEM((2 * SLOTS, 6) + block, F32),
            pltpu.VMEM((2 * SLOTS,) + block, F32),
            pltpu.VMEM((LONGEST, 2 * SLOTS) + block, F32),
            pltpu.VMEM((LONGEST, 4) + block, F32),
            pltpu.VMEM((2,) + block, F32),
            pltpu.VMEM((2, 2, FY, HALF), F32),
            pltpu.VMEM((4, FY), F32),
            pltpu.SMEM((4, MATS), F32),
            dma((4,)),
            dma((5,)),
            dma((7, 2)),
            dma((7, 2)),
            dma((2,)),
            dma((2,)),
            dma((2, 2 * PAIRS + 1)),
            dma((SLOTS,)),
            dma((2 * PAIRS + 1,)),
            dma((LONGEST, SLOTS)),
            dma((2 * PAIRS + 1,)),
            dma((2 * PAIRS + 1,)),
            dma((LONGEST, 2)),
            dma((1,)),
        ],
        compiler_params=pltpu.CompilerParams(
            collective_id=0, has_side_effects=True, vmem_limit_bytes=63 * 1024 * 1024
        ),
    )(conductivity, dispersivity, freundlich_k, freundlich_n, surface_load, initial_states, material)


def solution(mesh):
    in_specs = (
        P("tm", "tile", None, None),
        P("tile", None, None),
        P(),
        P(),
        P(),
        P(),
        P("tile", None),
    )
    out_specs = P("tm", "tile", None, None)
    return jax.shard_map(shards, mesh=mesh, in_specs=in_specs, out_specs=out_specs, check_vma=False)
```
